32 devices in a mesh: gx: 4 (over y, x), yz: 8 (over z, core).
Axes of the slice: x: 2, y: 2, z: 4, core: 2. Of those that a mesh axis runs over, the one named last changes fastest.
Arguments:
- spin_vectors: float32 [3, 2, 16, 16, 128], P(None, None, 'gx', 'yz'), may hold values from -1 to 1, as said below
- pair_weight: float32 [112, 128], replicated, may hold values from -0.5 to 0.5
- mix_weight: float32 [128, 128], replicated, may hold values from -0.5 to 0.5
- mix_bias: float32 [128], replicated, may hold values from -3 to 3
- out_weight: float32 [128], replicated, may hold values from -0.5 to 0.5
Outputs:
- spins_next: float32 [3, 2, 16, 16, 128], P(None, None, 'gx', 'yz')
- field_next: float32 [3, 2, 16, 16, 128], P(None, None, 'gx', 'yz')
The draws below stay inside these ranges and needn't reach their ends.
Inputs may be any that keep to these rules, and one draw needn't show every extreme that they name: `spin_vectors`: every atom's spin has unit length.
All inputs are finite; a program needn't handle non-finite values.
Results may differ from the reference program's by a relative error of at most 0.0003.
Values sent between devices are 32-bit elements; how exact they have to be, the bound alone decides.
No kernel may reach another device: no remote copies, remote signals or barrier semaphores. Data moves between devices by JAX's collectives and lax.ppermute only.
A program may use at most 128 MiB of HBM per device.

```python
import math
from functools import reduce
import jax
import jax.numpy as jnp
from jax import lax

CX = 4
CY = 2
CZ = 128
NB = 8
K = 128
H = 128
NX = 16
NY = 16


def draw_spin_vectors(key, part):
    raw_draw = jax.random.normal(jax.random.fold_in(key, 11), (3, 2, NX, NY, CZ), jnp.float32)
    length = jnp.sqrt(jnp.sum(raw_draw * raw_draw, axis=0, keepdims=True))
    return raw_draw / jnp.maximum(length, 1e-06)


def centred(rng, shape, spread, limit, kind=jnp.bfloat16):
    values = spread * jax.random.normal(rng, shape, jnp.float32)
    return jnp.clip(values, min=-limit, max=limit).astype(kind)


def setup_inputs(seed: int = 0) -> dict:
    seeds = jax.random.split(jax.random.key(seed), 6)
    return {
        "spin_vectors": draw_spin_vectors(jax.random.fold_in(seeds[5], 71), 0),
        "pair_weight": centred(seeds[1], (14 * NB, K), (14 * NB) ** -0.5, 0.5, jnp.float32),
        "mix_weight": centred(seeds[2], (K, H), K ** -0.5, 0.5, jnp.float32),
        "mix_bias": centred(seeds[3], (H,), 0.5, 3.0, jnp.float32),
        "out_weight": centred(seeds[4], (H,), H ** -0.5, 0.5, jnp.float32),
    }


time_step = 0.1
first_shell = [(-1, -1, -1), (-1, -1, 0), (-1, 0, -1), (-1, 0, 0), (0, -1, -1), (0, -1, 0), (0, 0, -1), (0, 0, 0)]
second_shell = [(1, 0, 0), (-1, 0, 0), (0, 1, 0), (0, -1, 0), (0, 0, 1), (0, 0, -1)]

def bond_list(lattice):
    result = []
    for step_x, step_y, step_z in first_shell:
        if lattice == 0:
            result.append((1, step_x, step_y, step_z))
        else:
            result.append((0, -step_x, -step_y, -step_z))
    for step_x, step_y, step_z in second_shell:
        result.append((lattice, step_x, step_y, step_z))
    return result

def partner(bond_index):
    if bond_index < 8:
        return bond_index
    return 8 + (bond_index - 8 ^ 1)

def shifted(padded, target, step_x, step_y, step_z, width_x, width_y):
    window = padded[:, target, 1 + step_x:1 + step_x + width_x, 1 + step_y:1 + step_y + width_y, :]
    return jnp.roll(window, -step_z, axis=-1)

def coefficients(centre, padded, pair_weight, mix_weight, mix_bias, out_weight):
    width_x, width_y, width_z = (centre.shape[2], centre.shape[3], centre.shape[4])
    cosines = []
    for lattice in range(2):
        column = []
        for bond_entry in bond_list(lattice):
            target, step_x, step_y, step_z = bond_entry
            neighbour = shifted(padded, target, step_x, step_y, step_z, width_x, width_y)
            column.append(lax.optimization_barrier(jnp.sum(centre[:, lattice] * neighbour, axis=0)))
        cosines.append(jnp.stack(column, 0))
    cosine = jnp.stack(cosines, 1)
    first_kind = [jnp.ones_like(cosine), cosine]
    second_kind = [jnp.ones_like(cosine), 2.0 * cosine]
    for degree in range(2, NB + 1):
        first_kind.append(2.0 * cosine * first_kind[-1] - first_kind[-2])
        second_kind.append(2.0 * cosine * second_kind[-1] - second_kind[-2])
    atom_count = 2 * width_x * width_y * width_z
    features = jnp.stack(first_kind[1:NB + 1], 1).reshape(14 * NB, atom_count)
    slopes = jnp.stack([(degree + 1) * second_kind[degree] for degree in range(NB)], 1).reshape(14, NB, atom_count)
    contract_lead = (((0,), (0,)), ((), ()))
    best = lax.Precision.HIGHEST
    basis_vals = lax.dot_general(pair_weight, features, contract_lead, precision=best, preferred_element_type=jnp.float32)
    hidden = jnp.tanh(lax.dot_general(mix_weight, basis_vals, contract_lead, precision=best, preferred_element_type=jnp.float32) + mix_bias[:, None])
    hidden_grad = out_weight[:, None] * (1.0 - hidden * hidden)
    basis_grad = jnp.dot(mix_weight, hidden_grad, precision=best, preferred_element_type=jnp.float32)
    feature_grad = jnp.dot(pair_weight, basis_grad, precision=best, preferred_element_type=jnp.float32).reshape(14, NB, atom_count)
    return lax.optimization_barrier(jnp.sum(feature_grad * slopes, axis=1)).reshape(14, 2, width_x, width_y, width_z)

def field_from(coeff_own, coeff_padded, spins_padded):
    width_x, width_y = (coeff_own.shape[2], coeff_own.shape[3])
    fields = []
    for lattice in range(2):
        term_list = []
        for bond_index, bond_entry in enumerate(bond_list(lattice)):
            target, step_x, step_y, step_z = bond_entry
            mate = partner(bond_index)
            partner_coeff = shifted(coeff_padded[mate:mate + 1], target, step_x, step_y, step_z, width_x, width_y)[0]
            neighbour = shifted(spins_padded, target, step_x, step_y, step_z, width_x, width_y)
            term_list.append((coeff_own[bond_index, lattice] + partner_coeff) * neighbour)
        fields.append(-reduce(jnp.add, term_list))
    return jnp.stack(fields, 1)

def rotate(spin_now, field_now):
    angle_vec = time_step * field_now
    angle_size = jnp.sqrt(lax.optimization_barrier(jnp.sum(angle_vec * angle_vec, axis=0)))
    cross_term = jnp.cross(angle_vec, spin_now, axis=0)
    projection = lax.optimization_barrier(jnp.sum(angle_vec * spin_now, axis=0))
    half_sinc = jnp.sinc(angle_size / (2.0 * math.pi))
    return jnp.cos(angle_size) * spin_now + jnp.sinc(angle_size / math.pi) * cross_term + 0.5 * half_sinc * half_sinc * projection * angle_vec

def sectors(size_x, size_y, size_z):
    shape = (size_x, size_y, size_z)
    along_x = (lax.broadcasted_iota(jnp.int32, shape, 0) % CX >= CX // 2).astype(jnp.int32)
    along_y = (lax.broadcasted_iota(jnp.int32, shape, 1) % CY >= CY // 2).astype(jnp.int32)
    along_z = (lax.broadcasted_iota(jnp.int32, shape, 2) % CZ >= CZ // 2).astype(jnp.int32)
    return 4 * along_x + 2 * along_y + along_z

def evaluate(spin_now, pair_weight, mix_weight, mix_bias, out_weight):
    padded = jnp.pad(spin_now, ((0, 0), (0, 0), (1, 1), (1, 1), (0, 0)), mode='wrap')

    def plane_coeff(position):
        slab_block = lax.dynamic_slice_in_dim(padded, position, 3, 2)
        return coefficients(slab_block[:, :, 1:2, 1:-1], slab_block, pair_weight, mix_weight, mix_bias, out_weight)
    planes = lax.map(plane_coeff, jnp.arange(NX, dtype=jnp.int32))
    coeff_all = jnp.moveaxis(planes[:, :, :, 0], 0, 2)
    coeff_padded = jnp.pad(coeff_all, ((0, 0), (0, 0), (1, 1), (1, 1), (0, 0)), mode='wrap')
    return field_from(coeff_all, coeff_padded, padded)

def reference(spin_vectors, pair_weight, mix_weight, mix_bias, out_weight):
    sector = sectors(NX, NY, CZ)
    spin_now = spin_vectors
    for colour in range(8):
        field_now = evaluate(spin_now, pair_weight, mix_weight, mix_bias, out_weight)
        spin_now = jnp.where(sector[None, None] == colour, rotate(spin_now, field_now), spin_now)
    return (spin_now, evaluate(spin_now, pair_weight, mix_weight, mix_bias, out_weight))
```

```python
import functools

import jax
import jax.numpy as jnp
from jax import lax
from jax.experimental import pallas as pl
from jax.experimental.pallas import tpu as pltpu
from jax.sharding import PartitionSpec as P

NB = 8
TIME_STEP = 0.1
PAD = 8
OP = 16
LANES = 128
REACH = 12

FIRST = [(x, y, z) for x in (-1, 0) for y in (-1, 0) for z in (-1, 0)]
SECOND = [(1, 0, 0), (-1, 0, 0), (0, 1, 0), (0, -1, 0), (0, 0, 1), (0, 0, -1)]


def bonds(a):
    sign = 1 if a == 0 else -1
    first = [(1 - a, sign * x, sign * y, sign * z) for x, y, z in FIRST]
    return first + [(a, *e) for e in SECOND]


def mate_of(o):
    return o if o < 8 else 8 + ((o - 8) ^ 1)


def versions(a):
    s = 1 if a == 0 else -1
    return [(0, 0), (s, 0), (0, s), (s, s), (-s, 0), (0, -s)]


class Plane:
    def __init__(self, gx, yz, bx, by, rows=8):
        self.bx, self.by, self.yz, self.cells = bx, by, yz, bx * by
        self.nl = gx * yz * bx * by
        self.nt = self.nl // LANES
        self.lane = lax.broadcasted_iota(jnp.int32, (rows, LANES), 1)
        self.rows = rows

    def at(self, t):
        lane = self.lane + t * LANES
        return (lane // self.by) % self.bx, lane % self.by, (lane // self.cells) % self.yz

    def roll(self, v, s):
        s = s % self.nl
        q, r = divmod(s, LANES)
        nt = self.nt
        if r == 0:
            return [v[(t + q) % nt] for t in range(nt)]
        rot = [pltpu.roll(x, LANES - r, axis=1) for x in v]
        if nt == 1:
            return rot
        keep = self.lane < LANES - r
        return [jnp.where(keep, rot[(t + q) % nt], rot[(t + q + 1) % nt]) for t in range(nt)]

    def step_x(self, v, d):
        if d == 0:
            return v
        ring = self.cells * self.yz
        inner = self.roll(v, d * self.by)
        outer = self.roll(v, d * (ring - (self.bx - 1) * self.by))
        edge = self.bx - 1 if d > 0 else 0
        return [jnp.where(self.at(t)[0] == edge, outer[t], inner[t]) for t in range(self.nt)]

    def step_y(self, v, d):
        if d == 0:
            return v
        ring = self.cells * self.yz
        hop = d * (self.cells - (self.by - 1))
        inner = self.roll(v, d)
        outer = self.roll(v, hop)
        wrap = self.roll(v, hop - d * ring)
        edge = self.by - 1 if d > 0 else 0
        last = self.yz - 1 if d > 0 else 0
        out = []
        for t in range(self.nt):
            _, yl, brick = self.at(t)
            far = jnp.where(brick == last, wrap[t], outer[t])
            out.append(jnp.where(yl == edge, far, inner[t]))
        return out

    def step(self, v, dx, dy):
        return self.step_x(self.step_y(v, dy), dx)


def split(x):
    hi = x.astype(jnp.bfloat16)
    return hi, (x - hi.astype(jnp.float32)).astype(jnp.bfloat16)


def pack_kernel(n, sz, rep, half, halo, x_ref, out_ref, ext):
    rows, cz = x_ref.shape
    x = jnp.concatenate([x_ref[...], jnp.zeros((LANES - rows, cz), jnp.float32)], 0)
    cells = x.T
    ext[pl.ds(0, cz), :] = cells
    ext[pl.ds(cz, half), :] = cells[:half]
    upper = pltpu.roll(ext[pl.ds(half, cz), :], LANES // 2, axis=1)
    lane = lax.broadcasted_iota(jnp.int32, (cz, LANES), 1)
    both = jnp.where(lane < LANES // 2, cells, upper)
    ext[pl.ds(half, cz), :] = both
    ext[pl.ds(0, half), :] = both[cz - half :]

    def send(d, carry):
        start = (d // rep) * sz - halo + half
        out_ref[d] = ext[pl.ds(start, half), :]
        return carry

    lax.fori_loop(0, n, send, 0, unroll=8)


def unpack_kernel(in_ref, out_ref):
    out_ref[...] = in_ref[...].T[: out_ref.shape[0]]


def sweep_kernel(
    gx, yz, bx, by, cz, sz, rep, half, halo,
    recv_ref, pair_ref, mix_ref, bias_ref, outw_ref,
    out_ref,
    spin, spin2, ver, cosv, grad, w1, w2, bias,
):
    pp = Plane(gx, yz, bx, by)
    nt, cells = pp.nt, pp.cells
    rows = spin.shape[2]
    stride = 2 * rows
    blk = LANES // cells
    window = 2 * half

    parts = []
    for k in range(NB):
        part = pair_ref[pl.ds(k, 14, stride=NB), :]
        parts.append(jnp.concatenate([part, jnp.zeros((OP - 14, part.shape[1]), jnp.float32)], 0))
    pair = jnp.concatenate(parts, 0)
    w = jnp.dot(pair, mix_ref[...], precision=lax.Precision.HIGHEST, preferred_element_type=jnp.float32)
    hi, lo = split(w.T)
    w1[...] = jnp.concatenate(
        [jnp.concatenate([hi, hi], 1), jnp.concatenate([lo, lo], 1)], 0
    )
    degree = lax.broadcasted_iota(jnp.int32, w.shape, 0) // OP + 1
    hi, lo = split(w * degree.astype(jnp.float32) * outw_ref[...])
    w2[...] = jnp.concatenate(
        [jnp.concatenate([hi, hi], 1), jnp.concatenate([lo, lo], 1)], 0
    )
    bias[...] = jnp.broadcast_to(bias_ref[...], (LANES, bias_ref.shape[1])).T

    lane16 = lax.broadcasted_iota(jnp.int32, (half, LANES), 1) // cells

    def gather(t, carry):
        moved = []
        for k in range(blk):
            v = recv_ref[t * blk + k]
            moved.append(pltpu.roll(v, k * cells, axis=1) if k else v)
        for ca in range(6):
            for h in range(2):
                j = ca + h * (LANES // 2 // cells)
                u = moved[0]
                for k in range(1, blk):
                    u = jnp.where(lane16 == (j + k) % blk, moved[k], u)
                if j:
                    u = pltpu.roll(u, LANES - j * cells, axis=1)
                spin[ca, t, pl.ds(PAD + h * half, half), :] = u
                spin2[ca, t, pl.ds(PAD + h * half, half), :] = u
        return carry

    if nt <= 2:
        for t in range(nt):
            gather(t, 0)
    else:
        lax.fori_loop(0, nt, gather, 0)
    for t in range(nt):
        cosv[t, pl.ds(14 * stride, 2 * stride), :] = jnp.zeros((2 * stride, LANES), jnp.float32)

    me = lax.axis_index("gx") * yz + lax.axis_index("yz")
    z0 = (me // rep) * sz
    hz = cz // 2
    zs = (z0 - halo + cz) % cz
    first = ((zs + hz - 1) // hz) * hz
    inside = first - zs < window
    border = PAD + first - zs
    hi_above = first % cz == hz
    own = PAD + halo

    def is_hi(row):
        z = row - PAD + zs
        z = jnp.where(z >= cz, z - cz, z)
        return z >= hz

    low, high = own - 2, own + sz + 2
    ranges = []
    for _ in range(4):
        near_low = inside & hi_above & (border > low - 2) & (border < low + 2)
        near_high = inside & jnp.logical_not(hi_above) & (border > high - 2) & (border < high + 2)
        f_low = jnp.where(near_low, low - 2, low)
        f_high = jnp.where(near_high, high + 2, high)
        ranges.append((f_low, f_high))
        low, high = f_low - 2, f_high + 2
    ranges = ranges[::-1]

    def shifted_spins(start, count):
        def body(i, carry):
            r = start + 8 * i
            for ca in range(6):
                v = [spin[ca, t, pl.ds(r, 8), :] for t in range(nt)]
                a = ca % 2
                xs = {}
                for n, (dx, dy) in enumerate(versions(a)):
                    if n == 0:
                        continue
                    if dx and dy:
                        got = pp.step_x(xs[(0, dy)], dx)
                    else:
                        got = pp.step(v, dx, dy)
                    xs[(dx, dy)] = got
                    for t in range(nt):
                        ver[n - 1, ca, t, pl.ds(r, 8), :] = got[t]
            return carry

        lax.fori_loop(0, count, body, 0)

    def neighbour(c, a, dx, dy, t, r):
        n = versions(a).index((dx, dy))
        if n == 0:
            return spin[2 * c + a, t, pl.ds(r, 8), :]
        return ver[n - 1, 2 * c + a, t, pl.ds(r, 8), :]

    def cosines(start, count):
        def body(i, carry):
            r = start + 8 * i
            for t in range(nt):
                for a in range(2):
                    mine = [spin[2 * c + a, t, pl.ds(r, 8), :] for c in range(3)]
                    for o, (b, dx, dy, dz) in enumerate(bonds(a)):
                        total = mine[0] * neighbour(0, b, dx, dy, t, r + dz)
                        for c in (1, 2):
                            total += mine[c] * neighbour(c, b, dx, dy, t, r + dz)
                        cosv[t, pl.ds(o * stride + a * rows + r, 8), :] = total
            return carry

        lax.fori_loop(0, count, body, 0)

    tc = 2 if nt % 2 == 0 else 1
    chunks = nt // tc

    def gradients(start, count):
        def body(i, carry):
            if chunks == 1:
                r, t0 = start + 2 * i, 0
            else:
                r, t0 = start + 2 * (i // chunks), (i % chunks) * tc
            places = [(d, a, t) for d in range(2) for a in range(2) for t in range(tc)]
            c = jnp.concatenate(
                [cosv[t0 + t, pl.ds(a * rows + r + d, OP, stride=stride), :] for d, a, t in places], 1
            )
            c2 = c + c
            kinds = [c, c2 * c - 1.0]
            for _ in range(2, NB):
                kinds.append(c2 * kinds[-1] - kinds[-2])
            f_hi, f_lo = split(jnp.concatenate(kinds, 0))
            z = jnp.dot(w1[...], jnp.concatenate([f_hi, f_lo], 0), preferred_element_type=jnp.float32)
            hid = z[:LANES] + z[LANES:]
            hid = hid + jnp.concatenate([bias[...]] * len(places), 1)
            u = jnp.tanh(hid)
            d_hi, d_lo = split(1.0 - u * u)
            y = jnp.dot(w2[...], jnp.concatenate([d_hi, d_lo], 0), preferred_element_type=jnp.float32)
            y = y[:LANES] + y[LANES:]
            b1 = y[(NB - 1) * OP :]
            b2 = None
            for k in range(NB - 2, -1, -1):
                new = y[k * OP : (k + 1) * OP] + c2 * b1
                if b2 is not None:
                    new = new - b2
                b1, b2 = new, b1
            for n, (d, a, t) in enumerate(places):
                grad[t0 + t, pl.ds(a * rows + r + d, OP, stride=stride), :] = b1[:, n * LANES : (n + 1) * LANES]
            return carry

        lax.fori_loop(0, count * chunks, body, 0)

    def field(r):
        out = []
        for a in range(2):
            total = [[None] * nt for _ in range(3)]
            for o, (b, dx, dy, dz) in enumerate(bonds(a)):
                m = mate_of(o)
                theirs = [grad[t, pl.ds(m * stride + b * rows + r + dz, 8), :] for t in range(nt)]
                theirs = pp.step(theirs, dx, dy)
                for t in range(nt):
                    coeff = grad[t, pl.ds(o * stride + a * rows + r, 8), :] + theirs[t]
                    for c in range(3):
                        term = coeff * neighbour(c, b, dx, dy, t, r + dz)
                        total[c][t] = term if total[c][t] is None else total[c][t] + term
            out.append([[-x for x in per] for per in total])
        return out

    def update(start, count, stage, only_border):
        def body(i, carry):
            r = start + 8 * i
            row = lax.broadcasted_iota(jnp.int32, (8, LANES), 0) + r
            from_border = jnp.where(hi_above, row - border, border - 1 - row)
            wanted = jnp.logical_not(only_border) | ((from_border >= 0) & (from_border < 2))
            h = field(r)
            for a in range(2):
                for t in range(nt):
                    xl, yl, _ = pp.at(t)
                    mask = (
                        ((xl >= bx // 2).astype(jnp.int32) == stage // 2)
                        & ((yl >= by // 2).astype(jnp.int32) == stage % 2)
                        & wanted
                    )
                    s = [spin[2 * c + a, t, pl.ds(r, 8), :] for c in range(3)]
                    w = [TIME_STEP * h[a][c][t] for c in range(3)]
                    half_r = 0.5 * jnp.sqrt(w[0] * w[0] + w[1] * w[1] + w[2] * w[2])
                    sn, cs = jnp.sin(half_r), jnp.cos(half_r)
                    zero = half_r == 0.0
                    hs = jnp.where(zero, 1.0, sn / jnp.where(zero, 1.0, half_r))
                    cosr = 1.0 - 2.0 * sn * sn
                    sinc = hs * cs
                    proj = 0.5 * hs * hs * (w[0] * s[0] + w[1] * s[1] + w[2] * s[2])
                    for c in range(3):
                        p, q = (c + 1) % 3, (c + 2) % 3
                        cross = w[p] * s[q] - w[q] * s[p]
                        new = cosr * s[c] + sinc * cross + proj * w[c]
                        old = spin2[2 * c + a, t, pl.ds(r, 8), :]
                        spin2[2 * c + a, t, pl.ds(r, 8), :] = jnp.where(mask, new, old)
            return carry

        lax.fori_loop(0, count, body, 0)

    def take(everything):
        for i in range(window // 8):
            r = PAD + 8 * i
            row = lax.broadcasted_iota(jnp.int32, (8, LANES), 0) + r
            sel = everything | jnp.logical_not(is_hi(row))
            for ca in range(6):
                for t in range(nt):
                    place = (ca, t, pl.ds(r, 8), slice(None))
                    spin[place] = jnp.where(sel, spin2[place], spin[place])

    def phase(p, carry):
        stage, fix = p // 2, p % 2 == 1
        f_low, f_high = ranges[0]
        for s in range(1, 5):
            lo_s, hi_s = ranges[s] if s < 4 else (own, own + sz)
            f_low = jnp.where(stage == s, lo_s, f_low)
            f_high = jnp.where(stage == s, hi_s, f_high)
        n = f_high - f_low
        last = stage == 4
        crosses = inside & (f_low < border) & (border < f_high)

        @pl.when(jnp.logical_not(fix) | crosses)
        def _():
            shifted_spins(jnp.where(fix, border - 4, f_low - 2), jnp.where(fix, 1, (n + 11) // 8))
            cosines(jnp.where(fix, border - 4, f_low - 1), jnp.where(fix, 1, (n + 9) // 8))
            gradients(jnp.where(fix, border - 1, f_low - 1), jnp.where(fix, 1, (n + 3) // 2))

            @pl.when(jnp.logical_not(last))
            def _():
                update(
                    jnp.where(fix, border - 4, f_low), jnp.where(fix, 1, (n + 7) // 8), stage, fix
                )
                take(fix | jnp.logical_not(crosses))

        return carry

    lax.fori_loop(0, 9, phase, 0)

    final = field(own)
    lane16s = lax.broadcasted_iota(jnp.int32, (8, LANES), 1) // cells
    for t in range(nt):
        moved = []
        for j in range(12):
            ca = j % 6
            v = spin[ca, t, pl.ds(own, 8), :] if j < 6 else final[ca % 2][ca // 2][t]
            moved.append(pltpu.roll(v, j * cells, axis=1) if j else v)
        for k in range(blk):
            u = moved[0]
            for j in range(1, 12):
                u = jnp.where(lane16s == (j + k) % blk, moved[j], u)
            if k:
                u = pltpu.roll(u, LANES - k * cells, axis=1)
            out_ref[t * blk + k] = u[:sz]


def per_device(gx, yz, spin_vectors, pair_weight, mix_weight, mix_bias, out_weight):
    three, two, bx, by, cz = spin_vectors.shape
    n = gx * yz
    sz = max(1, cz // n)
    rep = n * sz // cz
    half = -(-(sz + 2 * REACH) // 16) * 8
    halo = (2 * half - sz) // 2
    rows = 2 * half + 2 * PAD
    nt = n * bx * by // LANES
    brick = three * two * bx * by
    vmem = pl.BlockSpec(memory_space=pltpu.VMEM)

    packed = pl.pallas_call(
        functools.partial(pack_kernel, n, sz, rep, half, halo),
        out_shape=jax.ShapeDtypeStruct((n, half, LANES), jnp.float32),
        in_specs=[vmem],
        out_specs=vmem,
        scratch_shapes=[pltpu.VMEM((cz + 2 * half, LANES), jnp.float32)],
        name="pack",
    )(spin_vectors.reshape(brick, cz))
    received = lax.all_to_all(packed, ("gx", "yz"), 0, 0, tiled=True)

    f32, bf16 = jnp.float32, jnp.bfloat16
    result = pl.pallas_call(
        functools.partial(sweep_kernel, gx, yz, bx, by, cz, sz, rep, half, halo),
        out_shape=jax.ShapeDtypeStruct((n, sz, LANES), f32),
        in_specs=[vmem] * 5,
        out_specs=vmem,
        scratch_shapes=[
            pltpu.VMEM((6, nt, rows, LANES), f32),
            pltpu.VMEM((6, nt, rows, LANES), f32),
            pltpu.VMEM((5, 6, nt, rows, LANES), f32),
            pltpu.VMEM((nt, OP * 2 * rows, LANES), f32),
            pltpu.VMEM((nt, OP * 2 * rows, LANES), f32),
            pltpu.VMEM((2 * LANES, 2 * LANES), bf16),
            pltpu.VMEM((2 * LANES, 2 * LANES), bf16),
            pltpu.VMEM((LANES, LANES), f32),
        ],
        compiler_params=pltpu.CompilerParams(vmem_limit_bytes=58 * 2**20),
        name="sweep",
    )(received, pair_weight, mix_weight, mix_bias[None], out_weight[None])
    returned = lax.all_to_all(result, ("gx", "yz"), 0, 0, tiled=True)
    if rep > 1:
        returned = returned[::rep]

    both = pl.pallas_call(
        unpack_kernel,
        out_shape=jax.ShapeDtypeStruct((2 * brick, cz), f32),
        in_specs=[vmem],
        out_specs=vmem,
        name="unpack",
    )(returned.reshape(cz, LANES))
    both = both.reshape(2, three, two, bx, by, cz)
    return both[0], both[1]


def solution(mesh):
    gx, yz = mesh.shape["gx"], mesh.shape["yz"]
    spec = P(None, None, "gx", "yz", None)
    return jax.shard_map(
        functools.partial(per_device, gx, yz),
        mesh=mesh,
        in_specs=(spec, P(), P(), P(), P()),
        out_specs=(spec, spec),
        check_vma=False,
    )
```

```python
import functools
import math

import jax
import jax.numpy as jnp
from jax import lax
from jax.experimental import pallas as pl
from jax.experimental.pallas import tpu as pltpu
from jax.sharding import PartitionSpec as P

NB = 8
TIME_STEP = 0.1
PAD = 8
OP = 16
LANES = 128
REACH = 12

FIRST = [(x, y, z) for x in (-1, 0) for y in (-1, 0) for z in (-1, 0)]
SECOND = [(1, 0, 0), (-1, 0, 0), (0, 1, 0), (0, -1, 0), (0, 0, 1), (0, 0, -1)]


def bonds(a):
    sign = 1 if a == 0 else -1
    first = [(1 - a, sign * x, sign * y, sign * z) for x, y, z in FIRST]
    return first + [(a, *e) for e in SECOND]


def mate_of(o):
    return o if o < 8 else 8 + ((o - 8) ^ 1)


def versions(a):
    s = 1 if a == 0 else -1
    return [(0, 0), (s, 0), (0, s), (s, s), (-s, 0), (0, -s)]


class Plane:
    def __init__(self, gx, yz, bx, by, rows=8):
        self.bx, self.by, self.yz, self.cells = bx, by, yz, bx * by
        self.nl = gx * yz * bx * by
        self.nt = self.nl // LANES
        self.lane = lax.broadcasted_iota(jnp.int32, (rows, LANES), 1)
        self.rows = rows

    def at(self, t):
        lane = self.lane + t * LANES
        return (lane // self.by) % self.bx, lane % self.by, (lane // self.cells) % self.yz

    def roll(self, v, s):
        s = s % self.nl
        q, r = divmod(s, LANES)
        nt = self.nt
        if r == 0:
            return [v[(t + q) % nt] for t in range(nt)]
        rot = [pltpu.roll(x, LANES - r, axis=1) for x in v]
        if nt == 1:
            return rot
        keep = self.lane < LANES - r
        return [jnp.where(keep, rot[(t + q) % nt], rot[(t + q + 1) % nt]) for t in range(nt)]

    def step_x(self, v, d):
        if d == 0:
            return v
        ring = self.cells * self.yz
        inner = self.roll(v, d * self.by)
        outer = self.roll(v, d * (ring - (self.bx - 1) * self.by))
        edge = self.bx - 1 if d > 0 else 0
        return [jnp.where(self.at(t)[0] == edge, outer[t], inner[t]) for t in range(self.nt)]

    def step_y(self, v, d):
        if d == 0:
            return v
        ring = self.cells * self.yz
        hop = d * (self.cells - (self.by - 1))
        inner = self.roll(v, d)
        outer = self.roll(v, hop)
        wrap = self.roll(v, hop - d * ring)
        edge = self.by - 1 if d > 0 else 0
        last = self.yz - 1 if d > 0 else 0
        out = []
        for t in range(self.nt):
            _, yl, brick = self.at(t)
            far = jnp.where(brick == last, wrap[t], outer[t])
            out.append(jnp.where(yl == edge, far, inner[t]))
        return out

    def step(self, v, dx, dy):
        return self.step_x(self.step_y(v, dy), dx)


def split(x):
    hi = x.astype(jnp.bfloat16)
    return hi, (x - hi.astype(jnp.float32)).astype(jnp.bfloat16)


def half_turn(square):
    v = jnp.sqrt(square)
    n = jnp.round(v * (1.0 / math.pi))
    p = ((v - n * 3.140625) - n * 9.67502593994140625e-4) - n * 1.5099579909783764e-7
    s = p * p
    sine, cosine = -1.0 / 39916800, 1.0 / 479001600
    for k in (9, 7, 5, 3, 1):
        sine = sine * s + (-1.0) ** (k // 2) / math.factorial(k)
    for k in (10, 8, 6, 4, 2, 0):
        cosine = cosine * s + (-1.0) ** (k // 2) / math.factorial(k)
    sn = sine * p
    small = n == 0.0
    return sn, cosine, jnp.where(small, sine, sn / jnp.where(small, 1.0, v))


def pack_kernel(n, sz, rep, half, halo, x_ref, out_ref, ext):
    rows, cz = x_ref.shape
    x = jnp.concatenate([x_ref[...], jnp.zeros((LANES - rows, cz), jnp.float32)], 0)
    cells = x.T
    ext[pl.ds(0, cz), :] = cells
    ext[pl.ds(cz, half), :] = cells[:half]
    upper = pltpu.roll(ext[pl.ds(half, cz), :], LANES // 2, axis=1)
    lane = lax.broadcasted_iota(jnp.int32, (cz, LANES), 1)
    both = jnp.where(lane < LANES // 2, cells, upper)
    ext[pl.ds(half, cz), :] = both
    ext[pl.ds(0, half), :] = both[cz - half :]

    def send(d, carry):
        start = (d // rep) * sz - halo + half
        out_ref[d] = ext[pl.ds(start, half), :]
        return carry

    lax.fori_loop(0, n, send, 0, unroll=8)


def unpack_kernel(in_ref, spin_ref, field_ref):
    x = in_ref[...].T
    n = spin_ref.shape[0]
    spin_ref[...] = x[:n]
    field_ref[...] = x[n : 2 * n]


def sweep_kernel(
    gx, yz, bx, by, cz, sz, rep, half, halo,
    recv_ref, pair_ref, mix_ref, bias_ref, outw_ref,
    out_ref,
    spin, spin2, ver, cosv, grad, w1, w2, hidden,
):
    pp = Plane(gx, yz, bx, by)
    nt, cells = pp.nt, pp.cells
    rows = spin.shape[2]
    stride = 2 * rows + 1
    blk = LANES // cells
    window = 2 * half

    parts = []
    for k in range(NB):
        part = pair_ref[pl.ds(k, 14, stride=NB), :]
        parts.append(jnp.concatenate([part, jnp.zeros((OP - 14, part.shape[1]), jnp.float32)], 0))
    pair = jnp.concatenate(parts, 0)
    w = jnp.dot(pair, mix_ref[...], precision=lax.Precision.HIGHEST, preferred_element_type=jnp.float32)
    row = lax.broadcasted_iota(jnp.int32, w.shape, 0)
    shift = bias_ref[...]
    rest = shift - split(shift)[0].astype(jnp.float32)
    rest = rest - split(rest)[0].astype(jnp.float32)
    hi, lo = split(jnp.where(row == 14, shift, jnp.where(row == 15, rest, w)).T)
    w1[...] = jnp.concatenate(
        [jnp.concatenate([hi, hi], 1), jnp.concatenate([lo, lo], 1)], 0
    )
    degree = lax.broadcasted_iota(jnp.int32, w.shape, 0) // OP + 1
    hi, lo = split(w * degree.astype(jnp.float32) * outw_ref[...])
    w2[...] = jnp.concatenate(
        [jnp.concatenate([hi, hi], 1), jnp.concatenate([lo, lo], 1)], 0
    )

    lane16 = lax.broadcasted_iota(jnp.int32, (half, LANES), 1) // cells

    def gather(t, carry):
        moved = []
        for k in range(blk):
            v = recv_ref[t * blk + k]
            moved.append(pltpu.roll(v, k * cells, axis=1) if k else v)
        for ca in range(6):
            for h in range(2):
                j = ca + h * (LANES // 2 // cells)
                u = moved[0]
                for k in range(1, blk):
                    u = jnp.where(lane16 == (j + k) % blk, moved[k], u)
                if j:
                    u = pltpu.roll(u, LANES - j * cells, axis=1)
                spin[ca, t, pl.ds(PAD + h * half, half), :] = u
                spin2[ca, t, pl.ds(PAD + h * half, half), :] = u
        return carry

    if nt <= 2:
        for t in range(nt):
            gather(t, 0)
    else:
        lax.fori_loop(0, nt, gather, 0)
    for t in range(nt):
        cosv[t, pl.ds(14 * stride, 2 * stride), :] = jnp.ones((2 * stride, LANES), jnp.float32)

    me = lax.axis_index("gx") * yz + lax.axis_index("yz")
    z0 = (me // rep) * sz
    hz = cz // 2
    zs = (z0 - halo + cz) % cz
    first = ((zs + hz - 1) // hz) * hz
    inside = first - zs < window
    border = PAD + first - zs
    hi_above = first % cz == hz
    own = PAD + halo

    def is_hi(row):
        z = row - PAD + zs
        z = jnp.where(z >= cz, z - cz, z)
        return z >= hz

    low, high = own - 2, own + sz + 2
    ranges = []
    for _ in range(4):
        near_low = inside & hi_above & (border > low - 2) & (border < low + 2)
        near_high = inside & jnp.logical_not(hi_above) & (border > high - 2) & (border < high + 2)
        f_low = jnp.where(near_low, low - 2, low)
        f_high = jnp.where(near_high, high + 2, high)
        ranges.append((f_low, f_high))
        low, high = f_low - 2, f_high + 2
    ranges = ranges[::-1]

    def shifted_spins(start, count):
        def body(i, carry):
            r = start + 8 * i
            for ca in range(6):
                v = [spin[ca, t, pl.ds(r, 8), :] for t in range(nt)]
                a = ca % 2
                xs = {}
                for n, (dx, dy) in enumerate(versions(a)):
                    if n == 0:
                        continue
                    if dx and dy:
                        got = pp.step_x(xs[(0, dy)], dx)
                    else:
                        got = pp.step(v, dx, dy)
                    xs[(dx, dy)] = got
                    for t in range(nt):
                        ver[n - 1, ca, t, pl.ds(r, 8), :] = got[t]
            return carry

        lax.fori_loop(0, count, body, 0)

    def neighbour(c, a, dx, dy, t, r):
        n = versions(a).index((dx, dy))
        if n == 0:
            return spin[2 * c + a, t, pl.ds(r, 8), :]
        return ver[n - 1, 2 * c + a, t, pl.ds(r, 8), :]

    def cosines(start, count):
        def body(i, carry):
            r = start + 8 * i
            for t in range(nt):
                for a in range(2):
                    mine = [spin[2 * c + a, t, pl.ds(r, 8), :] for c in range(3)]
                    for o, (b, dx, dy, dz) in enumerate(bonds(a)):
                        total = mine[0] * neighbour(0, b, dx, dy, t, r + dz)
                        for c in (1, 2):
                            total += mine[c] * neighbour(c, b, dx, dy, t, r + dz)
                        cosv[t, pl.ds(o * stride + a * rows + r, 8), :] = total
            return carry

        lax.fori_loop(0, count, body, 0)

    tc = 2 if nt % 2 == 0 else 1
    chunks = nt // tc

    def gradients(start, count):
        places = [(d, a, t) for d in range(2) for a in range(2) for t in range(tc)]

        def place(i):
            if chunks == 1:
                return start + 2 * i, 0
            return start + 2 * (i // chunks), (i % chunks) * tc

        def cosine(i):
            r, t0 = place(i)
            return jnp.concatenate(
                [cosv[t0 + t, pl.ds(a * rows + r + d, OP, stride=stride), :] for d, a, t in places], 1
            )

        def basis(i):
            c = cosine(i)
            c2 = c + c
            kinds = [c, c2 * c - 1.0]
            for _ in range(2, NB):
                kinds.append(c2 * kinds[-1] - kinds[-2])
            f_hi, f_lo = split(jnp.concatenate(kinds, 0))
            return jnp.concatenate([f_hi, f_lo], 0)

        def forward(rhs):
            z = jnp.dot(w1[...], rhs, preferred_element_type=jnp.float32)
            hidden[...] = z[:LANES] + z[LANES:]

        def activate():
            u = jnp.tanh(hidden[...])
            d_hi, d_lo = split(1.0 - u * u)
            return jnp.concatenate([d_hi, d_lo], 0)

        def backward(rhs):
            y = jnp.dot(w2[...], rhs, preferred_element_type=jnp.float32)
            return y[:LANES] + y[LANES:]

        def combine(i, y):
            r, t0 = place(i)
            c2 = 2.0 * cosine(i)
            b1 = y[(NB - 1) * OP :]
            b2 = None
            for k in range(NB - 2, -1, -1):
                new = y[k * OP : (k + 1) * OP] + c2 * b1
                if b2 is not None:
                    new = new - b2
                b1, b2 = new, b1
            for n, (d, a, t) in enumerate(places):
                grad[t0 + t, pl.ds(a * rows + r + d, OP, stride=stride), :] = b1[:, n * LANES : (n + 1) * LANES]

        forward(basis(0))

        def body(i, carry):
            rhs2 = activate()
            rhs1 = basis(i)
            y = backward(rhs2)
            forward(rhs1)
            combine(i - 1, y)
            return carry

        lax.fori_loop(1, count * chunks, body, 0)
        combine(count * chunks - 1, backward(activate()))

    def field(r):
        out = []
        for a in range(2):
            total = [[None] * nt for _ in range(3)]
            for o, (b, dx, dy, dz) in enumerate(bonds(a)):
                m = mate_of(o)
                theirs = [grad[t, pl.ds(m * stride + b * rows + r + dz, 8), :] for t in range(nt)]
                theirs = pp.step(theirs, dx, dy)
                for t in range(nt):
                    coeff = grad[t, pl.ds(o * stride + a * rows + r, 8), :] + theirs[t]
                    for c in range(3):
                        term = coeff * neighbour(c, b, dx, dy, t, r + dz)
                        total[c][t] = term if total[c][t] is None else total[c][t] + term
            out.append([[-x for x in per] for per in total])
        return out

    def update(start, count, stage, only_border):
        def body(i, carry):
            r = start + 8 * i
            row = lax.broadcasted_iota(jnp.int32, (8, LANES), 0) + r
            from_border = jnp.where(hi_above, row - border, border - 1 - row)
            wanted = jnp.logical_not(only_border) | ((from_border >= 0) & (from_border < 2))
            h = field(r)
            for a in range(2):
                for t in range(nt):
                    xl, yl, _ = pp.at(t)
                    mask = (
                        ((xl >= bx // 2).astype(jnp.int32) == stage // 2)
                        & ((yl >= by // 2).astype(jnp.int32) == stage % 2)
                        & wanted
                    )
                    s = [spin[2 * c + a, t, pl.ds(r, 8), :] for c in range(3)]
                    w = [TIME_STEP * h[a][c][t] for c in range(3)]
                    square = 0.25 * (w[0] * w[0] + w[1] * w[1] + w[2] * w[2])
                    sn, cs, hs = half_turn(square)
                    cosr = 1.0 - 2.0 * sn * sn
                    sinc = hs * cs
                    proj = 0.5 * hs * hs * (w[0] * s[0] + w[1] * s[1] + w[2] * s[2])
                    for c in range(3):
                        p, q = (c + 1) % 3, (c + 2) % 3
                        cross = w[p] * s[q] - w[q] * s[p]
                        new = cosr * s[c] + sinc * cross + proj * w[c]
                        old = spin2[2 * c + a, t, pl.ds(r, 8), :]
                        spin2[2 * c + a, t, pl.ds(r, 8), :] = jnp.where(mask, new, old)
            return carry

        lax.fori_loop(0, count, body, 0)

    def take(everything):
        for i in range(window // 8):
            r = PAD + 8 * i
            row = lax.broadcasted_iota(jnp.int32, (8, LANES), 0) + r
            sel = everything | jnp.logical_not(is_hi(row))
            for ca in range(6):
                for t in range(nt):
                    place = (ca, t, pl.ds(r, 8), slice(None))
                    spin[place] = jnp.where(sel, spin2[place], spin[place])

    def phase(p, carry):
        stage, fix = p // 2, p % 2 == 1
        f_low, f_high = ranges[0]
        for s in range(1, 5):
            lo_s, hi_s = ranges[s] if s < 4 else (own, own + sz)
            f_low = jnp.where(stage == s, lo_s, f_low)
            f_high = jnp.where(stage == s, hi_s, f_high)
        n = f_high - f_low
        last = stage == 4
        crosses = inside & (f_low < border) & (border < f_high)

        @pl.when(jnp.logical_not(fix) | crosses)
        def _():
            shifted_spins(jnp.where(fix, border - 4, f_low - 2), jnp.where(fix, 1, (n + 11) // 8))
            cosines(jnp.where(fix, border - 4, f_low - 1), jnp.where(fix, 1, (n + 9) // 8))
            gradients(jnp.where(fix, border - 1, f_low - 1), jnp.where(fix, 1, (n + 3) // 2))

            @pl.when(jnp.logical_not(last))
            def _():
                update(
                    jnp.where(fix, border - 4, f_low), jnp.where(fix, 1, (n + 7) // 8), stage, fix
                )
                take(fix | jnp.logical_not(crosses))

        return carry

    lax.fori_loop(0, 9, phase, 0)

    final = field(own)
    lane16s = lax.broadcasted_iota(jnp.int32, (8, LANES), 1) // cells
    for t in range(nt):
        moved = []
        for j in range(12):
            ca = j % 6
            v = spin[ca, t, pl.ds(own, 8), :] if j < 6 else final[ca % 2][ca // 2][t]
            moved.append(pltpu.roll(v, j * cells, axis=1) if j else v)
        for k in range(blk):
            u = moved[0]
            for j in range(1, 12):
                u = jnp.where(lane16s == (j + k) % blk, moved[j], u)
            if k:
                u = pltpu.roll(u, LANES - k * cells, axis=1)
            out_ref[t * blk + k] = u[:sz]


def per_device(gx, yz, spin_vectors, pair_weight, mix_weight, mix_bias, out_weight):
    three, two, bx, by, cz = spin_vectors.shape
    n = gx * yz
    sz = max(1, cz // n)
    rep = n * sz // cz
    half = -(-(sz + 2 * REACH) // 16) * 8
    halo = (2 * half - sz) // 2
    rows = 2 * half + 2 * PAD
    nt = n * bx * by // LANES
    brick = three * two * bx * by
    vmem = pl.BlockSpec(memory_space=pltpu.VMEM)

    packed = pl.pallas_call(
        functools.partial(pack_kernel, n, sz, rep, half, halo),
        out_shape=jax.ShapeDtypeStruct((n, half, LANES), jnp.float32),
        in_specs=[vmem],
        out_specs=vmem,
        scratch_shapes=[pltpu.VMEM((cz + 2 * half, LANES), jnp.float32)],
        name="pack",
    )(spin_vectors.reshape(brick, cz))
    received = lax.all_to_all(packed, ("gx", "yz"), 0, 0, tiled=True)

    f32, bf16 = jnp.float32, jnp.bfloat16
    result = pl.pallas_call(
        functools.partial(sweep_kernel, gx, yz, bx, by, cz, sz, rep, half, halo),
        out_shape=jax.ShapeDtypeStruct((n, sz, LANES), f32),
        in_specs=[vmem] * 5,
        out_specs=vmem,
        scratch_shapes=[
            pltpu.VMEM((6, nt, rows, LANES), f32),
            pltpu.VMEM((6, nt, rows, LANES), f32),
            pltpu.VMEM((5, 6, nt, rows, LANES), f32),
            pltpu.VMEM((nt, OP * (2 * rows + 1) + 7, LANES), f32),
            pltpu.VMEM((nt, OP * (2 * rows + 1) + 7, LANES), f32),
            pltpu.VMEM((2 * LANES, 2 * LANES), bf16),
            pltpu.VMEM((2 * LANES, 2 * LANES), bf16),
            pltpu.VMEM((LANES, 4 * (2 - nt % 2) * LANES), f32),
        ],
        compiler_params=pltpu.CompilerParams(vmem_limit_bytes=58 * 2**20),
        name="sweep",
    )(received, pair_weight, mix_weight, mix_bias[None], out_weight[None])
    returned = lax.all_to_all(result, ("gx", "yz"), 0, 0, tiled=True)
    if rep > 1:
        returned = returned[::rep]

    outs = pl.pallas_call(
        unpack_kernel,
        out_shape=[jax.ShapeDtypeStruct((brick, cz), f32)] * 2,
        in_specs=[vmem],
        out_specs=[vmem] * 2,
        name="unpack",
    )(returned.reshape(cz, LANES))
    return tuple(x.reshape(three, two, bx, by, cz) for x in outs)


def solution(mesh):
    gx, yz = mesh.shape["gx"], mesh.shape["yz"]
    spec = P(None, None, "gx", "yz", None)
    return jax.shard_map(
        functools.partial(per_device, gx, yz),
        mesh=mesh,
        in_specs=(spec, P(), P(), P(), P()),
        out_specs=(spec, spec),
        check_vma=False,
    )
```

```python
import functools
import math

import jax
import jax.numpy as jnp
from jax import lax
from jax.experimental import pallas as pl
from jax.experimental.pallas import tpu as pltpu
from jax.sharding import PartitionSpec as P

NB = 8
TIME_STEP = 0.1
PAD = 8
OP = 16
LANES = 128
REACH = 12

FIRST = [(x, y, z) for x in (-1, 0) for y in (-1, 0) for z in (-1, 0)]
SECOND = [(1, 0, 0), (-1, 0, 0), (0, 1, 0), (0, -1, 0), (0, 0, 1), (0, 0, -1)]


def bonds(a):
    sign = 1 if a == 0 else -1
    first = [(1 - a, sign * x, sign * y, sign * z) for x, y, z in FIRST]
    return first + [(a, *e) for e in SECOND]


def mate_of(o):
    return o if o < 8 else 8 + ((o - 8) ^ 1)


def versions(a):
    s = 1 if a == 0 else -1
    return [(0, 0), (s, 0), (0, s), (s, s), (-s, 0), (0, -s)]


class Plane:
    def __init__(self, gx, yz, bx, by, rows=8):
        self.bx, self.by, self.yz, self.cells = bx, by, yz, bx * by
        self.nl = gx * yz * bx * by
        self.nt = self.nl // LANES
        self.lane = lax.broadcasted_iota(jnp.int32, (rows, LANES), 1)
        ring = yz * self.cells
        self.within = LANES % ring == 0
        if self.within:
            xl, yl, brick = self.at(0)
            x_at = {0: self.lane, 1: jnp.where(xl == bx - 1, self.lane + ring - (bx - 1) * by, self.lane + by),
                    -1: jnp.where(xl == 0, self.lane - ring + (bx - 1) * by, self.lane - by)}
            hop = self.cells - (by - 1)
            y_at = {0: 0, 1: jnp.where(yl < by - 1, 1, jnp.where(brick < yz - 1, hop, hop - ring)),
                    -1: jnp.where(yl > 0, -1, jnp.where(brick > 0, -hop, ring - hop))}
            self.source = {
                (dx, dy): (x_at[dx] + y_at[dy] + LANES) % LANES for dx in (-1, 0, 1) for dy in (-1, 0, 1)
            }
            self.from_next = {1: (self.lane < ring) & (xl == 0), -1: (self.lane >= LANES - ring) & (xl == bx - 1)}

    def at(self, t):
        lane = self.lane + t * LANES
        return (lane // self.by) % self.bx, lane % self.by, (lane // self.cells) % self.yz

    def roll(self, v, s):
        s = s % self.nl
        q, r = divmod(s, LANES)
        nt = self.nt
        if r == 0:
            return [v[(t + q) % nt] for t in range(nt)]
        rot = [pltpu.roll(x, LANES - r, axis=1) for x in v]
        if nt == 1:
            return rot
        keep = self.lane < LANES - r
        return [jnp.where(keep, rot[(t + q) % nt], rot[(t + q + 1) % nt]) for t in range(nt)]

    def step_x(self, v, d):
        if d == 0:
            return v
        ring = self.cells * self.yz
        inner = self.roll(v, d * self.by)
        outer = self.roll(v, d * (ring - (self.bx - 1) * self.by))
        edge = self.bx - 1 if d > 0 else 0
        return [jnp.where(self.at(t)[0] == edge, outer[t], inner[t]) for t in range(self.nt)]

    def step_y(self, v, d):
        if d == 0:
            return v
        ring = self.cells * self.yz
        hop = d * (self.cells - (self.by - 1))
        inner = self.roll(v, d)
        outer = self.roll(v, hop)
        wrap = self.roll(v, hop - d * ring)
        edge = self.by - 1 if d > 0 else 0
        last = self.yz - 1 if d > 0 else 0
        out = []
        for t in range(self.nt):
            _, yl, brick = self.at(t)
            far = jnp.where(brick == last, wrap[t], outer[t])
            out.append(jnp.where(yl == edge, far, inner[t]))
        return out

    def step(self, v, dx, dy):
        if not (dx or dy):
            return v
        if self.within:
            if dx and self.nt > 1:
                swap = self.from_next[dx]
                v = [jnp.where(swap, v[(t + dx) % self.nt], v[t]) for t in range(self.nt)]
            where = self.source[(dx, dy)]
            return [jnp.take_along_axis(x, where, axis=1, mode="promise_in_bounds") for x in v]
        return self.step_x(self.step_y(v, dy), dx)


def split(x):
    hi = x.astype(jnp.bfloat16)
    return hi, (x - hi.astype(jnp.float32)).astype(jnp.bfloat16)


def half_turn(square):
    v = jnp.sqrt(square)
    n = jnp.round(v * (1.0 / math.pi))
    p = ((v - n * 3.140625) - n * 9.67502593994140625e-4) - n * 1.5099579909783764e-7
    s = p * p
    sine, cosine = -1.0 / 39916800, 1.0 / 479001600
    for k in (9, 7, 5, 3, 1):
        sine = sine * s + (-1.0) ** (k // 2) / math.factorial(k)
    for k in (10, 8, 6, 4, 2, 0):
        cosine = cosine * s + (-1.0) ** (k // 2) / math.factorial(k)
    sn = sine * p
    small = n == 0.0
    return sn, cosine, jnp.where(small, sine, sn / jnp.where(small, 1.0, v))


def pack_kernel(n, sz, rep, half, halo, x_ref, out_ref, ext):
    rows, cz = x_ref.shape
    x = jnp.concatenate([x_ref[...], jnp.zeros((LANES - rows, cz), jnp.float32)], 0)
    cells = x.T
    ext[pl.ds(0, cz), :] = cells
    ext[pl.ds(cz, half), :] = cells[:half]
    upper = pltpu.roll(ext[pl.ds(half, cz), :], LANES // 2, axis=1)
    lane = lax.broadcasted_iota(jnp.int32, (cz, LANES), 1)
    both = jnp.where(lane < LANES // 2, cells, upper)
    ext[pl.ds(half, cz), :] = both
    ext[pl.ds(0, half), :] = both[cz - half :]

    def send(d, carry):
        start = (d // rep) * sz - halo + half
        out_ref[d] = ext[pl.ds(start, half), :]
        return carry

    lax.fori_loop(0, n, send, 0, unroll=8)


def unpack_kernel(in_ref, spin_ref, field_ref):
    x = in_ref[...].T
    n = spin_ref.shape[0]
    spin_ref[...] = x[:n]
    field_ref[...] = x[n : 2 * n]


def sweep_kernel(
    gx, yz, bx, by, cz, sz, rep, half, halo,
    recv_ref, pair_ref, mix_ref, bias_ref, outw_ref,
    out_ref,
    spin, spin2, ver, cosv, grad, w1, w2, hidden,
):
    pp = Plane(gx, yz, bx, by)
    nt, cells = pp.nt, pp.cells
    rows = spin.shape[2]
    stride = 2 * rows + 1
    blk = LANES // cells
    window = 2 * half

    parts = []
    for k in range(NB):
        part = pair_ref[pl.ds(k, 14, stride=NB), :]
        parts.append(jnp.concatenate([part, jnp.zeros((OP - 14, part.shape[1]), jnp.float32)], 0))
    pair = jnp.concatenate(parts, 0)
    w = jnp.dot(pair, mix_ref[...], precision=lax.Precision.HIGHEST, preferred_element_type=jnp.float32)
    row = lax.broadcasted_iota(jnp.int32, w.shape, 0)
    shift = bias_ref[...]
    rest = shift - split(shift)[0].astype(jnp.float32)
    rest = rest - split(rest)[0].astype(jnp.float32)
    hi, lo = split(jnp.where(row == 14, shift, jnp.where(row == 15, rest, w)).T)
    w1[...] = jnp.concatenate(
        [jnp.concatenate([hi, hi], 1), jnp.concatenate([lo, lo], 1)], 0
    )
    degree = lax.broadcasted_iota(jnp.int32, w.shape, 0) // OP + 1
    hi, lo = split(w * degree.astype(jnp.float32) * outw_ref[...])
    w2[...] = jnp.concatenate(
        [jnp.concatenate([hi, hi], 1), jnp.concatenate([lo, lo], 1)], 0
    )

    lane16 = lax.broadcasted_iota(jnp.int32, (half, LANES), 1) // cells

    def gather(t, carry):
        moved = []
        for k in range(blk):
            v = recv_ref[t * blk + k]
            moved.append(pltpu.roll(v, k * cells, axis=1) if k else v)
        for ca in range(6):
            for h in range(2):
                j = ca + h * (LANES // 2 // cells)
                u = moved[0]
                for k in range(1, blk):
                    u = jnp.where(lane16 == (j + k) % blk, moved[k], u)
                if j:
                    u = pltpu.roll(u, LANES - j * cells, axis=1)
                spin[ca, t, pl.ds(PAD + h * half, half), :] = u
                spin2[ca, t, pl.ds(PAD + h * half, half), :] = u
        return carry

    if nt <= 2:
        for t in range(nt):
            gather(t, 0)
    else:
        lax.fori_loop(0, nt, gather, 0)
    for t in range(nt):
        cosv[t, pl.ds(14 * stride, 2 * stride), :] = jnp.ones((2 * stride, LANES), jnp.float32)

    me = lax.axis_index("gx") * yz + lax.axis_index("yz")
    z0 = (me // rep) * sz
    hz = cz // 2
    zs = (z0 - halo + cz) % cz
    first = ((zs + hz - 1) // hz) * hz
    inside = first - zs < window
    border = PAD + first - zs
    hi_above = first % cz == hz
    own = PAD + halo

    def is_hi(row):
        z = row - PAD + zs
        z = jnp.where(z >= cz, z - cz, z)
        return z >= hz

    low, high = own - 2, own + sz + 2
    ranges = []
    for _ in range(4):
        near_low = inside & hi_above & (border > low - 2) & (border < low + 2)
        near_high = inside & jnp.logical_not(hi_above) & (border > high - 2) & (border < high + 2)
        f_low = jnp.where(near_low, low - 2, low)
        f_high = jnp.where(near_high, high + 2, high)
        ranges.append((f_low, f_high))
        low, high = f_low - 2, f_high + 2
    ranges = ranges[::-1]

    def shifted_spins(start, count):
        def body(i, carry):
            r = start + 8 * i
            for dx, dy in ((1, 0), (-1, 0), (0, 1), (0, -1), (1, 1), (-1, -1)):
                for ca in range(6):
                    if (dx, dy) not in versions(ca % 2):
                        continue
                    n = versions(ca % 2).index((dx, dy))
                    got = pp.step([spin[ca, t, pl.ds(r, 8), :] for t in range(nt)], dx, dy)
                    for t in range(nt):
                        ver[n - 1, ca, t, pl.ds(r, 8), :] = got[t]
            return carry

        lax.fori_loop(0, count, body, 0)

    def neighbour(c, a, dx, dy, t, r):
        n = versions(a).index((dx, dy))
        if n == 0:
            return spin[2 * c + a, t, pl.ds(r, 8), :]
        return ver[n - 1, 2 * c + a, t, pl.ds(r, 8), :]

    def cosines(start, count):
        def body(i, carry):
            r = start + 8 * i
            for t in range(nt):
                for a in range(2):
                    mine = [spin[2 * c + a, t, pl.ds(r, 8), :] for c in range(3)]
                    for o, (b, dx, dy, dz) in enumerate(bonds(a)):
                        total = mine[0] * neighbour(0, b, dx, dy, t, r + dz)
                        for c in (1, 2):
                            total += mine[c] * neighbour(c, b, dx, dy, t, r + dz)
                        cosv[t, pl.ds(o * stride + a * rows + r, 8), :] = total
            return carry

        lax.fori_loop(0, count, body, 0)

    tc = 2 if nt % 2 == 0 else 1
    chunks = nt // tc

    def gradients(start, count):
        places = [(d, a, t) for d in range(1) for a in range(2) for t in range(tc)]

        def place(i):
            if chunks == 1:
                return start + 1 * i, 0
            return start + 1 * (i // chunks), (i % chunks) * tc

        def cosine(i):
            r, t0 = place(i)
            return jnp.concatenate(
                [cosv[t0 + t, pl.ds(a * rows + r + d, OP, stride=stride), :] for d, a, t in places], 1
            )

        def basis(i):
            c = cosine(i)
            c2 = c + c
            kinds = [c, c2 * c - 1.0]
            for _ in range(2, NB):
                kinds.append(c2 * kinds[-1] - kinds[-2])
            f_hi, f_lo = split(jnp.concatenate(kinds, 0))
            return jnp.concatenate([f_hi, f_lo], 0)

        def forward(rhs, slot):
            z = jnp.dot(w1[...], rhs, preferred_element_type=jnp.float32)
            hidden[slot] = z[:LANES] + z[LANES:]

        def activate(slot):
            u = jnp.tanh(hidden[slot])
            d_hi, d_lo = split(1.0 - u * u)
            return jnp.concatenate([d_hi, d_lo], 0)

        def backward(rhs):
            y = jnp.dot(w2[...], rhs, preferred_element_type=jnp.float32)
            return y[:LANES] + y[LANES:]

        def combine(i, y):
            r, t0 = place(i)
            c2 = 2.0 * cosine(i)
            b1 = y[(NB - 1) * OP :]
            b2 = None
            for k in range(NB - 2, -1, -1):
                new = y[k * OP : (k + 1) * OP] + c2 * b1
                if b2 is not None:
                    new = new - b2
                b1, b2 = new, b1
            for n, (d, a, t) in enumerate(places):
                grad[t0 + t, pl.ds(a * rows + r + d, OP, stride=stride), :] = b1[:, n * LANES : (n + 1) * LANES]

        for k in range(2):
            forward(basis(k), k)

        def one(i, slot):
            y = backward(activate(slot))
            forward(basis(i), slot)
            combine(i - 2, y)

        total = count * chunks
        done = 2
        for many in (4, 2):
            def body(i, first, many=many):
                for k in range(many):
                    one(first + i * many + k, k % 2)
                return first

            times = (total - done) // many
            lax.fori_loop(0, times, body, done)
            done = done + times * many
        for k in range(2):
            combine(total - 2 + k, backward(activate(k)))

    def field(r):
        out = []
        for a in range(2):
            total = [[None] * nt for _ in range(3)]
            for o, (b, dx, dy, dz) in enumerate(bonds(a)):
                m = mate_of(o)
                theirs = [grad[t, pl.ds(m * stride + b * rows + r + dz, 8), :] for t in range(nt)]
                theirs = pp.step(theirs, dx, dy)
                for t in range(nt):
                    coeff = grad[t, pl.ds(o * stride + a * rows + r, 8), :] + theirs[t]
                    for c in range(3):
                        term = coeff * neighbour(c, b, dx, dy, t, r + dz)
                        total[c][t] = term if total[c][t] is None else total[c][t] + term
            out.append([[-x for x in per] for per in total])
        return out

    def update(start, count, stage, only_border):
        def body(i, carry):
            r = start + 8 * i
            row = lax.broadcasted_iota(jnp.int32, (8, LANES), 0) + r
            from_border = jnp.where(hi_above, row - border, border - 1 - row)
            wanted = jnp.logical_not(only_border) | ((from_border >= 0) & (from_border < 2))
            h = field(r)
            for a in range(2):
                for t in range(nt):
                    xl, yl, _ = pp.at(t)
                    mask = (
                        ((xl >= bx // 2).astype(jnp.int32) == stage // 2)
                        & ((yl >= by // 2).astype(jnp.int32) == stage % 2)
                        & wanted
                    )
                    s = [spin[2 * c + a, t, pl.ds(r, 8), :] for c in range(3)]
                    w = [TIME_STEP * h[a][c][t] for c in range(3)]
                    square = 0.25 * (w[0] * w[0] + w[1] * w[1] + w[2] * w[2])
                    sn, cs, hs = half_turn(square)
                    cosr = 1.0 - 2.0 * sn * sn
                    sinc = hs * cs
                    proj = 0.5 * hs * hs * (w[0] * s[0] + w[1] * s[1] + w[2] * s[2])
                    for c in range(3):
                        p, q = (c + 1) % 3, (c + 2) % 3
                        cross = w[p] * s[q] - w[q] * s[p]
                        new = cosr * s[c] + sinc * cross + proj * w[c]
                        old = spin2[2 * c + a, t, pl.ds(r, 8), :]
                        spin2[2 * c + a, t, pl.ds(r, 8), :] = jnp.where(mask, new, old)
            return carry

        lax.fori_loop(0, count, body, 0)

    def take(everything):
        for i in range(window // 8):
            r = PAD + 8 * i
            row = lax.broadcasted_iota(jnp.int32, (8, LANES), 0) + r
            sel = everything | jnp.logical_not(is_hi(row))
            for ca in range(6):
                for t in range(nt):
                    place = (ca, t, pl.ds(r, 8), slice(None))
                    spin[place] = jnp.where(sel, spin2[place], spin[place])

    def phase(p, carry):
        stage, fix = p // 2, p % 2 == 1
        f_low, f_high = ranges[0]
        for s in range(1, 5):
            lo_s, hi_s = ranges[s] if s < 4 else (own, own + sz)
            f_low = jnp.where(stage == s, lo_s, f_low)
            f_high = jnp.where(stage == s, hi_s, f_high)
        n = f_high - f_low
        last = stage == 4
        crosses = inside & (f_low < border) & (border < f_high)

        @pl.when(jnp.logical_not(fix) | crosses)
        def _():
            shifted_spins(jnp.where(fix, border - 4, f_low - 2), jnp.where(fix, 1, (n + 11) // 8))
            cosines(jnp.where(fix, border - 4, f_low - 1), jnp.where(fix, 1, (n + 9) // 8))
            gradients(jnp.where(fix, border - 1, f_low - 1), jnp.where(fix, 2, (n + 3) // 2 * 2))

            @pl.when(jnp.logical_not(last))
            def _():
                update(
                    jnp.where(fix, border - 4, f_low), jnp.where(fix, 1, (n + 7) // 8), stage, fix
                )
                take(fix | jnp.logical_not(crosses))

        return carry

    lax.fori_loop(0, 9, phase, 0)

    final = field(own)
    lane16s = lax.broadcasted_iota(jnp.int32, (8, LANES), 1) // cells
    for t in range(nt):
        moved = []
        for j in range(12):
            ca = j % 6
            v = spin[ca, t, pl.ds(own, 8), :] if j < 6 else final[ca % 2][ca // 2][t]
            moved.append(pltpu.roll(v, j * cells, axis=1) if j else v)
        for k in range(blk):
            u = moved[0]
            for j in range(1, 12):
                u = jnp.where(lane16s == (j + k) % blk, moved[j], u)
            if k:
                u = pltpu.roll(u, LANES - k * cells, axis=1)
            out_ref[t * blk + k] = u[:sz]


def per_device(gx, yz, spin_vectors, pair_weight, mix_weight, mix_bias, out_weight):
    three, two, bx, by, cz = spin_vectors.shape
    n = gx * yz
    sz = max(1, cz // n)
    rep = n * sz // cz
    half = -(-(sz + 2 * REACH) // 16) * 8
    halo = (2 * half - sz) // 2
    rows = 2 * half + 2 * PAD
    nt = n * bx * by // LANES
    brick = three * two * bx * by
    vmem = pl.BlockSpec(memory_space=pltpu.VMEM)

    packed = pl.pallas_call(
        functools.partial(pack_kernel, n, sz, rep, half, halo),
        out_shape=jax.ShapeDtypeStruct((n, half, LANES), jnp.float32),
        in_specs=[vmem],
        out_specs=vmem,
        scratch_shapes=[pltpu.VMEM((cz + 2 * half, LANES), jnp.float32)],
        name="pack",
    )(spin_vectors.reshape(brick, cz))
    received = lax.all_to_all(packed, ("gx", "yz"), 0, 0, tiled=True)

    f32, bf16 = jnp.float32, jnp.bfloat16
    result = pl.pallas_call(
        functools.partial(sweep_kernel, gx, yz, bx, by, cz, sz, rep, half, halo),
        out_shape=jax.ShapeDtypeStruct((n, sz, LANES), f32),
        in_specs=[vmem] * 5,
        out_specs=vmem,
        scratch_shapes=[
            pltpu.VMEM((6, nt, rows, LANES), f32),
            pltpu.VMEM((6, nt, rows, LANES), f32),
            pltpu.VMEM((5, 6, nt, rows, LANES), f32),
            pltpu.VMEM((nt, OP * (2 * rows + 1) + 7, LANES), f32),
            pltpu.VMEM((nt, OP * (2 * rows + 1) + 7, LANES), f32),
            pltpu.VMEM((2 * LANES, 2 * LANES), bf16),
            pltpu.VMEM((2 * LANES, 2 * LANES), bf16),
            pltpu.VMEM((2, LANES, 2 * (2 - nt % 2) * LANES), f32),
        ],
        compiler_params=pltpu.CompilerParams(vmem_limit_bytes=58 * 2**20),
        name="sweep",
    )(received, pair_weight, mix_weight, mix_bias[None], out_weight[None])
    returned = lax.all_to_all(result, ("gx", "yz"), 0, 0, tiled=True)
    if rep > 1:
        returned = returned[::rep]

    outs = pl.pallas_call(
        unpack_kernel,
        out_shape=[jax.ShapeDtypeStruct((brick, cz), f32)] * 2,
        in_specs=[vmem],
        out_specs=[vmem] * 2,
        name="unpack",
    )(returned.reshape(cz, LANES))
    return tuple(x.reshape(three, two, bx, by, cz) for x in outs)


def solution(mesh):
    gx, yz = mesh.shape["gx"], mesh.shape["yz"]
    spec = P(None, None, "gx", "yz", None)
    return jax.shard_map(
        functools.partial(per_device, gx, yz),
        mesh=mesh,
        in_specs=(spec, P(), P(), P(), P()),
        out_specs=(spec, spec),
        check_vma=False,
    )
```

```python
import functools
import math

import jax
import jax.numpy as jnp
from jax import lax
from jax.experimental import pallas as pl
from jax.experimental.pallas import tpu as pltpu
from jax.sharding import PartitionSpec as P

NB = 8
TIME_STEP = 0.1
PAD = 8
OP = 16
LANES = 128
REACH = 12

FIRST = [(x, y, z) for x in (-1, 0) for y in (-1, 0) for z in (-1, 0)]
SECOND = [(1, 0, 0), (-1, 0, 0), (0, 1, 0), (0, -1, 0), (0, 0, 1), (0, 0, -1)]


def bonds(a):
    sign = 1 if a == 0 else -1
    first = [(1 - a, sign * x, sign * y, sign * z) for x, y, z in FIRST]
    return first + [(a, *e) for e in SECOND]


def mate_of(o):
    return o if o < 8 else 8 + ((o - 8) ^ 1)


def versions(a):
    s = 1 if a == 0 else -1
    return [(0, 0), (s, 0), (0, s), (s, s), (-s, 0), (0, -s)]


class Plane:
    def __init__(self, gx, yz, bx, by, rows=8):
        self.bx, self.by, self.yz, self.cells = bx, by, yz, bx * by
        self.nl = gx * yz * bx * by
        self.nt = self.nl // LANES
        self.lane = lax.broadcasted_iota(jnp.int32, (rows, LANES), 1)
        ring = yz * self.cells
        self.within = LANES % ring == 0
        if self.within:
            xl, yl, brick = self.at(0)
            x_at = {0: self.lane, 1: jnp.where(xl == bx - 1, self.lane + ring - (bx - 1) * by, self.lane + by),
                    -1: jnp.where(xl == 0, self.lane - ring + (bx - 1) * by, self.lane - by)}
            hop = self.cells - (by - 1)
            y_at = {0: 0, 1: jnp.where(yl < by - 1, 1, jnp.where(brick < yz - 1, hop, hop - ring)),
                    -1: jnp.where(yl > 0, -1, jnp.where(brick > 0, -hop, ring - hop))}
            self.source = {
                (dx, dy): (x_at[dx] + y_at[dy] + LANES) % LANES for dx in (-1, 0, 1) for dy in (-1, 0, 1)
            }
            self.from_next = {1: (self.lane < ring) & (xl == 0), -1: (self.lane >= LANES - ring) & (xl == bx - 1)}

    def at(self, t):
        lane = self.lane + t * LANES
        return (lane // self.by) % self.bx, lane % self.by, (lane // self.cells) % self.yz

    def roll(self, v, s):
        s = s % self.nl
        q, r = divmod(s, LANES)
        nt = self.nt
        if r == 0:
            return [v[(t + q) % nt] for t in range(nt)]
        rot = [pltpu.roll(x, LANES - r, axis=1) for x in v]
        if nt == 1:
            return rot
        keep = self.lane < LANES - r
        return [jnp.where(keep, rot[(t + q) % nt], rot[(t + q + 1) % nt]) for t in range(nt)]

    def step_x(self, v, d):
        if d == 0:
            return v
        ring = self.cells * self.yz
        inner = self.roll(v, d * self.by)
        outer = self.roll(v, d * (ring - (self.bx - 1) * self.by))
        edge = self.bx - 1 if d > 0 else 0
        return [jnp.where(self.at(t)[0] == edge, outer[t], inner[t]) for t in range(self.nt)]

    def step_y(self, v, d):
        if d == 0:
            return v
        ring = self.cells * self.yz
        hop = d * (self.cells - (self.by - 1))
        inner = self.roll(v, d)
        outer = self.roll(v, hop)
        wrap = self.roll(v, hop - d * ring)
        edge = self.by - 1 if d > 0 else 0
        last = self.yz - 1 if d > 0 else 0
        out = []
        for t in range(self.nt):
            _, yl, brick = self.at(t)
            far = jnp.where(brick == last, wrap[t], outer[t])
            out.append(jnp.where(yl == edge, far, inner[t]))
        return out

    def step(self, v, dx, dy):
        if not (dx or dy):
            return v
        if self.within:
            if dx and self.nt > 1:
                swap = self.from_next[dx]
                v = [jnp.where(swap, v[(t + dx) % self.nt], v[t]) for t in range(self.nt)]
            where = self.source[(dx, dy)]
            return [jnp.take_along_axis(x, where, axis=1, mode="promise_in_bounds") for x in v]
        return self.step_x(self.step_y(v, dy), dx)


def split(x):
    hi = x.astype(jnp.bfloat16)
    return hi, (x - hi.astype(jnp.float32)).astype(jnp.bfloat16)


def half_turn(square):
    v = jnp.sqrt(square)
    n = jnp.round(v * (1.0 / math.pi))
    p = ((v - n * 3.140625) - n * 9.67502593994140625e-4) - n * 1.5099579909783764e-7
    s = p * p
    sine, cosine = -1.0 / 39916800, 1.0 / 479001600
    for k in (9, 7, 5, 3, 1):
        sine = sine * s + (-1.0) ** (k // 2) / math.factorial(k)
    for k in (10, 8, 6, 4, 2, 0):
        cosine = cosine * s + (-1.0) ** (k // 2) / math.factorial(k)
    sn = sine * p
    small = n == 0.0
    return sn, cosine, jnp.where(small, sine, sn / jnp.where(small, 1.0, v))


def runs_of(window, depth):
    runs = []
    for slot in range(8):
        f, end = slot * depth, min((slot + 1) * depth, 3 * window)
        while f < end:
            c, z = divmod(f, window)
            length = min(end - f, window - z)
            runs.append((slot, f - slot * depth, length, c, z))
            f += length
    return runs


def reach_below(z0, cz):
    return jnp.where((z0 - 1 - cz // 2 + cz) % cz < REACH, REACH, REACH - 2)


def pack_kernel(
    n, sz, rep, window, depth,
    x_ref, pair_ref, mix_ref, bias_ref, outw_ref,
    out_ref, w1, w2,
    ext, first, second,
):
    parts = []
    for k in range(NB):
        part = pair_ref[pl.ds(k, 14, stride=NB), :]
        parts.append(jnp.concatenate([part, jnp.zeros((OP - 14, part.shape[1]), jnp.float32)], 0))
    pair = jnp.concatenate(parts, 0)
    w = jnp.dot(pair, mix_ref[...], precision=lax.Precision.HIGHEST, preferred_element_type=jnp.float32)
    row = lax.broadcasted_iota(jnp.int32, w.shape, 0)
    shift = bias_ref[...]
    rest = shift - split(shift)[0].astype(jnp.float32)
    rest = rest - split(rest)[0].astype(jnp.float32)
    hi, lo = split(jnp.where(row == 14, shift, jnp.where(row == 15, rest, w)).T)
    w1[...] = jnp.concatenate([jnp.concatenate([hi, hi], 1), jnp.concatenate([lo, lo], 1)], 0)
    degree = row // OP + 1
    hi, lo = split(w * degree.astype(jnp.float32) * outw_ref[...])
    w2[...] = jnp.concatenate([jnp.concatenate([hi, hi], 1), jnp.concatenate([lo, lo], 1)], 0)

    rows, cz = x_ref.shape
    field = rows // 3
    x = jnp.concatenate([x_ref[...], jnp.zeros((LANES - rows, cz), jnp.float32)], 0)
    cells = x.T
    ext[pl.ds(0, cz), :] = cells
    ext[pl.ds(cz, cz), :] = cells
    runs = runs_of(window, depth)
    lane = lax.broadcasted_iota(jnp.int32, (cz, LANES), 1) // field
    margin = 16
    for buf, chosen in ((first, [r for r in runs if r[1] == 0]), (second, [r for r in runs if r[1] > 0])):
        total = cells
        for slot, r, _, c, z in chosen:
            part = ext[pl.ds((z - r) % cz, cz), :]
            turn = (slot - c) * field % LANES
            total = jnp.where(lane == slot, pltpu.roll(part, turn, axis=1) if turn else part, total)
        buf[pl.ds(margin, cz), :] = total
        buf[pl.ds(0, margin), :] = total[cz - margin :]
        buf[pl.ds(margin + cz, margin), :] = total[:margin]

    late = [(slot, r) for slot, r, _, _, _ in runs if r > 0]
    row2 = lax.broadcasted_iota(jnp.int32, (2, LANES), 0)
    slot2 = lax.broadcasted_iota(jnp.int32, (2, LANES), 1) // field

    def send(d, carry):
        z0 = (d // rep) * sz
        start = z0 - reach_below(z0, cz) + margin
        for q in range(depth // 2):
            piece = first[pl.ds(start + 2 * q, 2), :]
            mask = None
            for slot, r in late:
                if r < 2 * q + 2:
                    m = (slot2 == slot) & (row2 + 2 * q >= r)
                    mask = m if mask is None else mask | m
            if mask is not None:
                piece = jnp.where(mask, second[pl.ds(start + 2 * q, 2), :], piece)
            out_ref[d, q] = piece
        return carry

    lax.fori_loop(0, n, send, 0, unroll=8)


def unpack_kernel(in_ref, spin_ref, field_ref):
    x = in_ref[...].T
    n = spin_ref.shape[0]
    spin_ref[...] = x[:n]
    field_ref[...] = x[n : 2 * n]


def sweep_kernel(
    gx, yz, bx, by, cz, sz, rep, window, depth,
    recv_ref, w1, w2,
    out_ref,
    spin, spin2, ver, cosv, grad, hidden, bricks,
):
    pp = Plane(gx, yz, bx, by)
    nt, cells = pp.nt, pp.cells
    rows = spin.shape[2]
    stride = 2 * rows + 1
    blk = LANES // cells

    lane16 = lax.broadcasted_iota(jnp.int32, (16, LANES), 1) // cells
    runs = runs_of(window, depth)

    def arrive(d, carry):
        for q in range(depth // 2):
            bricks[d, pl.ds(2 * q, 2), :] = recv_ref[d, q]
        return carry

    lax.fori_loop(0, gx * yz, arrive, 0, unroll=8)

    def gather(t, carry):
        moved = []
        for k in range(blk):
            v = bricks[t * blk + k]
            moved.append(pltpu.roll(v, k * cells, axis=1) if k else v)
        for j in range(16):
            u = moved[0]
            for k in range(1, blk):
                u = jnp.where(lane16 == (j + k) % blk, moved[k], u)
            if j:
                u = pltpu.roll(u, LANES - j * cells, axis=1)
            for slot, r, length, c, z in runs:
                if slot == j // 2:
                    spin[2 * c + j % 2, t, pl.ds(PAD + z, length), :] = u[r : r + length]
                    spin2[2 * c + j % 2, t, pl.ds(PAD + z, length), :] = u[r : r + length]
        return carry

    if nt <= 2:
        for t in range(nt):
            gather(t, 0)
    else:
        lax.fori_loop(0, nt, gather, 0)
    for t in range(nt):
        cosv[t, pl.ds(14 * stride, 2 * stride), :] = jnp.ones((2 * stride, LANES), jnp.float32)

    me = lax.axis_index("gx") * yz + lax.axis_index("yz")
    z0 = (me // rep) * sz
    hz = cz // 2
    below = reach_below(z0, cz)
    zs = (z0 - below + cz) % cz
    first = ((zs + hz - 1) // hz) * hz
    inside = first - zs < window
    border = PAD + first - zs
    hi_above = first % cz == hz
    own = PAD + below

    def is_hi(row):
        z = row - PAD + zs
        z = jnp.where(z >= cz, z - cz, z)
        return z >= hz

    low, high = own - 2, own + sz + 2
    ranges = []
    for _ in range(4):
        near_low = inside & hi_above & (border > low - 2) & (border < low + 2)
        near_high = inside & jnp.logical_not(hi_above) & (border > high - 2) & (border < high + 2)
        f_low = jnp.where(near_low, low - 2, low)
        f_high = jnp.where(near_high, high + 2, high)
        ranges.append((f_low, f_high))
        low, high = f_low - 2, f_high + 2
    ranges = ranges[::-1]

    def shifted_spins(start, count):
        def body(i, carry):
            r = start + 8 * i
            for dx, dy in ((1, 0), (-1, 0), (0, 1), (0, -1), (1, 1), (-1, -1)):
                for ca in range(6):
                    if (dx, dy) not in versions(ca % 2):
                        continue
                    n = versions(ca % 2).index((dx, dy))
                    got = pp.step([spin[ca, t, pl.ds(r, 8), :] for t in range(nt)], dx, dy)
                    for t in range(nt):
                        ver[n - 1, ca, t, pl.ds(r, 8), :] = got[t]
            return carry

        lax.fori_loop(0, count, body, 0)

    def neighbour(c, a, dx, dy, t, r):
        n = versions(a).index((dx, dy))
        if n == 0:
            return spin[2 * c + a, t, pl.ds(r, 8), :]
        return ver[n - 1, 2 * c + a, t, pl.ds(r, 8), :]

    def cosines(start, count):
        def body(i, carry):
            r = start + 8 * i
            for t in range(nt):
                for a in range(2):
                    mine = [spin[2 * c + a, t, pl.ds(r, 8), :] for c in range(3)]
                    for o, (b, dx, dy, dz) in enumerate(bonds(a)):
                        total = mine[0] * neighbour(0, b, dx, dy, t, r + dz)
                        for c in (1, 2):
                            total += mine[c] * neighbour(c, b, dx, dy, t, r + dz)
                        cosv[t, pl.ds(o * stride + a * rows + r, 8), :] = total
            return carry

        lax.fori_loop(0, count, body, 0)

    tc = 2 if nt % 2 == 0 else 1
    chunks = nt // tc

    def gradients(start, count):
        places = [(d, a, t) for d in range(1) for a in range(2) for t in range(tc)]

        def place(i):
            if chunks == 1:
                return start + 1 * i, 0
            return start + 1 * (i // chunks), (i % chunks) * tc

        def cosine(i):
            r, t0 = place(i)
            return jnp.concatenate(
                [cosv[t0 + t, pl.ds(a * rows + r + d, OP, stride=stride), :] for d, a, t in places], 1
            )

        def basis(i):
            c = cosine(i)
            c2 = c + c
            kinds = [c, c2 * c - 1.0]
            for _ in range(2, NB):
                kinds.append(c2 * kinds[-1] - kinds[-2])
            f_hi, f_lo = split(jnp.concatenate(kinds, 0))
            return jnp.concatenate([f_hi, f_lo], 0)

        def forward(rhs, slot):
            z = jnp.dot(w1[...], rhs, preferred_element_type=jnp.float32)
            hidden[slot] = z[:LANES] + z[LANES:]

        def activate(slot):
            u = jnp.tanh(hidden[slot])
            d_hi, d_lo = split(1.0 - u * u)
            return jnp.concatenate([d_hi, d_lo], 0)

        def backward(rhs):
            y = jnp.dot(w2[...], rhs, preferred_element_type=jnp.float32)
            return y[:LANES] + y[LANES:]

        def combine(i, y):
            r, t0 = place(i)
            c2 = 2.0 * cosine(i)
            b1 = y[(NB - 1) * OP :]
            b2 = None
            for k in range(NB - 2, -1, -1):
                new = y[k * OP : (k + 1) * OP] + c2 * b1
                if b2 is not None:
                    new = new - b2
                b1, b2 = new, b1
            for n, (d, a, t) in enumerate(places):
                grad[t0 + t, pl.ds(a * rows + r + d, OP, stride=stride), :] = b1[:, n * LANES : (n + 1) * LANES]

        for k in range(2):
            forward(basis(k), k)

        def one(i, slot):
            y = backward(activate(slot))
            forward(basis(i), slot)
            combine(i - 2, y)

        total = count * chunks
        done = 2
        for many in (4, 2):
            def body(i, first, many=many):
                for k in range(many):
                    one(first + i * many + k, k % 2)
                return first

            times = (total - done) // many
            lax.fori_loop(0, times, body, done)
            done = done + times * many
        for k in range(2):
            combine(total - 2 + k, backward(activate(k)))

    def field(r):
        out = []
        for a in range(2):
            total = [[None] * nt for _ in range(3)]
            for o, (b, dx, dy, dz) in enumerate(bonds(a)):
                m = mate_of(o)
                theirs = [grad[t, pl.ds(m * stride + b * rows + r + dz, 8), :] for t in range(nt)]
                theirs = pp.step(theirs, dx, dy)
                for t in range(nt):
                    coeff = grad[t, pl.ds(o * stride + a * rows + r, 8), :] + theirs[t]
                    for c in range(3):
                        term = coeff * neighbour(c, b, dx, dy, t, r + dz)
                        total[c][t] = term if total[c][t] is None else total[c][t] + term
            out.append([[-x for x in per] for per in total])
        return out

    def update(start, count, stage, only_border):
        def body(i, carry):
            r = start + 8 * i
            row = lax.broadcasted_iota(jnp.int32, (8, LANES), 0) + r
            from_border = jnp.where(hi_above, row - border, border - 1 - row)
            wanted = jnp.logical_not(only_border) | ((from_border >= 0) & (from_border < 2))
            h = field(r)
            for a in range(2):
                for t in range(nt):
                    xl, yl, _ = pp.at(t)
                    mask = (
                        ((xl >= bx // 2).astype(jnp.int32) == stage // 2)
                        & ((yl >= by // 2).astype(jnp.int32) == stage % 2)
                        & wanted
                    )
                    s = [spin[2 * c + a, t, pl.ds(r, 8), :] for c in range(3)]
                    w = [TIME_STEP * h[a][c][t] for c in range(3)]
                    square = 0.25 * (w[0] * w[0] + w[1] * w[1] + w[2] * w[2])
                    sn, cs, hs = half_turn(square)
                    cosr = 1.0 - 2.0 * sn * sn
                    sinc = hs * cs
                    proj = 0.5 * hs * hs * (w[0] * s[0] + w[1] * s[1] + w[2] * s[2])
                    for c in range(3):
                        p, q = (c + 1) % 3, (c + 2) % 3
                        cross = w[p] * s[q] - w[q] * s[p]
                        new = cosr * s[c] + sinc * cross + proj * w[c]
                        old = spin2[2 * c + a, t, pl.ds(r, 8), :]
                        spin2[2 * c + a, t, pl.ds(r, 8), :] = jnp.where(mask, new, old)
            return carry

        lax.fori_loop(0, count, body, 0)

    def take(everything):
        for i in range((window + 7) // 8):
            r = PAD + 8 * i
            row = lax.broadcasted_iota(jnp.int32, (8, LANES), 0) + r
            sel = everything | jnp.logical_not(is_hi(row))
            for ca in range(6):
                for t in range(nt):
                    place = (ca, t, pl.ds(r, 8), slice(None))
                    spin[place] = jnp.where(sel, spin2[place], spin[place])

    def phase(p, carry):
        stage, fix = p // 2, p % 2 == 1
        f_low, f_high = ranges[0]
        for s in range(1, 5):
            lo_s, hi_s = ranges[s] if s < 4 else (own, own + sz)
            f_low = jnp.where(stage == s, lo_s, f_low)
            f_high = jnp.where(stage == s, hi_s, f_high)
        n = f_high - f_low
        last = stage == 4
        crosses = inside & (f_low < border) & (border < f_high)

        @pl.when(jnp.logical_not(fix) | crosses)
        def _():
            shifted_spins(jnp.where(fix, border - 4, f_low - 2), jnp.where(fix, 1, (n + 11) // 8))
            cosines(jnp.where(fix, border - 4, f_low - 1), jnp.where(fix, 1, (n + 9) // 8))
            gradients(jnp.where(fix, border - 1, f_low - 1), jnp.where(fix, 2, (n + 3) // 2 * 2))

            @pl.when(jnp.logical_not(last))
            def _():
                update(
                    jnp.where(fix, border - 4, f_low), jnp.where(fix, 1, (n + 7) // 8), stage, fix
                )
                take(fix | jnp.logical_not(crosses))

        return carry

    lax.fori_loop(0, 9, phase, 0)

    final = field(own)
    lane16s = lax.broadcasted_iota(jnp.int32, (8, LANES), 1) // cells
    for t in range(nt):
        moved = []
        for j in range(12):
            ca = j % 6
            v = spin[ca, t, pl.ds(own, 8), :] if j < 6 else final[ca % 2][ca // 2][t]
            moved.append(pltpu.roll(v, j * cells, axis=1) if j else v)
        for k in range(blk):
            u = moved[0]
            for j in range(1, 12):
                u = jnp.where(lane16s == (j + k) % blk, moved[j], u)
            if k:
                u = pltpu.roll(u, LANES - k * cells, axis=1)
            out_ref[t * blk + k] = u[:sz]


def per_device(gx, yz, spin_vectors, pair_weight, mix_weight, mix_bias, out_weight):
    three, two, bx, by, cz = spin_vectors.shape
    n = gx * yz
    sz = max(1, cz // n)
    rep = n * sz // cz
    window = sz + 2 * REACH - 2
    depth = -(-3 * window // 16) * 2
    rows = -(-window // 8) * 8 + 2 * PAD
    nt = n * bx * by // LANES
    brick = three * two * bx * by
    vmem = pl.BlockSpec(memory_space=pltpu.VMEM)

    f32, bf16 = jnp.float32, jnp.bfloat16
    packed, w1, w2 = pl.pallas_call(
        functools.partial(pack_kernel, n, sz, rep, window, depth),
        out_shape=[
            jax.ShapeDtypeStruct((n, depth // 2, 2, LANES), f32),
            jax.ShapeDtypeStruct((2 * LANES, 2 * LANES), bf16),
            jax.ShapeDtypeStruct((2 * LANES, 2 * LANES), bf16),
        ],
        in_specs=[vmem] * 5,
        out_specs=[vmem] * 3,
        scratch_shapes=[
            pltpu.VMEM((2 * cz, LANES), f32),
            pltpu.VMEM((cz + 32, LANES), f32),
            pltpu.VMEM((cz + 32, LANES), f32),
        ],
        name="pack",
    )(spin_vectors.reshape(brick, cz), pair_weight, mix_weight, mix_bias[None], out_weight[None])
    received = lax.all_to_all(packed, ("gx", "yz"), 0, 0, tiled=True)

    result = pl.pallas_call(
        functools.partial(sweep_kernel, gx, yz, bx, by, cz, sz, rep, window, depth),
        out_shape=jax.ShapeDtypeStruct((n, sz, LANES), f32),
        in_specs=[vmem] * 3,
        out_specs=vmem,
        scratch_shapes=[
            pltpu.VMEM((6, nt, rows, LANES), f32),
            pltpu.VMEM((6, nt, rows, LANES), f32),
            pltpu.VMEM((5, 6, nt, rows, LANES), f32),
            pltpu.VMEM((nt, OP * (2 * rows + 1) + 7, LANES), f32),
            pltpu.VMEM((nt, OP * (2 * rows + 1) + 7, LANES), f32),
            pltpu.VMEM((2, LANES, 2 * (2 - nt % 2) * LANES), f32),
            pltpu.VMEM((n, 16, LANES), f32),
        ],
        compiler_params=pltpu.CompilerParams(vmem_limit_bytes=min(56, 8 + 4 * nt) * 2**20),
        name="sweep",
    )(received, w1, w2)
    returned = lax.all_to_all(result, ("gx", "yz"), 0, 0, tiled=True)
    if rep > 1:
        returned = returned[::rep]

    outs = pl.pallas_call(
        unpack_kernel,
        out_shape=[jax.ShapeDtypeStruct((brick, cz), f32)] * 2,
        in_specs=[vmem],
        out_specs=[vmem] * 2,
        name="unpack",
    )(returned.reshape(cz, LANES))
    return tuple(x.reshape(three, two, bx, by, cz) for x in outs)


def solution(mesh):
    gx, yz = mesh.shape["gx"], mesh.shape["yz"]
    spec = P(None, None, "gx", "yz", None)
    return jax.shard_map(
        functools.partial(per_device, gx, yz),
        mesh=mesh,
        in_specs=(spec, P(), P(), P(), P()),
        out_specs=(spec, spec),
        check_vma=False,
    )
```

```python
import functools
import math

import jax
import jax.numpy as jnp
from jax import lax
from jax.experimental import pallas as pl
from jax.experimental.pallas import tpu as pltpu
from jax.sharding import PartitionSpec as P

NB = 8
TIME_STEP = 0.1
PAD = 8
OP = 16
LANES = 128
REACH = 12

FIRST = [(x, y, z) for x in (-1, 0) for y in (-1, 0) for z in (-1, 0)]
SECOND = [(1, 0, 0), (-1, 0, 0), (0, 1, 0), (0, -1, 0), (0, 0, 1), (0, 0, -1)]


def bonds(a):
    sign = 1 if a == 0 else -1
    first = [(1 - a, sign * x, sign * y, sign * z) for x, y, z in FIRST]
    return first + [(a, *e) for e in SECOND]


def mate_of(o):
    return o if o < 8 else 8 + ((o - 8) ^ 1)


def versions(a):
    s = 1 if a == 0 else -1
    return [(0, 0), (s, 0), (0, s), (s, s), (-s, 0), (0, -s)]


class Plane:
    def __init__(self, gx, yz, bx, by, rows=8):
        self.bx, self.by, self.yz, self.cells = bx, by, yz, bx * by
        self.nl = gx * yz * bx * by
        self.nt = self.nl // LANES
        self.lane = lax.broadcasted_iota(jnp.int32, (rows, LANES), 1)
        ring = yz * self.cells
        self.within = LANES % ring == 0
        if self.within:
            xl, yl, brick = self.at(0)
            x_at = {0: self.lane, 1: jnp.where(xl == bx - 1, self.lane + ring - (bx - 1) * by, self.lane + by),
                    -1: jnp.where(xl == 0, self.lane - ring + (bx - 1) * by, self.lane - by)}
            hop = self.cells - (by - 1)
            y_at = {0: 0, 1: jnp.where(yl < by - 1, 1, jnp.where(brick < yz - 1, hop, hop - ring)),
                    -1: jnp.where(yl > 0, -1, jnp.where(brick > 0, -hop, ring - hop))}
            self.source = {
                (dx, dy): (x_at[dx] + y_at[dy] + LANES) % LANES for dx in (-1, 0, 1) for dy in (-1, 0, 1)
            }
            self.from_next = {1: (self.lane < ring) & (xl == 0), -1: (self.lane >= LANES - ring) & (xl == bx - 1)}

    def at(self, t):
        lane = self.lane + t * LANES
        return (lane // self.by) % self.bx, lane % self.by, (lane // self.cells) % self.yz

    def roll(self, v, s):
        s = s % self.nl
        q, r = divmod(s, LANES)
        nt = self.nt
        if r == 0:
            return [v[(t + q) % nt] for t in range(nt)]
        rot = [pltpu.roll(x, LANES - r, axis=1) for x in v]
        if nt == 1:
            return rot
        keep = self.lane < LANES - r
        return [jnp.where(keep, rot[(t + q) % nt], rot[(t + q + 1) % nt]) for t in range(nt)]

    def step_x(self, v, d):
        if d == 0:
            return v
        ring = self.cells * self.yz
        inner = self.roll(v, d * self.by)
        outer = self.roll(v, d * (ring - (self.bx - 1) * self.by))
        edge = self.bx - 1 if d > 0 else 0
        return [jnp.where(self.at(t)[0] == edge, outer[t], inner[t]) for t in range(self.nt)]

    def step_y(self, v, d):
        if d == 0:
            return v
        ring = self.cells * self.yz
        hop = d * (self.cells - (self.by - 1))
        inner = self.roll(v, d)
        outer = self.roll(v, hop)
        wrap = self.roll(v, hop - d * ring)
        edge = self.by - 1 if d > 0 else 0
        last = self.yz - 1 if d > 0 else 0
        out = []
        for t in range(self.nt):
            _, yl, brick = self.at(t)
            far = jnp.where(brick == last, wrap[t], outer[t])
            out.append(jnp.where(yl == edge, far, inner[t]))
        return out

    def step(self, v, dx, dy):
        if not (dx or dy):
            return v
        if self.within:
            if dx and self.nt > 1:
                swap = self.from_next[dx]
                v = [jnp.where(swap, v[(t + dx) % self.nt], v[t]) for t in range(self.nt)]
            where = self.source[(dx, dy)]
            return [jnp.take_along_axis(x, where, axis=1, mode="promise_in_bounds") for x in v]
        return self.step_x(self.step_y(v, dy), dx)


def split(x):
    hi = x.astype(jnp.bfloat16)
    return hi, (x - hi.astype(jnp.float32)).astype(jnp.bfloat16)


def half_turn(square):
    v = jnp.sqrt(square)
    n = jnp.round(v * (1.0 / math.pi))
    p = ((v - n * 3.140625) - n * 9.67502593994140625e-4) - n * 1.5099579909783764e-7
    s = p * p
    sine, cosine = -1.0 / 39916800, 1.0 / 479001600
    for k in (9, 7, 5, 3, 1):
        sine = sine * s + (-1.0) ** (k // 2) / math.factorial(k)
    for k in (10, 8, 6, 4, 2, 0):
        cosine = cosine * s + (-1.0) ** (k // 2) / math.factorial(k)
    sn = sine * p
    small = n == 0.0
    return sn, cosine, jnp.where(small, sine, sn / jnp.where(small, 1.0, v))


def runs_of(window, depth):
    runs = []
    for slot in range(8):
        f, end = slot * depth, min((slot + 1) * depth, 3 * window)
        while f < end:
            c, z = divmod(f, window)
            length = min(end - f, window - z)
            runs.append((slot, f - slot * depth, length, c, z))
            f += length
    return runs


def reach_below(z0, cz):
    return jnp.where((z0 - 1 - cz // 2 + cz) % cz < REACH, REACH, REACH - 2)


def pack_kernel(
    n, sz, rep, window, depth,
    x_ref, pair_ref, mix_ref, bias_ref, outw_ref,
    out_ref, w1, w2,
    ext, first, second,
):
    parts = []
    for k in range(NB):
        part = pair_ref[pl.ds(k, 14, stride=NB), :]
        parts.append(jnp.concatenate([part, jnp.zeros((OP - 14, part.shape[1]), jnp.float32)], 0))
    pair = jnp.concatenate(parts, 0)
    w = jnp.dot(pair, mix_ref[...], precision=lax.Precision.HIGHEST, preferred_element_type=jnp.float32)
    row = lax.broadcasted_iota(jnp.int32, w.shape, 0)
    shift = bias_ref[...]
    rest = shift - split(shift)[0].astype(jnp.float32)
    rest = rest - split(rest)[0].astype(jnp.float32)
    hi, lo = split(jnp.where(row == 14, shift, jnp.where(row == 15, rest, w)).T)
    w1[...] = jnp.concatenate([jnp.concatenate([hi, hi], 1), jnp.concatenate([lo, lo], 1)], 0)
    degree = row // OP + 1
    hi, lo = split(w * degree.astype(jnp.float32) * outw_ref[...])
    w2[...] = jnp.concatenate([jnp.concatenate([hi, hi], 1), jnp.concatenate([lo, lo], 1)], 0)

    rows, cz = x_ref.shape
    field = rows // 3
    x = jnp.concatenate([x_ref[...], jnp.zeros((LANES - rows, cz), jnp.float32)], 0)
    cells = x.T
    ext[pl.ds(0, cz), :] = cells
    ext[pl.ds(cz, cz), :] = cells
    runs = runs_of(window, depth)
    lane = lax.broadcasted_iota(jnp.int32, (cz, LANES), 1) // field
    margin = 16
    for buf, chosen in ((first, [r for r in runs if r[1] == 0]), (second, [r for r in runs if r[1] > 0])):
        total = cells
        for slot, r, _, c, z in chosen:
            part = ext[pl.ds((z - r) % cz, cz), :]
            turn = (slot - c) * field % LANES
            total = jnp.where(lane == slot, pltpu.roll(part, turn, axis=1) if turn else part, total)
        buf[pl.ds(margin, cz), :] = total
        buf[pl.ds(0, margin), :] = total[cz - margin :]
        buf[pl.ds(margin + cz, margin), :] = total[:margin]

    late = [(slot, r) for slot, r, _, _, _ in runs if r > 0]
    row2 = lax.broadcasted_iota(jnp.int32, (2, LANES), 0)
    slot2 = lax.broadcasted_iota(jnp.int32, (2, LANES), 1) // field

    def send(d, carry):
        z0 = (d // rep) * sz
        start = z0 - reach_below(z0, cz) + margin
        for q in range(depth // 2):
            piece = first[pl.ds(start + 2 * q, 2), :]
            mask = None
            for slot, r in late:
                if r < 2 * q + 2:
                    m = (slot2 == slot) & (row2 + 2 * q >= r)
                    mask = m if mask is None else mask | m
            if mask is not None:
                piece = jnp.where(mask, second[pl.ds(start + 2 * q, 2), :], piece)
            out_ref[d, q] = piece
        return carry

    lax.fori_loop(0, n, send, 0, unroll=8)


def unpack_kernel(in_ref, spin_ref, field_ref):
    x = in_ref[...].T
    n = spin_ref.shape[0]
    spin_ref[...] = x[:n]
    field_ref[...] = x[n : 2 * n]


def sweep_kernel(
    gx, yz, bx, by, cz, sz, rep, window, depth,
    recv_ref, w1, w2,
    out_ref,
    spin, spin2, ver, cosv, grad, hidden, bricks,
):
    pp = Plane(gx, yz, bx, by)
    nt, cells = pp.nt, pp.cells
    rows = spin.shape[2]
    stride = 2 * rows + 1
    blk = LANES // cells

    lane16 = lax.broadcasted_iota(jnp.int32, (16, LANES), 1) // cells
    runs = runs_of(window, depth)

    def arrive(d, carry):
        for q in range(depth // 2):
            bricks[d, pl.ds(2 * q, 2), :] = recv_ref[d, q]
        return carry

    lax.fori_loop(0, gx * yz, arrive, 0, unroll=8)

    def gather(t, carry):
        moved = []
        for k in range(blk):
            v = bricks[t * blk + k]
            moved.append(pltpu.roll(v, k * cells, axis=1) if k else v)
        for j in range(16):
            u = moved[0]
            for k in range(1, blk):
                u = jnp.where(lane16 == (j + k) % blk, moved[k], u)
            if j:
                u = pltpu.roll(u, LANES - j * cells, axis=1)
            for slot, r, length, c, z in runs:
                if slot == j // 2:
                    spin[2 * c + j % 2, t, pl.ds(PAD + z, length), :] = u[r : r + length]
                    spin2[2 * c + j % 2, t, pl.ds(PAD + z, length), :] = u[r : r + length]
        return carry

    if nt <= 2:
        for t in range(nt):
            gather(t, 0)
    else:
        lax.fori_loop(0, nt, gather, 0)
    for t in range(nt):
        cosv[t, pl.ds(14 * stride, 2 * stride), :] = jnp.ones((2 * stride, LANES), jnp.float32)

    me = lax.axis_index("gx") * yz + lax.axis_index("yz")
    z0 = (me // rep) * sz
    hz = cz // 2
    below = reach_below(z0, cz)
    zs = (z0 - below + cz) % cz
    first = ((zs + hz - 1) // hz) * hz
    inside = first - zs < window
    border = PAD + first - zs
    hi_above = first % cz == hz
    own = PAD + below

    def is_hi(row):
        z = row - PAD + zs
        z = jnp.where(z >= cz, z - cz, z)
        return z >= hz

    low, high = own - 2, own + sz + 2
    ranges = []
    for _ in range(4):
        near_low = inside & hi_above & (border > low - 2) & (border < low + 2)
        near_high = inside & jnp.logical_not(hi_above) & (border > high - 2) & (border < high + 2)
        f_low = jnp.where(near_low, low - 2, low)
        f_high = jnp.where(near_high, high + 2, high)
        ranges.append((f_low, f_high))
        low, high = f_low - 2, f_high + 2
    ranges = ranges[::-1]

    def by_twos(count, body):
        if isinstance(count, int):
            for i in range(count):
                body(i, 0)
            return

        def two(i, carry):
            body(2 * i, carry)
            return body(2 * i + 1, carry)

        lax.fori_loop(0, count // 2, two, 0)

        @pl.when(count % 2 == 1)
        def _():
            body(count - 1, 0)

    def shifted_spins(start, count):
        def body(i, carry):
            r = start + 8 * i
            for dx, dy in ((1, 0), (-1, 0), (0, 1), (0, -1), (1, 1), (-1, -1)):
                for ca in range(6):
                    if (dx, dy) not in versions(ca % 2):
                        continue
                    n = versions(ca % 2).index((dx, dy))
                    got = pp.step([spin[ca, t, pl.ds(r, 8), :] for t in range(nt)], dx, dy)
                    for t in range(nt):
                        ver[n - 1, ca, t, pl.ds(r, 8), :] = got[t]
            return carry

        by_twos(count, body)

    def neighbour(c, a, dx, dy, t, r):
        n = versions(a).index((dx, dy))
        if n == 0:
            return spin[2 * c + a, t, pl.ds(r, 8), :]
        return ver[n - 1, 2 * c + a, t, pl.ds(r, 8), :]

    def cosines(start, count):
        def body(i, carry):
            r = start + 8 * i
            for t in range(nt):
                for a in range(2):
                    mine = [spin[2 * c + a, t, pl.ds(r, 8), :] for c in range(3)]
                    for o, (b, dx, dy, dz) in enumerate(bonds(a)):
                        total = mine[0] * neighbour(0, b, dx, dy, t, r + dz)
                        for c in (1, 2):
                            total += mine[c] * neighbour(c, b, dx, dy, t, r + dz)
                        cosv[t, pl.ds(o * stride + a * rows + r, 8), :] = total
            return carry

        by_twos(count, body)

    tc = 2 if nt % 2 == 0 else 1
    chunks = nt // tc

    def gradients(start, count):
        places = [(d, a, t) for d in range(1) for a in range(2) for t in range(tc)]

        def place(i):
            if chunks == 1:
                return start + 1 * i, 0
            return start + 1 * (i // chunks), (i % chunks) * tc

        def cosine(i):
            r, t0 = place(i)
            return jnp.concatenate(
                [cosv[t0 + t, pl.ds(a * rows + r + d, OP, stride=stride), :] for d, a, t in places], 1
            )

        def basis(i):
            c = cosine(i)
            c2 = c + c
            kinds = [c, c2 * c - 1.0]
            for _ in range(2, NB):
                kinds.append(c2 * kinds[-1] - kinds[-2])
            f_hi, f_lo = split(jnp.concatenate(kinds, 0))
            return jnp.concatenate([f_hi, f_lo], 0)

        def forward(rhs, slot):
            z = jnp.dot(w1[...], rhs, preferred_element_type=jnp.float32)
            hidden[slot] = z[:LANES] + z[LANES:]

        def activate(slot):
            u = jnp.tanh(hidden[slot])
            d_hi, d_lo = split(1.0 - u * u)
            return jnp.concatenate([d_hi, d_lo], 0)

        def backward(rhs):
            y = jnp.dot(w2[...], rhs, preferred_element_type=jnp.float32)
            return y[:LANES] + y[LANES:]

        def combine(i, y):
            r, t0 = place(i)
            c2 = 2.0 * cosine(i)
            b1 = y[(NB - 1) * OP :]
            b2 = None
            for k in range(NB - 2, -1, -1):
                new = y[k * OP : (k + 1) * OP] + c2 * b1
                if b2 is not None:
                    new = new - b2
                b1, b2 = new, b1
            for n, (d, a, t) in enumerate(places):
                grad[t0 + t, pl.ds(a * rows + r + d, OP, stride=stride), :] = b1[:, n * LANES : (n + 1) * LANES]

        for k in range(2):
            forward(basis(k), k)

        def one(i, slot):
            y = backward(activate(slot))
            forward(basis(i), slot)
            combine(i - 2, y)

        total = count * chunks
        done = 2
        if isinstance(total, int) and total <= 8:
            for i in range(done, total):
                one(i, i % 2)
        else:
            for many in (16, 8, 4, 2):
                def body(i, first, many=many):
                    for k in range(many):
                        one(first + i * many + k, k % 2)
                    return first

                times = (total - done) // many
                lax.fori_loop(0, times, body, done)
                done = done + times * many
        for k in range(2):
            combine(total - 2 + k, backward(activate(k)))

    def field(r):
        out = []
        for a in range(2):
            total = [[None] * nt for _ in range(3)]
            for o, (b, dx, dy, dz) in enumerate(bonds(a)):
                m = mate_of(o)
                theirs = [grad[t, pl.ds(m * stride + b * rows + r + dz, 8), :] for t in range(nt)]
                theirs = pp.step(theirs, dx, dy)
                for t in range(nt):
                    coeff = grad[t, pl.ds(o * stride + a * rows + r, 8), :] + theirs[t]
                    for c in range(3):
                        term = coeff * neighbour(c, b, dx, dy, t, r + dz)
                        total[c][t] = term if total[c][t] is None else total[c][t] + term
            out.append([[-x for x in per] for per in total])
        return out

    def update(start, count, stage, only_border):
        def body(i, carry):
            r = start + 8 * i
            row = lax.broadcasted_iota(jnp.int32, (8, LANES), 0) + r
            if only_border:
                from_border = jnp.where(hi_above, row - border, border - 1 - row)
                wanted = (from_border >= 0) & (from_border < 2)
            else:
                wanted = True
            h = field(r)
            for a in range(2):
                for t in range(nt):
                    xl, yl, _ = pp.at(t)
                    mask = (
                        ((xl >= bx // 2).astype(jnp.int32) == stage // 2)
                        & ((yl >= by // 2).astype(jnp.int32) == stage % 2)
                        & wanted
                    )
                    s = [spin[2 * c + a, t, pl.ds(r, 8), :] for c in range(3)]
                    w = [TIME_STEP * h[a][c][t] for c in range(3)]
                    square = 0.25 * (w[0] * w[0] + w[1] * w[1] + w[2] * w[2])
                    sn, cs, hs = half_turn(square)
                    cosr = 1.0 - 2.0 * sn * sn
                    sinc = hs * cs
                    proj = 0.5 * hs * hs * (w[0] * s[0] + w[1] * s[1] + w[2] * s[2])
                    for c in range(3):
                        p, q = (c + 1) % 3, (c + 2) % 3
                        cross = w[p] * s[q] - w[q] * s[p]
                        new = cosr * s[c] + sinc * cross + proj * w[c]
                        old = spin2[2 * c + a, t, pl.ds(r, 8), :]
                        spin2[2 * c + a, t, pl.ds(r, 8), :] = jnp.where(mask, new, old)
            return carry

        by_twos(count, body)

    def take(everything):
        for i in range((window + 7) // 8):
            r = PAD + 8 * i
            row = lax.broadcasted_iota(jnp.int32, (8, LANES), 0) + r
            sel = True if everything is True else everything | jnp.logical_not(is_hi(row))
            for ca in range(6):
                for t in range(nt):
                    place = (ca, t, pl.ds(r, 8), slice(None))
                    spin[place] = spin2[place] if sel is True else jnp.where(sel, spin2[place], spin[place])

    def stage_pair(stage, carry):
        f_low, f_high = ranges[0]
        for s in range(1, 4):
            f_low = jnp.where(stage == s, ranges[s][0], f_low)
            f_high = jnp.where(stage == s, ranges[s][1], f_high)
        n = f_high - f_low
        crosses = inside & (f_low < border) & (border < f_high)
        shifted_spins(f_low - 2, (n + 11) // 8)
        cosines(f_low - 1, (n + 9) // 8)
        gradients(f_low - 1, (n + 3) // 2 * 2)
        update(f_low, (n + 7) // 8, stage, False)
        take(jnp.logical_not(crosses))

        @pl.when(crosses)
        def _():
            shifted_spins(border - 4, 1)
            cosines(border - 4, 1)
            gradients(border - 1, 2)
            update(border - 4, 1, stage, True)
            take(True)

        return carry

    lax.fori_loop(0, 4, stage_pair, 0)
    shifted_spins(own - 2, (sz + 11) // 8)
    cosines(own - 1, (sz + 9) // 8)
    gradients(own - 1, (sz + 3) // 2 * 2)

    final = field(own)
    lane16s = lax.broadcasted_iota(jnp.int32, (8, LANES), 1) // cells
    for t in range(nt):
        moved = []
        for j in range(12):
            ca = j % 6
            v = spin[ca, t, pl.ds(own, 8), :] if j < 6 else final[ca % 2][ca // 2][t]
            moved.append(pltpu.roll(v, j * cells, axis=1) if j else v)
        for k in range(blk):
            u = moved[0]
            for j in range(1, 12):
                u = jnp.where(lane16s == (j + k) % blk, moved[j], u)
            if k:
                u = pltpu.roll(u, LANES - k * cells, axis=1)
            out_ref[t * blk + k] = u[:sz]


def per_device(gx, yz, spin_vectors, pair_weight, mix_weight, mix_bias, out_weight):
    three, two, bx, by, cz = spin_vectors.shape
    n = gx * yz
    sz = max(1, cz // n)
    rep = n * sz // cz
    window = sz + 2 * REACH - 2
    depth = -(-3 * window // 16) * 2
    rows = -(-window // 8) * 8 + 2 * PAD
    nt = n * bx * by // LANES
    brick = three * two * bx * by
    vmem = pl.BlockSpec(memory_space=pltpu.VMEM)

    f32, bf16 = jnp.float32, jnp.bfloat16
    packed, w1, w2 = pl.pallas_call(
        functools.partial(pack_kernel, n, sz, rep, window, depth),
        out_shape=[
            jax.ShapeDtypeStruct((n, depth // 2, 2, LANES), f32),
            jax.ShapeDtypeStruct((2 * LANES, 2 * LANES), bf16),
            jax.ShapeDtypeStruct((2 * LANES, 2 * LANES), bf16),
        ],
        in_specs=[vmem] * 5,
        out_specs=[vmem] * 3,
        scratch_shapes=[
            pltpu.VMEM((2 * cz, LANES), f32),
            pltpu.VMEM((cz + 32, LANES), f32),
            pltpu.VMEM((cz + 32, LANES), f32),
        ],
        name="pack",
    )(spin_vectors.reshape(brick, cz), pair_weight, mix_weight, mix_bias[None], out_weight[None])
    received = lax.all_to_all(packed, ("gx", "yz"), 0, 0, tiled=True)

    result = pl.pallas_call(
        functools.partial(sweep_kernel, gx, yz, bx, by, cz, sz, rep, window, depth),
        out_shape=jax.ShapeDtypeStruct((n, sz, LANES), f32),
        in_specs=[vmem] * 3,
        out_specs=vmem,
        scratch_shapes=[
            pltpu.VMEM((6, nt, rows, LANES), f32),
            pltpu.VMEM((6, nt, rows, LANES), f32),
            pltpu.VMEM((5, 6, nt, rows, LANES), f32),
            pltpu.VMEM((nt, OP * (2 * rows + 1) + 7, LANES), f32),
            pltpu.VMEM((nt, OP * (2 * rows + 1) + 7, LANES), f32),
            pltpu.VMEM((2, LANES, 2 * (2 - nt % 2) * LANES), f32),
            pltpu.VMEM((n, 16, LANES), f32),
        ],
        compiler_params=pltpu.CompilerParams(vmem_limit_bytes=min(56, 8 + 4 * nt) * 2**20),
        name="sweep",
    )(received, w1, w2)
    returned = lax.all_to_all(result, ("gx", "yz"), 0, 0, tiled=True)
    if rep > 1:
        returned = returned[::rep]

    outs = pl.pallas_call(
        unpack_kernel,
        out_shape=[jax.ShapeDtypeStruct((brick, cz), f32)] * 2,
        in_specs=[vmem],
        out_specs=[vmem] * 2,
        name="unpack",
    )(returned.reshape(cz, LANES))
    return tuple(x.reshape(three, two, bx, by, cz) for x in outs)


def solution(mesh):
    gx, yz = mesh.shape["gx"], mesh.shape["yz"]
    spec = P(None, None, "gx", "yz", None)
    return jax.shard_map(
        functools.partial(per_device, gx, yz),
        mesh=mesh,
        in_specs=(spec, P(), P(), P(), P()),
        out_specs=(spec, spec),
        check_vma=False,
    )
```

```python
import functools
import math

import jax
import jax.numpy as jnp
from jax import lax
from jax.experimental import pallas as pl
from jax.experimental.pallas import tpu as pltpu
from jax.sharding import PartitionSpec as P

NB = 8
TIME_STEP = 0.1
PAD = 8
OP = 16
LANES = 128
REACH = 12

FIRST = [(x, y, z) for x in (-1, 0) for y in (-1, 0) for z in (-1, 0)]
SECOND = [(1, 0, 0), (-1, 0, 0), (0, 1, 0), (0, -1, 0), (0, 0, 1), (0, 0, -1)]


def bonds(a):
    sign = 1 if a == 0 else -1
    first = [(1 - a, sign * x, sign * y, sign * z) for x, y, z in FIRST]
    return first + [(a, *e) for e in SECOND]


def mate_of(o):
    return o if o < 8 else 8 + ((o - 8) ^ 1)


def versions(a):
    s = 1 if a == 0 else -1
    return [(0, 0), (s, 0), (0, s), (s, s), (-s, 0), (0, -s)]


class Plane:
    def __init__(self, gx, yz, bx, by, rows=8):
        self.bx, self.by, self.yz, self.cells = bx, by, yz, bx * by
        self.nl = gx * yz * bx * by
        self.nt = self.nl // LANES
        self.lane = lax.broadcasted_iota(jnp.int32, (rows, LANES), 1)
        ring = yz * self.cells
        self.within = LANES % ring == 0
        if self.within:
            xl, yl, brick = self.at(0)
            x_at = {0: self.lane, 1: jnp.where(xl == bx - 1, self.lane + ring - (bx - 1) * by, self.lane + by),
                    -1: jnp.where(xl == 0, self.lane - ring + (bx - 1) * by, self.lane - by)}
            hop = self.cells - (by - 1)
            y_at = {0: 0, 1: jnp.where(yl < by - 1, 1, jnp.where(brick < yz - 1, hop, hop - ring)),
                    -1: jnp.where(yl > 0, -1, jnp.where(brick > 0, -hop, ring - hop))}
            self.source = {
                (dx, dy): (x_at[dx] + y_at[dy] + LANES) % LANES for dx in (-1, 0, 1) for dy in (-1, 0, 1)
            }
            self.from_next = {1: (self.lane < ring) & (xl == 0), -1: (self.lane >= LANES - ring) & (xl == bx - 1)}

    def at(self, t):
        lane = self.lane + t * LANES
        return (lane // self.by) % self.bx, lane % self.by, (lane // self.cells) % self.yz

    def roll(self, v, s):
        s = s % self.nl
        q, r = divmod(s, LANES)
        nt = self.nt
        if r == 0:
            return [v[(t + q) % nt] for t in range(nt)]
        rot = [pltpu.roll(x, LANES - r, axis=1) for x in v]
        if nt == 1:
            return rot
        keep = self.lane < LANES - r
        return [jnp.where(keep, rot[(t + q) % nt], rot[(t + q + 1) % nt]) for t in range(nt)]

    def step_x(self, v, d):
        if d == 0:
            return v
        ring = self.cells * self.yz
        inner = self.roll(v, d * self.by)
        outer = self.roll(v, d * (ring - (self.bx - 1) * self.by))
        edge = self.bx - 1 if d > 0 else 0
        return [jnp.where(self.at(t)[0] == edge, outer[t], inner[t]) for t in range(self.nt)]

    def step_y(self, v, d):
        if d == 0:
            return v
        ring = self.cells * self.yz
        hop = d * (self.cells - (self.by - 1))
        inner = self.roll(v, d)
        outer = self.roll(v, hop)
        wrap = self.roll(v, hop - d * ring)
        edge = self.by - 1 if d > 0 else 0
        last = self.yz - 1 if d > 0 else 0
        out = []
        for t in range(self.nt):
            _, yl, brick = self.at(t)
            far = jnp.where(brick == last, wrap[t], outer[t])
            out.append(jnp.where(yl == edge, far, inner[t]))
        return out

    def step(self, v, dx, dy):
        if not (dx or dy):
            return v
        if self.within:
            if dx and self.nt > 1:
                swap = self.from_next[dx]
                v = [jnp.where(swap, v[(t + dx) % self.nt], v[t]) for t in range(self.nt)]
            where = self.source[(dx, dy)]
            return [jnp.take_along_axis(x, where, axis=1, mode="promise_in_bounds") for x in v]
        return self.step_x(self.step_y(v, dy), dx)


def split(x):
    hi = x.astype(jnp.bfloat16)
    return hi, (x - hi.astype(jnp.float32)).astype(jnp.bfloat16)


def half_turn(square):
    v = jnp.sqrt(square)
    n = jnp.round(v * (1.0 / math.pi))
    p = ((v - n * 3.140625) - n * 9.67502593994140625e-4) - n * 1.5099579909783764e-7
    s = p * p
    sine, cosine = -1.0 / 39916800, 1.0 / 479001600
    for k in (9, 7, 5, 3, 1):
        sine = sine * s + (-1.0) ** (k // 2) / math.factorial(k)
    for k in (10, 8, 6, 4, 2, 0):
        cosine = cosine * s + (-1.0) ** (k // 2) / math.factorial(k)
    sn = sine * p
    small = n == 0.0
    return sn, cosine, jnp.where(small, sine, sn / jnp.where(small, 1.0, v))


def runs_of(window, depth):
    runs = []
    for slot in range(8):
        f, end = slot * depth, min((slot + 1) * depth, 3 * window)
        while f < end:
            c, z = divmod(f, window)
            length = min(end - f, window - z)
            runs.append((slot, f - slot * depth, length, c, z))
            f += length
    return runs


def reach_below(z0, cz):
    return jnp.where((z0 - 1 - cz // 2 + cz) % cz < REACH, REACH, REACH - 2)


def pack_kernel(
    n, sz, rep, window, depth,
    x_ref, pair_ref, mix_ref, bias_ref, outw_ref,
    out_ref, w1, w2,
    ext, first, second,
):
    parts = []
    for k in range(NB):
        part = pair_ref[pl.ds(k, 14, stride=NB), :]
        parts.append(jnp.concatenate([part, jnp.zeros((OP - 14, part.shape[1]), jnp.float32)], 0))
    pair = jnp.concatenate(parts, 0)
    w = jnp.dot(pair, mix_ref[...], precision=lax.Precision.HIGHEST, preferred_element_type=jnp.float32)
    row = lax.broadcasted_iota(jnp.int32, w.shape, 0)
    shift = bias_ref[...]
    rest = shift - split(shift)[0].astype(jnp.float32)
    rest = rest - split(rest)[0].astype(jnp.float32)
    hi, lo = split(jnp.where(row == 14, shift, jnp.where(row == 15, rest, w)).T)
    w1[...] = jnp.concatenate([jnp.concatenate([hi, hi], 1), jnp.concatenate([lo, lo], 1)], 0)
    degree = row // OP + 1
    hi, lo = split(w * degree.astype(jnp.float32) * outw_ref[...])
    w2[...] = jnp.concatenate([jnp.concatenate([hi, hi], 1), jnp.concatenate([lo, lo], 1)], 0)

    rows, cz = x_ref.shape
    field = rows // 3
    x = jnp.concatenate([x_ref[...], jnp.zeros((LANES - rows, cz), jnp.float32)], 0)
    cells = x.T
    ext[pl.ds(0, cz), :] = cells
    ext[pl.ds(cz, cz), :] = cells
    runs = runs_of(window, depth)
    lane = lax.broadcasted_iota(jnp.int32, (cz, LANES), 1) // field
    margin = 16
    for buf, chosen in ((first, [r for r in runs if r[1] == 0]), (second, [r for r in runs if r[1] > 0])):
        total = cells
        for slot, r, _, c, z in chosen:
            part = ext[pl.ds((z - r) % cz, cz), :]
            turn = (slot - c) * field % LANES
            total = jnp.where(lane == slot, pltpu.roll(part, turn, axis=1) if turn else part, total)
        buf[pl.ds(margin, cz), :] = total
        buf[pl.ds(0, margin), :] = total[cz - margin :]
        buf[pl.ds(margin + cz, margin), :] = total[:margin]

    late = [(slot, r) for slot, r, _, _, _ in runs if r > 0]
    row2 = lax.broadcasted_iota(jnp.int32, (2, LANES), 0)
    slot2 = lax.broadcasted_iota(jnp.int32, (2, LANES), 1) // field

    def send(d, carry):
        z0 = (d // rep) * sz
        start = z0 - reach_below(z0, cz) + margin
        for q in range(depth // 2):
            piece = first[pl.ds(start + 2 * q, 2), :]
            mask = None
            for slot, r in late:
                if r < 2 * q + 2:
                    m = (slot2 == slot) & (row2 + 2 * q >= r)
                    mask = m if mask is None else mask | m
            if mask is not None:
                piece = jnp.where(mask, second[pl.ds(start + 2 * q, 2), :], piece)
            out_ref[d, q] = piece
        return carry

    lax.fori_loop(0, n, send, 0, unroll=8)


def sweep_kernel(
    gx, yz, bx, by, cz, sz, rep, window, depth,
    recv_ref, w1, w2,
    out_ref,
    spin, spin2, ver, cosv, grad, hidden, bricks,
):
    pp = Plane(gx, yz, bx, by)
    nt, cells = pp.nt, pp.cells
    rows = spin.shape[2]
    stride = 2 * rows + 1
    blk = LANES // cells

    lane16 = lax.broadcasted_iota(jnp.int32, (16, LANES), 1) // cells
    runs = runs_of(window, depth)

    def arrive(d, carry):
        for q in range(depth // 2):
            bricks[d, pl.ds(2 * q, 2), :] = recv_ref[d, q]
        return carry

    lax.fori_loop(0, gx * yz, arrive, 0, unroll=8)

    def gather(t, carry):
        moved = []
        for k in range(blk):
            v = bricks[t * blk + k]
            moved.append(pltpu.roll(v, k * cells, axis=1) if k else v)
        for j in range(16):
            u = moved[0]
            for k in range(1, blk):
                u = jnp.where(lane16 == (j + k) % blk, moved[k], u)
            if j:
                u = pltpu.roll(u, LANES - j * cells, axis=1)
            for slot, r, length, c, z in runs:
                if slot == j // 2:
                    spin[2 * c + j % 2, t, pl.ds(PAD + z, length), :] = u[r : r + length]
                    spin2[2 * c + j % 2, t, pl.ds(PAD + z, length), :] = u[r : r + length]
        return carry

    if nt <= 2:
        for t in range(nt):
            gather(t, 0)
    else:
        lax.fori_loop(0, nt, gather, 0)
    for t in range(nt):
        cosv[t, pl.ds(14 * stride, 2 * stride), :] = jnp.ones((2 * stride, LANES), jnp.float32)

    me = lax.axis_index("gx") * yz + lax.axis_index("yz")
    z0 = (me // rep) * sz
    hz = cz // 2
    below = reach_below(z0, cz)
    zs = (z0 - below + cz) % cz
    first = ((zs + hz - 1) // hz) * hz
    inside = first - zs < window
    border = PAD + first - zs
    hi_above = first % cz == hz
    own = PAD + below

    def is_hi(row):
        z = row - PAD + zs
        z = jnp.where(z >= cz, z - cz, z)
        return z >= hz

    low, high = own - 2, own + sz + 2
    ranges = []
    for _ in range(4):
        near_low = inside & hi_above & (border > low - 2) & (border < low + 2)
        near_high = inside & jnp.logical_not(hi_above) & (border > high - 2) & (border < high + 2)
        f_low = jnp.where(near_low, low - 2, low)
        f_high = jnp.where(near_high, high + 2, high)
        ranges.append((f_low, f_high))
        low, high = f_low - 2, f_high + 2
    ranges = ranges[::-1]

    def by_twos(count, body):
        if isinstance(count, int) and nt <= 2:
            for i in range(count):
                body(i, 0)
            return

        def two(i, carry):
            body(2 * i, carry)
            return body(2 * i + 1, carry)

        if nt > 2:
            lax.fori_loop(0, count, body, 0)
            return
        lax.fori_loop(0, count // 2, two, 0)

        @pl.when(count % 2 == 1)
        def _():
            body(count - 1, 0)

    def shifted_spins(start, count):
        def body(i, carry):
            r = start + 8 * i
            for dx, dy in ((1, 0), (-1, 0), (0, 1), (0, -1), (1, 1), (-1, -1)):
                for ca in range(6):
                    if (dx, dy) not in versions(ca % 2):
                        continue
                    n = versions(ca % 2).index((dx, dy))
                    got = pp.step([spin[ca, t, pl.ds(r, 8), :] for t in range(nt)], dx, dy)
                    for t in range(nt):
                        ver[n - 1, ca, t, pl.ds(r, 8), :] = got[t]
            return carry

        by_twos(count, body)

    def neighbour(c, a, dx, dy, t, r):
        n = versions(a).index((dx, dy))
        if n == 0:
            return spin[2 * c + a, t, pl.ds(r, 8), :]
        return ver[n - 1, 2 * c + a, t, pl.ds(r, 8), :]

    def cosines(start, count):
        def body(i, carry):
            r = start + 8 * i
            for t in range(nt):
                for a in range(2):
                    mine = [spin[2 * c + a, t, pl.ds(r, 8), :] for c in range(3)]
                    for o, (b, dx, dy, dz) in enumerate(bonds(a)):
                        total = mine[0] * neighbour(0, b, dx, dy, t, r + dz)
                        for c in (1, 2):
                            total += mine[c] * neighbour(c, b, dx, dy, t, r + dz)
                        cosv[t, pl.ds(o * stride + a * rows + r, 8), :] = total
            return carry

        by_twos(count, body)

    tc = 2 if nt % 2 == 0 else 1
    chunks = nt // tc

    def gradients(start, count):
        places = [(d, a, t) for d in range(1) for a in range(2) for t in range(tc)]

        def place(i):
            if chunks == 1:
                return start + 1 * i, 0
            return start + 1 * (i // chunks), (i % chunks) * tc

        def cosine(i):
            r, t0 = place(i)
            return jnp.concatenate(
                [cosv[t0 + t, pl.ds(a * rows + r + d, OP, stride=stride), :] for d, a, t in places], 1
            )

        def basis(i):
            c = cosine(i)
            c2 = c + c
            kinds = [c, c2 * c - 1.0]
            for _ in range(2, NB):
                kinds.append(c2 * kinds[-1] - kinds[-2])
            f_hi, f_lo = split(jnp.concatenate(kinds, 0))
            return jnp.concatenate([f_hi, f_lo], 0)

        def forward(rhs, slot):
            z = jnp.dot(w1[...], rhs, preferred_element_type=jnp.float32)
            hidden[slot] = z[:LANES] + z[LANES:]

        def activate(slot):
            u = jnp.tanh(hidden[slot])
            d_hi, d_lo = split(1.0 - u * u)
            return jnp.concatenate([d_hi, d_lo], 0)

        def backward(rhs):
            y = jnp.dot(w2[...], rhs, preferred_element_type=jnp.float32)
            return y[:LANES] + y[LANES:]

        def combine(i, y):
            r, t0 = place(i)
            c2 = 2.0 * cosine(i)
            b1 = y[(NB - 1) * OP :]
            b2 = None
            for k in range(NB - 2, -1, -1):
                new = y[k * OP : (k + 1) * OP] + c2 * b1
                if b2 is not None:
                    new = new - b2
                b1, b2 = new, b1
            for n, (d, a, t) in enumerate(places):
                grad[t0 + t, pl.ds(a * rows + r + d, OP, stride=stride), :] = b1[:, n * LANES : (n + 1) * LANES]

        for k in range(2):
            forward(basis(k), k)

        def one(i, slot):
            y = backward(activate(slot))
            forward(basis(i), slot)
            combine(i - 2, y)

        total = count * chunks
        done = 2
        if isinstance(total, int) and total <= 8:
            for i in range(done, total):
                one(i, i % 2)
        else:
            for many in (16, 8, 4, 2) if chunks == 1 else (2,):
                def body(i, first, many=many):
                    for k in range(many):
                        one(first + i * many + k, k % 2)
                    return first

                times = (total - done) // many
                lax.fori_loop(0, times, body, done)
                done = done + times * many
        for k in range(2):
            combine(total - 2 + k, backward(activate(k)))

    def field(r):
        out = []
        for a in range(2):
            total = [[None] * nt for _ in range(3)]
            for o, (b, dx, dy, dz) in enumerate(bonds(a)):
                m = mate_of(o)
                theirs = [grad[t, pl.ds(m * stride + b * rows + r + dz, 8), :] for t in range(nt)]
                theirs = pp.step(theirs, dx, dy)
                for t in range(nt):
                    coeff = grad[t, pl.ds(o * stride + a * rows + r, 8), :] + theirs[t]
                    for c in range(3):
                        term = coeff * neighbour(c, b, dx, dy, t, r + dz)
                        total[c][t] = term if total[c][t] is None else total[c][t] + term
            out.append([[-x for x in per] for per in total])
        return out

    def update(start, count, stage, only_border):
        def body(i, carry):
            r = start + 8 * i
            row = lax.broadcasted_iota(jnp.int32, (8, LANES), 0) + r
            if only_border:
                from_border = jnp.where(hi_above, row - border, border - 1 - row)
                wanted = (from_border >= 0) & (from_border < 2)
            else:
                wanted = True
            h = field(r)
            for a in range(2):
                for t in range(nt):
                    xl, yl, _ = pp.at(t)
                    mask = (
                        ((xl >= bx // 2).astype(jnp.int32) == stage // 2)
                        & ((yl >= by // 2).astype(jnp.int32) == stage % 2)
                        & wanted
                    )
                    s = [spin[2 * c + a, t, pl.ds(r, 8), :] for c in range(3)]
                    w = [TIME_STEP * h[a][c][t] for c in range(3)]
                    square = 0.25 * (w[0] * w[0] + w[1] * w[1] + w[2] * w[2])
                    sn, cs, hs = half_turn(square)
                    cosr = 1.0 - 2.0 * sn * sn
                    sinc = hs * cs
                    proj = 0.5 * hs * hs * (w[0] * s[0] + w[1] * s[1] + w[2] * s[2])
                    for c in range(3):
                        p, q = (c + 1) % 3, (c + 2) % 3
                        cross = w[p] * s[q] - w[q] * s[p]
                        new = cosr * s[c] + sinc * cross + proj * w[c]
                        old = spin2[2 * c + a, t, pl.ds(r, 8), :]
                        spin2[2 * c + a, t, pl.ds(r, 8), :] = jnp.where(mask, new, old)
            return carry

        by_twos(count, body)

    def take(everything):
        for i in range((window + 7) // 8):
            r = PAD + 8 * i
            row = lax.broadcasted_iota(jnp.int32, (8, LANES), 0) + r
            sel = True if everything is True else everything | jnp.logical_not(is_hi(row))
            for ca in range(6):
                for t in range(nt):
                    place = (ca, t, pl.ds(r, 8), slice(None))
                    spin[place] = spin2[place] if sel is True else jnp.where(sel, spin2[place], spin[place])

    def stage_pair(stage, carry):
        f_low, f_high = ranges[0]
        for s in range(1, 4):
            f_low = jnp.where(stage == s, ranges[s][0], f_low)
            f_high = jnp.where(stage == s, ranges[s][1], f_high)
        n = f_high - f_low
        crosses = inside & (f_low < border) & (border < f_high)
        shifted_spins(f_low - 2, (n + 11) // 8)
        cosines(f_low - 1, (n + 9) // 8)
        gradients(f_low - 1, (n + 3) // 2 * 2)
        update(f_low, (n + 7) // 8, stage, False)
        take(jnp.logical_not(crosses))

        @pl.when(crosses)
        def _():
            shifted_spins(border - 4, 1)
            cosines(border - 4, 1)
            gradients(border - 1, 2)
            update(border - 4, 1, stage, True)
            take(True)

        return carry

    lax.fori_loop(0, 4, stage_pair, 0)
    shifted_spins(own - 2, (sz + 11) // 8)
    cosines(own - 1, (sz + 9) // 8)
    gradients(own - 1, (sz + 3) // 2 * 2)

    final = field(own)
    lane16s = lax.broadcasted_iota(jnp.int32, (8, LANES), 1) // cells
    for t in range(nt):
        moved = []
        for j in range(12):
            ca = j % 6
            v = spin[ca, t, pl.ds(own, 8), :] if j < 6 else final[ca % 2][ca // 2][t]
            moved.append(pltpu.roll(v, j * cells, axis=1) if j else v)
        for k in range(blk):
            u = moved[0]
            for j in range(1, 12):
                u = jnp.where(lane16s == (j + k) % blk, moved[j], u)
            if k:
                u = pltpu.roll(u, LANES - k * cells, axis=1)
            out_ref[t * blk + k] = u[:sz]


def per_device(gx, yz, spin_vectors, pair_weight, mix_weight, mix_bias, out_weight):
    three, two, bx, by, cz = spin_vectors.shape
    n = gx * yz
    sz = max(1, cz // n)
    rep = n * sz // cz
    window = sz + 2 * REACH - 2
    depth = -(-3 * window // 16) * 2
    rows = -(-window // 8) * 8 + 2 * PAD
    nt = n * bx * by // LANES
    brick = three * two * bx * by
    vmem = pl.BlockSpec(memory_space=pltpu.VMEM)

    f32, bf16 = jnp.float32, jnp.bfloat16
    packed, w1, w2 = pl.pallas_call(
        functools.partial(pack_kernel, n, sz, rep, window, depth),
        out_shape=[
            jax.ShapeDtypeStruct((n, depth // 2, 2, LANES), f32),
            jax.ShapeDtypeStruct((2 * LANES, 2 * LANES), bf16),
            jax.ShapeDtypeStruct((2 * LANES, 2 * LANES), bf16),
        ],
        in_specs=[vmem] * 5,
        out_specs=[vmem] * 3,
        scratch_shapes=[
            pltpu.VMEM((2 * cz, LANES), f32),
            pltpu.VMEM((cz + 32, LANES), f32),
            pltpu.VMEM((cz + 32, LANES), f32),
        ],
        name="pack",
    )(spin_vectors.reshape(brick, cz), pair_weight, mix_weight, mix_bias[None], out_weight[None])
    received = lax.all_to_all(packed, ("gx", "yz"), 0, 0, tiled=True)

    result = pl.pallas_call(
        functools.partial(sweep_kernel, gx, yz, bx, by, cz, sz, rep, window, depth),
        out_shape=jax.ShapeDtypeStruct((n, sz, LANES), f32),
        in_specs=[vmem] * 3,
        out_specs=vmem,
        scratch_shapes=[
            pltpu.VMEM((6, nt, rows, LANES), f32),
            pltpu.VMEM((6, nt, rows, LANES), f32),
            pltpu.VMEM((5, 6, nt, rows, LANES), f32),
            pltpu.VMEM((nt, OP * (2 * rows + 1) + 7, LANES), f32),
            pltpu.VMEM((nt, OP * (2 * rows + 1) + 7, LANES), f32),
            pltpu.VMEM((2, LANES, 2 * (2 - nt % 2) * LANES), f32),
            pltpu.VMEM((n, 16, LANES), f32),
        ],
        compiler_params=pltpu.CompilerParams(vmem_limit_bytes=min(56, 8 + 4 * nt) * 2**20),
        name="sweep",
    )(received, w1, w2)
    returned = lax.all_to_all(result, ("gx", "yz"), 0, 0, tiled=True)
    if rep > 1:
        returned = returned[::rep]

    flat = returned.reshape(cz, LANES).T
    outs = [flat[:brick], flat[brick : 2 * brick]]
    return tuple(x.reshape(three, two, bx, by, cz) for x in outs)


def solution(mesh):
    gx, yz = mesh.shape["gx"], mesh.shape["yz"]
    spec = P(None, None, "gx", "yz", None)
    return jax.shard_map(
        functools.partial(per_device, gx, yz),
        mesh=mesh,
        in_specs=(spec, P(), P(), P(), P()),
        out_specs=(spec, spec),
        check_vma=False,
    )
```

```python
import functools
import math

import jax
import jax.numpy as jnp
from jax import lax
from jax.experimental import pallas as pl
from jax.experimental.pallas import tpu as pltpu
from jax.sharding import PartitionSpec as P

NB = 8
TIME_STEP = 0.1
PAD = 8
OP = 16
LANES = 128
REACH = 12

FIRST = [(x, y, z) for x in (-1, 0) for y in (-1, 0) for z in (-1, 0)]
SECOND = [(1, 0, 0), (-1, 0, 0), (0, 1, 0), (0, -1, 0), (0, 0, 1), (0, 0, -1)]


def bonds(a):
    sign = 1 if a == 0 else -1
    first = [(1 - a, sign * x, sign * y, sign * z) for x, y, z in FIRST]
    return first + [(a, *e) for e in SECOND]


def mate_of(o):
    return o if o < 8 else 8 + ((o - 8) ^ 1)


def versions(a):
    s = 1 if a == 0 else -1
    return [(0, 0), (s, 0), (0, s), (s, s), (-s, 0), (0, -s)]


class Plane:
    def __init__(self, gx, yz, bx, by, rows=8):
        self.bx, self.by, self.yz, self.cells = bx, by, yz, bx * by
        self.nl = gx * yz * bx * by
        self.nt = self.nl // LANES
        self.lane = lax.broadcasted_iota(jnp.int32, (rows, LANES), 1)
        self.halves = self.nt == 2 and by == 2
        if self.halves:
            bricks = gx * yz // 2
            x_in = self.lane // 2 % bx
            brick = self.lane // self.cells + self.lane % 2 * bricks
            self.source = {}
            for dx in (-1, 0, 1):
                for dy in (-1, 0, 1):
                    x = (brick // yz * bx + x_in + dx + gx * bx) % (gx * bx)
                    there = x // bx * yz + (brick % yz + dy + yz) % yz
                    self.source[(dx, dy)] = there % bricks * self.cells + x % bx * 2 + there // bricks

    def at(self, t):
        if self.halves:
            return self.lane // 2 % self.bx, jnp.full_like(self.lane, t), None
        lane = self.lane + t * LANES
        return (lane // self.by) % self.bx, lane % self.by, (lane // self.cells) % self.yz

    def roll(self, v, s):
        s = s % self.nl
        q, r = divmod(s, LANES)
        nt = self.nt
        if r == 0:
            return [v[(t + q) % nt] for t in range(nt)]
        rot = [pltpu.roll(x, LANES - r, axis=1) for x in v]
        if nt == 1:
            return rot
        keep = self.lane < LANES - r
        return [jnp.where(keep, rot[(t + q) % nt], rot[(t + q + 1) % nt]) for t in range(nt)]

    def step_x(self, v, d):
        if d == 0:
            return v
        ring = self.cells * self.yz
        inner = self.roll(v, d * self.by)
        outer = self.roll(v, d * (ring - (self.bx - 1) * self.by))
        edge = self.bx - 1 if d > 0 else 0
        return [jnp.where(self.at(t)[0] == edge, outer[t], inner[t]) for t in range(self.nt)]

    def step_y(self, v, d):
        if d == 0:
            return v
        ring = self.cells * self.yz
        hop = d * (self.cells - (self.by - 1))
        inner = self.roll(v, d)
        outer = self.roll(v, hop)
        wrap = self.roll(v, hop - d * ring)
        edge = self.by - 1 if d > 0 else 0
        last = self.yz - 1 if d > 0 else 0
        out = []
        for t in range(self.nt):
            _, yl, brick = self.at(t)
            far = jnp.where(brick == last, wrap[t], outer[t])
            out.append(jnp.where(yl == edge, far, inner[t]))
        return out

    def step_half(self, v, dx, dy, t):
        y = t + dy
        if dx == 0 and y // 2 == 0:
            return v[y % 2]
        return jnp.take_along_axis(v[y % 2], self.source[(dx, y // 2)], axis=1, mode="promise_in_bounds")

    def source_in(self, half, dx, dy):
        if dy == 0:
            return self.source[(dx, 0)]
        first, second = self.source[(dx, dy // 2)], self.source[(dx, (1 + dy) // 2)]
        return jnp.where(half == 0, first, second)

    def swapped(self, v):
        even = self.lane[: v[0].shape[0]] % 2 == 0
        return [
            jnp.where(even, v[0], pltpu.roll(v[1], 1, axis=1)),
            jnp.where(even, pltpu.roll(v[0], LANES - 1, axis=1), v[1]),
        ]

    def step(self, v, dx, dy):
        if not (dx or dy):
            return v
        if self.halves:
            return [self.step_half(v, dx, dy, t) for t in range(2)]
        return self.step_x(self.step_y(v, dy), dx)


def split(x):
    hi = x.astype(jnp.bfloat16)
    return hi, (x - hi.astype(jnp.float32)).astype(jnp.bfloat16)


def half_turn(square):
    v = jnp.sqrt(square)
    n = jnp.round(v * (1.0 / math.pi))
    p = ((v - n * 3.140625) - n * 9.67502593994140625e-4) - n * 1.5099579909783764e-7
    s = p * p
    sine, cosine = -1.0 / 39916800, 1.0 / 479001600
    for k in (9, 7, 5, 3, 1):
        sine = sine * s + (-1.0) ** (k // 2) / math.factorial(k)
    for k in (10, 8, 6, 4, 2, 0):
        cosine = cosine * s + (-1.0) ** (k // 2) / math.factorial(k)
    sn = sine * p
    small = n == 0.0
    return sn, cosine, jnp.where(small, sine, sn / jnp.where(small, 1.0, v))


def runs_of(window, depth):
    runs = []
    for slot in range(8):
        f, end = slot * depth, min((slot + 1) * depth, 3 * window)
        while f < end:
            c, z = divmod(f, window)
            length = min(end - f, window - z)
            runs.append((slot, f - slot * depth, length, c, z))
            f += length
    return runs


def reach_below(z0, cz):
    return jnp.where((z0 - 1 - cz // 2 + cz) % cz < REACH, REACH, REACH - 2)


def pack_kernel(
    n, sz, rep, window, depth,
    x_ref, pair_ref, mix_ref, bias_ref, outw_ref,
    out_ref, w1, w2,
    ext, first, second,
):
    parts = []
    for k in range(NB):
        part = pair_ref[pl.ds(k, 14, stride=NB), :]
        parts.append(jnp.concatenate([part, jnp.zeros((OP - 14, part.shape[1]), jnp.float32)], 0))
    pair = jnp.concatenate(parts, 0)
    w = jnp.dot(pair, mix_ref[...], precision=lax.Precision.HIGHEST, preferred_element_type=jnp.float32)
    row = lax.broadcasted_iota(jnp.int32, w.shape, 0)
    shift = bias_ref[...]
    rest = shift - split(shift)[0].astype(jnp.float32)
    rest = rest - split(rest)[0].astype(jnp.float32)
    hi, lo = split(jnp.where(row == 14, shift, jnp.where(row == 15, rest, w)).T)
    w1[...] = jnp.concatenate([jnp.concatenate([hi, hi], 1), jnp.concatenate([lo, lo], 1)], 0)
    degree = row // OP + 1
    hi, lo = split(w * degree.astype(jnp.float32) * outw_ref[...])
    w2[...] = jnp.concatenate([jnp.concatenate([hi, hi], 1), jnp.concatenate([lo, lo], 1)], 0)

    rows, cz = x_ref.shape
    field = rows // 3
    x = jnp.concatenate([x_ref[...], jnp.zeros((LANES - rows, cz), jnp.float32)], 0)
    cells = x.T
    ext[pl.ds(0, cz), :] = cells
    ext[pl.ds(cz, cz), :] = cells
    runs = runs_of(window, depth)
    lane = lax.broadcasted_iota(jnp.int32, (cz, LANES), 1) // field
    margin = 16
    for buf, chosen in ((first, [r for r in runs if r[1] == 0]), (second, [r for r in runs if r[1] > 0])):
        total = cells
        for slot, r, _, c, z in chosen:
            part = ext[pl.ds((z - r) % cz, cz), :]
            turn = (slot - c) * field % LANES
            total = jnp.where(lane == slot, pltpu.roll(part, turn, axis=1) if turn else part, total)
        buf[pl.ds(margin, cz), :] = total
        buf[pl.ds(0, margin), :] = total[cz - margin :]
        buf[pl.ds(margin + cz, margin), :] = total[:margin]

    late = [(slot, r) for slot, r, _, _, _ in runs if r > 0]
    row2 = lax.broadcasted_iota(jnp.int32, (2, LANES), 0)
    slot2 = lax.broadcasted_iota(jnp.int32, (2, LANES), 1) // field

    def send(d, carry):
        z0 = (d // rep) * sz
        start = z0 - reach_below(z0, cz) + margin
        for q in range(depth // 2):
            piece = first[pl.ds(start + 2 * q, 2), :]
            mask = None
            for slot, r in late:
                if r < 2 * q + 2:
                    m = (slot2 == slot) & (row2 + 2 * q >= r)
                    mask = m if mask is None else mask | m
            if mask is not None:
                piece = jnp.where(mask, second[pl.ds(start + 2 * q, 2), :], piece)
            out_ref[d, q] = piece
        return carry

    lax.fori_loop(0, n, send, 0, unroll=8)


def sweep_kernel(
    gx, yz, bx, by, cz, sz, rep, window, depth,
    recv_ref, w1, w2,
    out_ref,
    spin, spin2, ver, cosv, grad, hidden, bricks,
):
    pp = Plane(gx, yz, bx, by)
    nt, cells = pp.nt, pp.cells
    rows = spin.shape[2]
    stride = 2 * rows + 1
    blk = LANES // cells

    lane16 = lax.broadcasted_iota(jnp.int32, (16, LANES), 1) // cells
    runs = runs_of(window, depth)

    def arrive(d, carry):
        for q in range(depth // 2):
            bricks[d, pl.ds(2 * q, 2), :] = recv_ref[d, q]
        return carry

    lax.fori_loop(0, gx * yz, arrive, 0, unroll=8)

    def gather(t, carry):
        moved = []
        for k in range(blk):
            v = bricks[t * blk + k]
            moved.append(pltpu.roll(v, k * cells, axis=1) if k else v)
        for j in range(16):
            u = moved[0]
            for k in range(1, blk):
                u = jnp.where(lane16 == (j + k) % blk, moved[k], u)
            if j:
                u = pltpu.roll(u, LANES - j * cells, axis=1)
            for slot, r, length, c, z in runs:
                if slot == j // 2:
                    spin[2 * c + j % 2, t, pl.ds(PAD + z, length), :] = u[r : r + length]
                    spin2[2 * c + j % 2, t, pl.ds(PAD + z, length), :] = u[r : r + length]
        return carry

    if nt <= 2:
        for t in range(nt):
            gather(t, 0)
    else:
        lax.fori_loop(0, nt, gather, 0)
    if pp.halves:
        for ca in range(6):
            for i in range((window + 7) // 8):
                at = [(ca, t, pl.ds(PAD + 8 * i, 8), slice(None)) for t in range(2)]
                for t, v in enumerate(pp.swapped([spin[p] for p in at])):
                    spin[at[t]] = v
                    spin2[at[t]] = v
    for t in range(nt):
        cosv[t, pl.ds(14 * stride, 2 * stride), :] = jnp.ones((2 * stride, LANES), jnp.float32)

    me = lax.axis_index("gx") * yz + lax.axis_index("yz")
    z0 = (me // rep) * sz
    hz = cz // 2
    below = reach_below(z0, cz)
    zs = (z0 - below + cz) % cz
    first = ((zs + hz - 1) // hz) * hz
    inside = first - zs < window
    border = PAD + first - zs
    hi_above = first % cz == hz
    own = PAD + below

    def is_hi(row):
        z = row - PAD + zs
        z = jnp.where(z >= cz, z - cz, z)
        return z >= hz

    low, high = own - 2, own + sz + 2
    ranges = []
    for _ in range(4):
        near_low = inside & hi_above & (border > low - 2) & (border < low + 2)
        near_high = inside & jnp.logical_not(hi_above) & (border > high - 2) & (border < high + 2)
        f_low = jnp.where(near_low, low - 2, low)
        f_high = jnp.where(near_high, high + 2, high)
        ranges.append((f_low, f_high))
        low, high = f_low - 2, f_high + 2
    ranges = ranges[::-1]

    def by_twos(count, body):
        if isinstance(count, int) and nt <= 2:
            for i in range(count):
                body(i, 0)
            return

        def two(i, carry):
            body(2 * i, carry)
            return body(2 * i + 1, carry)

        if nt > 2:
            lax.fori_loop(0, count, body, 0)
            return
        lax.fori_loop(0, count // 2, two, 0)

        @pl.when(count % 2 == 1)
        def _():
            body(count - 1, 0)

    def shifted_spins(start, count):
        def body(i, carry):
            r = start + 8 * i
            for dx, dy in ((1, 0), (-1, 0), (0, 1), (0, -1), (1, 1), (-1, -1)):
                for ca in range(6):
                    if (dx, dy) not in versions(ca % 2):
                        continue
                    n = versions(ca % 2).index((dx, dy))
                    got = pp.step([spin[ca, t, pl.ds(r, 8), :] for t in range(nt)], dx, dy)
                    for t in range(nt):
                        ver[n - 1, ca, t, pl.ds(r, 8), :] = got[t]
            return carry

        by_twos(count, body)

    def neighbour(c, a, dx, dy, t, r):
        n = versions(a).index((dx, dy))
        if n == 0:
            return spin[2 * c + a, t, pl.ds(r, 8), :]
        return ver[n - 1, 2 * c + a, t, pl.ds(r, 8), :]

    def cosines(start, count):
        def body(i, carry):
            r = start + 8 * i
            for t in range(nt):
                for a in range(2):
                    mine = [spin[2 * c + a, t, pl.ds(r, 8), :] for c in range(3)]
                    for o, (b, dx, dy, dz) in enumerate(bonds(a)):
                        total = mine[0] * neighbour(0, b, dx, dy, t, r + dz)
                        for c in (1, 2):
                            total += mine[c] * neighbour(c, b, dx, dy, t, r + dz)
                        cosv[t, pl.ds(o * stride + a * rows + r, 8), :] = total
            return carry

        by_twos(count, body)

    tc = 2 if nt % 2 == 0 else 1
    chunks = nt // tc

    def features(c):
        c2 = c + c
        kinds = [c, c2 * c - 1.0]
        for _ in range(2, NB):
            kinds.append(c2 * kinds[-1] - kinds[-2])
        f_hi, f_lo = split(jnp.concatenate(kinds, 0))
        return jnp.concatenate([f_hi, f_lo], 0)

    def embedded(rhs):
        z = jnp.dot(w1[...], rhs, preferred_element_type=jnp.float32)
        return z[:LANES] + z[LANES:]

    def activated(hid):
        u = jnp.tanh(hid)
        d_hi, d_lo = split(1.0 - u * u)
        return jnp.concatenate([d_hi, d_lo], 0)

    def backward(rhs):
        y = jnp.dot(w2[...], rhs, preferred_element_type=jnp.float32)
        return y[:LANES] + y[LANES:]

    def slopes(c, y):
        c2 = c + c
        b1 = y[(NB - 1) * OP :]
        b2 = None
        for k in range(NB - 2, -1, -1):
            new = y[k * OP : (k + 1) * OP] + c2 * b1
            if b2 is not None:
                new = new - b2
            b1, b2 = new, b1
        return b1

    def bonds_at(t, a, r):
        return t, pl.ds(a * rows + r, OP, stride=stride), slice(None)

    def border_gradients(half):
        near = [bonds_at(t, a, border - a) for a in range(2) for t in range(2)]
        far = [bonds_at(half, a, border - 1 + a) for a in range(2)]
        chunks_of = [near + far]
        rhs = []
        for part in chunks_of:
            rhs.append(embedded(features(jnp.concatenate([cosv[p] for p in part], 1))))
        for part, hid in zip(chunks_of, rhs):
            c = jnp.concatenate([cosv[p] for p in part], 1)
            g = slopes(c, backward(activated(hid)))
            for n, p in enumerate(part):
                grad[p] = g[:, n * LANES : (n + 1) * LANES]

    def gradients(start, count):
        places = [(a, t) for a in range(2) for t in range(tc)]

        def place(i):
            if chunks == 1:
                return start + i, 0
            return start + i // chunks, (i % chunks) * tc

        def cosine(i):
            r, t0 = place(i)
            return jnp.concatenate([cosv[bonds_at(t0 + t, a, r)] for a, t in places], 1)

        def basis(i):
            return features(cosine(i))

        def forward(rhs, slot):
            hidden[slot] = embedded(rhs)

        def activate(slot):
            return activated(hidden[slot])

        def combine(i, y):
            r, t0 = place(i)
            g = slopes(cosine(i), y)
            for n, (a, t) in enumerate(places):
                grad[bonds_at(t0 + t, a, r)] = g[:, n * LANES : (n + 1) * LANES]

        for k in range(2):
            forward(basis(k), k)

        def one(i, slot):
            y = backward(activate(slot))
            forward(basis(i), slot)
            combine(i - 2, y)

        total = count * chunks
        done = 2
        if isinstance(total, int) and total <= 8:
            for i in range(done, total):
                one(i, i % 2)
        else:
            for many in (16, 8, 4, 2) if chunks == 1 else (2,):
                def body(i, first, many=many):
                    for k in range(many):
                        one(first + i * many + k, k % 2)
                    return first

                times = (total - done) // many
                lax.fori_loop(0, times, body, done)
                done = done + times * many
        for k in range(2):
            combine(total - 2 + k, backward(activate(k)))

    def half_field(r, half, lanes):
        out = []
        for a in range(2):
            total = [None] * 3
            for o, (b, dx, dy, dz) in enumerate(bonds(a)):
                m = mate_of(o)
                theirs = grad[half if dy == 0 else 1 - half, pl.ds(m * stride + b * rows + r + dz, 8), :]
                if dx or dy:
                    theirs = jnp.take_along_axis(theirs, lanes[(dx, dy)], axis=1, mode="promise_in_bounds")
                coeff = grad[half, pl.ds(o * stride + a * rows + r, 8), :] + theirs
                for c in range(3):
                    term = coeff * neighbour(c, b, dx, dy, half, r + dz)
                    total[c] = term if total[c] is None else total[c] + term
            out.append([-x for x in total])
        return out

    def field(r, tiles):
        out = []
        for a in range(2):
            total = [[None] * nt for _ in range(3)]
            for o, (b, dx, dy, dz) in enumerate(bonds(a)):
                m = mate_of(o)
                theirs = [grad[t, pl.ds(m * stride + b * rows + r + dz, 8), :] for t in range(nt)]
                if pp.halves:
                    theirs = [pp.step_half(theirs, dx, dy, t) if t in tiles else None for t in range(nt)]
                else:
                    theirs = pp.step(theirs, dx, dy)
                for t in tiles:
                    coeff = grad[t, pl.ds(o * stride + a * rows + r, 8), :] + theirs[t]
                    for c in range(3):
                        term = coeff * neighbour(c, b, dx, dy, t, r + dz)
                        total[c][t] = term if total[c][t] is None else total[c][t] + term
            out.append([[None if x is None else -x for x in per] for per in total])
        return out

    def update(start, count, stage, only_border):
        tiles = [stage % 2] if pp.halves else range(nt)
        if pp.halves:
            lanes = {(dx, dy): pp.source_in(tiles[0], dx, dy) for dx in (-1, 0, 1) for dy in (-1, 0, 1)}

        def body(i, carry):
            r = start + 8 * i
            row = lax.broadcasted_iota(jnp.int32, (8, LANES), 0) + r
            if only_border:
                from_border = jnp.where(hi_above, row - border, border - 1 - row)
                wanted = (from_border >= 0) & (from_border < 2)
            else:
                wanted = True
            h = half_field(r, tiles[0], lanes) if pp.halves else field(r, tiles)
            for a in range(2):
                for t in tiles:
                    xl, yl, _ = pp.at(t)
                    mask = (
                        ((xl >= bx // 2).astype(jnp.int32) == stage // 2)
                        & ((yl >= by // 2).astype(jnp.int32) == stage % 2)
                        & wanted
                    )
                    s = [spin[2 * c + a, t, pl.ds(r, 8), :] for c in range(3)]
                    w = [TIME_STEP * (h[a][c] if pp.halves else h[a][c][t]) for c in range(3)]
                    square = 0.25 * (w[0] * w[0] + w[1] * w[1] + w[2] * w[2])
                    sn, cs, hs = half_turn(square)
                    cosr = 1.0 - 2.0 * sn * sn
                    sinc = hs * cs
                    proj = 0.5 * hs * hs * (w[0] * s[0] + w[1] * s[1] + w[2] * s[2])
                    for c in range(3):
                        p, q = (c + 1) % 3, (c + 2) % 3
                        cross = w[p] * s[q] - w[q] * s[p]
                        new = cosr * s[c] + sinc * cross + proj * w[c]
                        old = spin2[2 * c + a, t, pl.ds(r, 8), :]
                        spin2[2 * c + a, t, pl.ds(r, 8), :] = jnp.where(mask, new, old)
            return carry

        by_twos(count, body)

    def take(everything):
        for i in range((window + 7) // 8):
            r = PAD + 8 * i
            row = lax.broadcasted_iota(jnp.int32, (8, LANES), 0) + r
            sel = True if everything is True else everything | jnp.logical_not(is_hi(row))
            for ca in range(6):
                for t in range(nt):
                    place = (ca, t, pl.ds(r, 8), slice(None))
                    spin[place] = spin2[place] if sel is True else jnp.where(sel, spin2[place], spin[place])

    def stage_pair(stage, carry):
        f_low, f_high = ranges[0]
        for s in range(1, 4):
            f_low = jnp.where(stage == s, ranges[s][0], f_low)
            f_high = jnp.where(stage == s, ranges[s][1], f_high)
        n = f_high - f_low
        crosses = inside & (f_low < border) & (border < f_high)
        shifted_spins(f_low - 2, (n + 11) // 8)
        cosines(f_low - 1, (n + 9) // 8)
        gradients(f_low - 1, (n + 3) // 2 * 2)
        update(f_low, (n + 7) // 8, stage, False)
        take(jnp.logical_not(crosses))

        @pl.when(crosses)
        def _():
            shifted_spins(border - 4, 1)
            cosines(border - 4, 1)
            if pp.halves:
                border_gradients(stage % 2)
            else:
                gradients(border - 1, 2)
            update(border - 4, 1, stage, True)
            take(True)

        return carry

    lax.fori_loop(0, 4, stage_pair, 0)
    shifted_spins(own - 2, (sz + 11) // 8)
    cosines(own - 1, (sz + 9) // 8)
    gradients(own - 1, (sz + 3) // 2 * 2)

    final = field(own, range(nt))
    results = []
    for j in range(12):
        ca = j % 6
        v = [spin[ca, t, pl.ds(own, 8), :] for t in range(nt)] if j < 6 else final[ca % 2][ca // 2]
        results.append(pp.swapped(v) if pp.halves else v)
    lane16s = lax.broadcasted_iota(jnp.int32, (8, LANES), 1) // cells
    for t in range(nt):
        moved = []
        for j in range(12):
            v = results[j][t]
            moved.append(pltpu.roll(v, j * cells, axis=1) if j else v)
        for k in range(blk):
            u = moved[0]
            for j in range(1, 12):
                u = jnp.where(lane16s == (j + k) % blk, moved[j], u)
            if k:
                u = pltpu.roll(u, LANES - k * cells, axis=1)
            out_ref[t * blk + k] = u[:sz]


def per_device(gx, yz, spin_vectors, pair_weight, mix_weight, mix_bias, out_weight):
    three, two, bx, by, cz = spin_vectors.shape
    n = gx * yz
    sz = max(1, cz // n)
    rep = n * sz // cz
    window = sz + 2 * REACH - 2
    depth = -(-3 * window // 16) * 2
    rows = -(-window // 8) * 8 + 2 * PAD
    nt = n * bx * by // LANES
    brick = three * two * bx * by
    vmem = pl.BlockSpec(memory_space=pltpu.VMEM)

    f32, bf16 = jnp.float32, jnp.bfloat16
    packed, w1, w2 = pl.pallas_call(
        functools.partial(pack_kernel, n, sz, rep, window, depth),
        out_shape=[
            jax.ShapeDtypeStruct((n, depth // 2, 2, LANES), f32),
            jax.ShapeDtypeStruct((2 * LANES, 2 * LANES), bf16),
            jax.ShapeDtypeStruct((2 * LANES, 2 * LANES), bf16),
        ],
        in_specs=[vmem] * 5,
        out_specs=[vmem] * 3,
        scratch_shapes=[
            pltpu.VMEM((2 * cz, LANES), f32),
            pltpu.VMEM((cz + 32, LANES), f32),
            pltpu.VMEM((cz + 32, LANES), f32),
        ],
        name="pack",
    )(spin_vectors.reshape(brick, cz), pair_weight, mix_weight, mix_bias[None], out_weight[None])
    received = lax.all_to_all(packed, ("gx", "yz"), 0, 0, tiled=True)

    result = pl.pallas_call(
        functools.partial(sweep_kernel, gx, yz, bx, by, cz, sz, rep, window, depth),
        out_shape=jax.ShapeDtypeStruct((n, sz, LANES), f32),
        in_specs=[vmem] * 3,
        out_specs=vmem,
        scratch_shapes=[
            pltpu.VMEM((6, nt, rows, LANES), f32),
            pltpu.VMEM((6, nt, rows, LANES), f32),
            pltpu.VMEM((5, 6, nt, rows, LANES), f32),
            pltpu.VMEM((nt, OP * (2 * rows + 1) + 7, LANES), f32),
            pltpu.VMEM((nt, OP * (2 * rows + 1) + 7, LANES), f32),
            pltpu.VMEM((2, LANES, 2 * (2 - nt % 2) * LANES), f32),
            pltpu.VMEM((n, 16, LANES), f32),
        ],
        compiler_params=pltpu.CompilerParams(vmem_limit_bytes=min(56, 8 + 4 * nt) * 2**20),
        name="sweep",
    )(received, w1, w2)
    returned = lax.all_to_all(result, ("gx", "yz"), 0, 0, tiled=True)
    if rep > 1:
        returned = returned[::rep]

    flat = returned.reshape(cz, LANES).T
    outs = [flat[:brick], flat[brick : 2 * brick]]
    return tuple(x.reshape(three, two, bx, by, cz) for x in outs)


def solution(mesh):
    gx, yz = mesh.shape["gx"], mesh.shape["yz"]
    spec = P(None, None, "gx", "yz", None)
    return jax.shard_map(
        functools.partial(per_device, gx, yz),
        mesh=mesh,
        in_specs=(spec, P(), P(), P(), P()),
        out_specs=(spec, spec),
        check_vma=False,
    )
```

```python
import functools
import math

import jax
import jax.numpy as jnp
from jax import lax
from jax.experimental import pallas as pl
from jax.experimental.pallas import tpu as pltpu
from jax.sharding import PartitionSpec as P

NB = 8
TIME_STEP = 0.1
PAD = 8
OP = 16
LANES = 128
REACH = 12

FIRST = [(x, y, z) for x in (-1, 0) for y in (-1, 0) for z in (-1, 0)]
SECOND = [(1, 0, 0), (-1, 0, 0), (0, 1, 0), (0, -1, 0), (0, 0, 1), (0, 0, -1)]


def bonds(a):
    sign = 1 if a == 0 else -1
    first = [(1 - a, sign * x, sign * y, sign * z) for x, y, z in FIRST]
    return first + [(a, *e) for e in SECOND]


def mate_of(o):
    return o if o < 8 else 8 + ((o - 8) ^ 1)


def versions(a):
    s = 1 if a == 0 else -1
    return [(0, 0), (s, 0), (0, s), (s, s), (-s, 0), (0, -s)]


class Plane:
    def __init__(self, gx, yz, bx, by, rows=8):
        self.bx, self.by, self.yz, self.cells = bx, by, yz, bx * by
        self.nl = gx * yz * bx * by
        self.nt = self.nl // LANES
        self.lane = lax.broadcasted_iota(jnp.int32, (rows, LANES), 1)
        self.halves = self.nt == 2 and by == 2
        if self.halves:
            bricks = gx * yz // 2
            x_in = self.lane // 2 % bx
            brick = self.lane // self.cells + self.lane % 2 * bricks
            self.source = {}
            for dx in (-1, 0, 1):
                for dy in (-1, 0, 1):
                    x = (brick // yz * bx + x_in + dx + gx * bx) % (gx * bx)
                    there = x // bx * yz + (brick % yz + dy + yz) % yz
                    self.source[(dx, dy)] = there % bricks * self.cells + x % bx * 2 + there // bricks

    def at(self, t):
        if self.halves:
            return self.lane // 2 % self.bx, jnp.full_like(self.lane, t), None
        lane = self.lane + t * LANES
        return (lane // self.by) % self.bx, lane % self.by, (lane // self.cells) % self.yz

    def roll(self, v, s):
        s = s % self.nl
        q, r = divmod(s, LANES)
        nt = self.nt
        if r == 0:
            return [v[(t + q) % nt] for t in range(nt)]
        rot = [pltpu.roll(x, LANES - r, axis=1) for x in v]
        if nt == 1:
            return rot
        keep = self.lane < LANES - r
        return [jnp.where(keep, rot[(t + q) % nt], rot[(t + q + 1) % nt]) for t in range(nt)]

    def step_x(self, v, d):
        if d == 0:
            return v
        ring = self.cells * self.yz
        inner = self.roll(v, d * self.by)
        outer = self.roll(v, d * (ring - (self.bx - 1) * self.by))
        edge = self.bx - 1 if d > 0 else 0
        return [jnp.where(self.at(t)[0] == edge, outer[t], inner[t]) for t in range(self.nt)]

    def step_y(self, v, d):
        if d == 0:
            return v
        ring = self.cells * self.yz
        hop = d * (self.cells - (self.by - 1))
        inner = self.roll(v, d)
        outer = self.roll(v, hop)
        wrap = self.roll(v, hop - d * ring)
        edge = self.by - 1 if d > 0 else 0
        last = self.yz - 1 if d > 0 else 0
        out = []
        for t in range(self.nt):
            _, yl, brick = self.at(t)
            far = jnp.where(brick == last, wrap[t], outer[t])
            out.append(jnp.where(yl == edge, far, inner[t]))
        return out

    def step_half(self, v, dx, dy, t):
        y = t + dy
        if dx == 0 and y // 2 == 0:
            return v[y % 2]
        return jnp.take_along_axis(v[y % 2], self.source[(dx, y // 2)], axis=1, mode="promise_in_bounds")

    def source_in(self, half, dx, dy):
        if dy == 0:
            return self.source[(dx, 0)]
        first, second = self.source[(dx, dy // 2)], self.source[(dx, (1 + dy) // 2)]
        return jnp.where(half == 0, first, second)

    def swapped(self, v):
        even = self.lane[: v[0].shape[0]] % 2 == 0
        return [
            jnp.where(even, v[0], pltpu.roll(v[1], 1, axis=1)),
            jnp.where(even, pltpu.roll(v[0], LANES - 1, axis=1), v[1]),
        ]

    def step(self, v, dx, dy):
        if not (dx or dy):
            return v
        if self.halves:
            return [self.step_half(v, dx, dy, t) for t in range(2)]
        return self.step_x(self.step_y(v, dy), dx)


def split(x):
    hi = x.astype(jnp.bfloat16)
    return hi, (x - hi.astype(jnp.float32)).astype(jnp.bfloat16)


def half_turn(square):
    v = jnp.sqrt(square)
    n = jnp.round(v * (1.0 / math.pi))
    p = ((v - n * 3.140625) - n * 9.67502593994140625e-4) - n * 1.5099579909783764e-7
    s = p * p
    sine, cosine = -1.0 / 39916800, 1.0 / 479001600
    for k in (9, 7, 5, 3, 1):
        sine = sine * s + (-1.0) ** (k // 2) / math.factorial(k)
    for k in (10, 8, 6, 4, 2, 0):
        cosine = cosine * s + (-1.0) ** (k // 2) / math.factorial(k)
    sn = sine * p
    small = n == 0.0
    return sn, cosine, jnp.where(small, sine, sn / jnp.where(small, 1.0, v))


def runs_of(window, depth):
    runs = []
    for slot in range(8):
        f, end = slot * depth, min((slot + 1) * depth, 3 * window)
        while f < end:
            c, z = divmod(f, window)
            length = min(end - f, window - z)
            runs.append((slot, f - slot * depth, length, c, z))
            f += length
    return runs


def reach_below(z0, cz):
    close = (z0 - 1 - cz // 2 + cz) % cz < REACH
    if isinstance(z0, int):
        return REACH if close else REACH - 2
    return jnp.where(close, REACH, REACH - 2)


def pack_kernel(
    n, sz, rep, window, depth,
    x_ref, pair_ref, mix_ref, bias_ref, outw_ref,
    out_ref, w1, w2,
    ext, first, second,
):
    parts = []
    for k in range(NB):
        part = pair_ref[pl.ds(k, 14, stride=NB), :]
        parts.append(jnp.concatenate([part, jnp.zeros((OP - 14, part.shape[1]), jnp.float32)], 0))
    pair = jnp.concatenate(parts, 0)
    w = jnp.dot(pair, mix_ref[...], precision=lax.Precision.HIGHEST, preferred_element_type=jnp.float32)
    row = lax.broadcasted_iota(jnp.int32, w.shape, 0)
    shift = bias_ref[...]
    rest = shift - split(shift)[0].astype(jnp.float32)
    rest = rest - split(rest)[0].astype(jnp.float32)
    hi, lo = split(jnp.where(row == 14, shift, jnp.where(row == 15, rest, w)).T)
    w1[...] = jnp.concatenate([jnp.concatenate([hi, hi], 1), jnp.concatenate([lo, lo], 1)], 0)
    degree = row // OP + 1
    hi, lo = split(w * degree.astype(jnp.float32) * outw_ref[...])
    w2[...] = jnp.concatenate([jnp.concatenate([hi, hi], 1), jnp.concatenate([lo, lo], 1)], 0)

    rows, cz = x_ref.shape
    field = rows // 3
    x = jnp.concatenate([x_ref[...], jnp.zeros((LANES - rows, cz), jnp.float32)], 0)
    cells = x.T
    ext[pl.ds(0, cz), :] = cells
    ext[pl.ds(cz, cz), :] = cells
    runs = runs_of(window, depth)
    lane = lax.broadcasted_iota(jnp.int32, (cz, LANES), 1) // field
    margin = 16
    for buf, chosen in ((first, [r for r in runs if r[1] == 0]), (second, [r for r in runs if r[1] > 0])):
        total = cells
        for slot, r, _, c, z in chosen:
            part = ext[pl.ds((z - r) % cz, cz), :]
            turn = (slot - c) * field % LANES
            total = jnp.where(lane == slot, pltpu.roll(part, turn, axis=1) if turn else part, total)
        buf[pl.ds(margin, cz), :] = total
        buf[pl.ds(0, margin), :] = total[cz - margin :]
        buf[pl.ds(margin + cz, margin), :] = total[:margin]

    late = [(slot, r) for slot, r, _, _, _ in runs if r > 0]
    row2 = lax.broadcasted_iota(jnp.int32, (2, LANES), 0)
    slot2 = lax.broadcasted_iota(jnp.int32, (2, LANES), 1) // field

    def send(d, carry):
        z0 = (d // rep) * sz
        start = z0 - reach_below(z0, cz) + margin
        for q in range(depth // 2):
            piece = first[pl.ds(start + 2 * q, 2), :]
            mask = None
            for slot, r in late:
                if r < 2 * q + 2:
                    m = (slot2 == slot) & (row2 + 2 * q >= r)
                    mask = m if mask is None else mask | m
            if mask is not None:
                piece = jnp.where(mask, second[pl.ds(start + 2 * q, 2), :], piece)
            out_ref[d, q] = piece
        return carry

    if n <= 32:
        for d in range(n):
            send(d, 0)
    else:
        lax.fori_loop(0, n, send, 0, unroll=8)


def sweep_kernel(
    gx, yz, bx, by, cz, sz, rep, window, depth,
    recv_ref, w1, w2,
    out_ref,
    spin, spin2, ver, cosv, grad, hidden, bricks,
):
    pp = Plane(gx, yz, bx, by)
    nt, cells = pp.nt, pp.cells
    rows = spin.shape[2]
    stride = 2 * rows + 1
    blk = LANES // cells

    lane16 = lax.broadcasted_iota(jnp.int32, (16, LANES), 1) // cells
    runs = runs_of(window, depth)

    def arrive(d, carry):
        for q in range(depth // 2):
            bricks[d, pl.ds(2 * q, 2), :] = recv_ref[d, q]
        return carry

    if gx * yz <= 32:
        for d in range(gx * yz):
            arrive(d, 0)
    else:
        lax.fori_loop(0, gx * yz, arrive, 0, unroll=8)

    def gather(t, carry):
        moved = []
        for k in range(blk):
            v = bricks[t * blk + k]
            moved.append(pltpu.roll(v, k * cells, axis=1) if k else v)
        for j in range(16):
            u = moved[0]
            for k in range(1, blk):
                u = jnp.where(lane16 == (j + k) % blk, moved[k], u)
            if j:
                u = pltpu.roll(u, LANES - j * cells, axis=1)
            for slot, r, length, c, z in runs:
                if slot == j // 2:
                    spin[2 * c + j % 2, t, pl.ds(PAD + z, length), :] = u[r : r + length]
                    if not pp.halves:
                        spin2[2 * c + j % 2, t, pl.ds(PAD + z, length), :] = u[r : r + length]
        return carry

    if nt <= 2:
        for t in range(nt):
            gather(t, 0)
    else:
        lax.fori_loop(0, nt, gather, 0)
    if pp.halves:
        for ca in range(6):
            for i in range((window + 7) // 8):
                at = [(ca, t, pl.ds(PAD + 8 * i, 8), slice(None)) for t in range(2)]
                for t, v in enumerate(pp.swapped([spin[p] for p in at])):
                    spin[at[t]] = v
                    spin2[at[t]] = v
    for t in range(nt):
        cosv[t, pl.ds(14 * stride, 2 * stride), :] = jnp.ones((2 * stride, LANES), jnp.float32)

    me = lax.axis_index("gx") * yz + lax.axis_index("yz")
    z0 = (me // rep) * sz
    hz = cz // 2
    below = reach_below(z0, cz)
    zs = (z0 - below + cz) % cz
    first = ((zs + hz - 1) // hz) * hz
    inside = first - zs < window
    border = PAD + first - zs
    hi_above = first % cz == hz
    own = PAD + below

    def is_hi(row):
        z = row - PAD + zs
        z = jnp.where(z >= cz, z - cz, z)
        return z >= hz

    low, high = own - 2, own + sz + 2
    ranges = []
    for _ in range(4):
        near_low = inside & hi_above & (border > low - 2) & (border < low + 2)
        near_high = inside & jnp.logical_not(hi_above) & (border > high - 2) & (border < high + 2)
        f_low = jnp.where(near_low, low - 2, low)
        f_high = jnp.where(near_high, high + 2, high)
        ranges.append((f_low, f_high))
        low, high = f_low - 2, f_high + 2
    ranges = ranges[::-1]

    def by_twos(count, body):
        if isinstance(count, int) and nt <= 2:
            for i in range(count):
                body(i, 0)
            return

        def two(i, carry):
            body(2 * i, carry)
            return body(2 * i + 1, carry)

        if nt > 2:
            lax.fori_loop(0, count, body, 0)
            return
        lax.fori_loop(0, count // 2, two, 0)

        @pl.when(count % 2 == 1)
        def _():
            body(count - 1, 0)

    def shifted_spins(start, count):
        def body(i, carry):
            r = start + 8 * i
            for dx, dy in ((1, 0), (-1, 0), (0, 1), (0, -1), (1, 1), (-1, -1)):
                for ca in range(6):
                    if (dx, dy) not in versions(ca % 2):
                        continue
                    n = versions(ca % 2).index((dx, dy))
                    got = pp.step([spin[ca, t, pl.ds(r, 8), :] for t in range(nt)], dx, dy)
                    for t in range(nt):
                        ver[n - 1, ca, t, pl.ds(r, 8), :] = got[t]
            return carry

        by_twos(count, body)

    def neighbour(c, a, dx, dy, t, r):
        n = versions(a).index((dx, dy))
        if n == 0:
            return spin[2 * c + a, t, pl.ds(r, 8), :]
        return ver[n - 1, 2 * c + a, t, pl.ds(r, 8), :]

    def cosines(start, count):
        def body(i, carry):
            r = start + 8 * i
            for t in range(nt):
                for a in range(2):
                    mine = [spin[2 * c + a, t, pl.ds(r, 8), :] for c in range(3)]
                    for o, (b, dx, dy, dz) in enumerate(bonds(a)):
                        total = mine[0] * neighbour(0, b, dx, dy, t, r + dz)
                        for c in (1, 2):
                            total += mine[c] * neighbour(c, b, dx, dy, t, r + dz)
                        cosv[t, pl.ds(o * stride + a * rows + r, 8), :] = total
            return carry

        by_twos(count, body)

    tc = 2 if nt % 2 == 0 else 1
    chunks = nt // tc

    def features(c):
        c2 = c + c
        kinds = [c, c2 * c - 1.0]
        for _ in range(2, NB):
            kinds.append(c2 * kinds[-1] - kinds[-2])
        f_hi, f_lo = split(jnp.concatenate(kinds, 0))
        return jnp.concatenate([f_hi, f_lo], 0)

    def embedded(rhs):
        z = jnp.dot(w1[...], rhs, preferred_element_type=jnp.float32)
        return z[:LANES] + z[LANES:]

    def activated(hid):
        u = jnp.tanh(hid)
        d_hi, d_lo = split(1.0 - u * u)
        return jnp.concatenate([d_hi, d_lo], 0)

    def backward(rhs):
        y = jnp.dot(w2[...], rhs, preferred_element_type=jnp.float32)
        return y[:LANES] + y[LANES:]

    def slopes(c, y):
        c2 = c + c
        b1 = y[(NB - 1) * OP :]
        b2 = None
        for k in range(NB - 2, -1, -1):
            new = y[k * OP : (k + 1) * OP] + c2 * b1
            if b2 is not None:
                new = new - b2
            b1, b2 = new, b1
        return b1

    def bonds_at(t, a, r):
        return t, pl.ds(a * rows + r, OP, stride=stride), slice(None)

    def border_gradients(half):
        near = [bonds_at(t, a, border - a) for a in range(2) for t in range(2)]
        far = [bonds_at(half, a, border - 1 + a) for a in range(2)]
        chunks_of = [near + far]
        rhs = []
        for part in chunks_of:
            rhs.append(embedded(features(jnp.concatenate([cosv[p] for p in part], 1))))
        for part, hid in zip(chunks_of, rhs):
            c = jnp.concatenate([cosv[p] for p in part], 1)
            g = slopes(c, backward(activated(hid)))
            for n, p in enumerate(part):
                grad[p] = g[:, n * LANES : (n + 1) * LANES]

    def gradients(start, count):
        places = [(a, t) for a in range(2) for t in range(tc)]

        def place(i):
            if chunks == 1:
                return start + i, 0
            return start + i // chunks, (i % chunks) * tc

        def cosine(i):
            r, t0 = place(i)
            return jnp.concatenate([cosv[bonds_at(t0 + t, a, r)] for a, t in places], 1)

        def basis(i):
            return features(cosine(i))

        def forward(rhs, slot):
            hidden[slot] = embedded(rhs)

        def activate(slot):
            return activated(hidden[slot])

        def combine(i, y):
            r, t0 = place(i)
            g = slopes(cosine(i), y)
            for n, (a, t) in enumerate(places):
                grad[bonds_at(t0 + t, a, r)] = g[:, n * LANES : (n + 1) * LANES]

        for k in range(2):
            forward(basis(k), k)

        def one(i, slot):
            y = backward(activate(slot))
            forward(basis(i), slot)
            combine(i - 2, y)

        total = count * chunks
        done = 2
        if isinstance(total, int) and total <= 8:
            for i in range(done, total):
                one(i, i % 2)
        else:
            for many in (20, 16, 8, 4, 2) if chunks == 1 else (2,):
                def body(i, first, many=many):
                    for k in range(many):
                        one(first + i * many + k, k % 2)
                    return first

                times = (total - done) // many
                lax.fori_loop(0, times, body, done)
                done = done + times * many
        for k in range(2):
            combine(total - 2 + k, backward(activate(k)))

    def half_field(r, half, lanes):
        out = []
        for a in range(2):
            total = [None] * 3
            for o, (b, dx, dy, dz) in enumerate(bonds(a)):
                m = mate_of(o)
                theirs = grad[half if dy == 0 else 1 - half, pl.ds(m * stride + b * rows + r + dz, 8), :]
                if dx or dy:
                    theirs = jnp.take_along_axis(theirs, lanes[(dx, dy)], axis=1, mode="promise_in_bounds")
                coeff = grad[half, pl.ds(o * stride + a * rows + r, 8), :] + theirs
                for c in range(3):
                    term = coeff * neighbour(c, b, dx, dy, half, r + dz)
                    total[c] = term if total[c] is None else total[c] + term
            out.append([-x for x in total])
        return out

    def field(r, tiles):
        out = []
        for a in range(2):
            total = [[None] * nt for _ in range(3)]
            for o, (b, dx, dy, dz) in enumerate(bonds(a)):
                m = mate_of(o)
                theirs = [grad[t, pl.ds(m * stride + b * rows + r + dz, 8), :] for t in range(nt)]
                if pp.halves:
                    theirs = [pp.step_half(theirs, dx, dy, t) if t in tiles else None for t in range(nt)]
                else:
                    theirs = pp.step(theirs, dx, dy)
                for t in tiles:
                    coeff = grad[t, pl.ds(o * stride + a * rows + r, 8), :] + theirs[t]
                    for c in range(3):
                        term = coeff * neighbour(c, b, dx, dy, t, r + dz)
                        total[c][t] = term if total[c][t] is None else total[c][t] + term
            out.append([[None if x is None else -x for x in per] for per in total])
        return out

    def update(start, count, stage, only_border):
        tiles = [stage % 2] if pp.halves else range(nt)
        if pp.halves:
            lanes = {(dx, dy): pp.source_in(tiles[0], dx, dy) for dx in (-1, 0, 1) for dy in (-1, 0, 1)}

        def body(i, carry):
            r = start + 8 * i
            row = lax.broadcasted_iota(jnp.int32, (8, LANES), 0) + r
            if only_border:
                from_border = jnp.where(hi_above, row - border, border - 1 - row)
                wanted = (from_border >= 0) & (from_border < 2)
            else:
                wanted = True
            h = half_field(r, tiles[0], lanes) if pp.halves else field(r, tiles)
            for a in range(2):
                for t in tiles:
                    xl, yl, _ = pp.at(t)
                    mask = (
                        ((xl >= bx // 2).astype(jnp.int32) == stage // 2)
                        & ((yl >= by // 2).astype(jnp.int32) == stage % 2)
                        & wanted
                    )
                    s = [spin[2 * c + a, t, pl.ds(r, 8), :] for c in range(3)]
                    w = [TIME_STEP * (h[a][c] if pp.halves else h[a][c][t]) for c in range(3)]
                    square = 0.25 * (w[0] * w[0] + w[1] * w[1] + w[2] * w[2])
                    sn, cs, hs = half_turn(square)
                    cosr = 1.0 - 2.0 * sn * sn
                    sinc = hs * cs
                    proj = 0.5 * hs * hs * (w[0] * s[0] + w[1] * s[1] + w[2] * s[2])
                    for c in range(3):
                        p, q = (c + 1) % 3, (c + 2) % 3
                        cross = w[p] * s[q] - w[q] * s[p]
                        new = cosr * s[c] + sinc * cross + proj * w[c]
                        old = spin2[2 * c + a, t, pl.ds(r, 8), :]
                        spin2[2 * c + a, t, pl.ds(r, 8), :] = jnp.where(mask, new, old)
            return carry

        by_twos(count, body)

    def take(everything):
        for i in range((window + 7) // 8):
            r = PAD + 8 * i
            row = lax.broadcasted_iota(jnp.int32, (8, LANES), 0) + r
            sel = True if everything is True else everything | jnp.logical_not(is_hi(row))
            for ca in range(6):
                for t in range(nt):
                    place = (ca, t, pl.ds(r, 8), slice(None))
                    spin[place] = spin2[place] if sel is True else jnp.where(sel, spin2[place], spin[place])

    def stage_pair(stage, carry):
        f_low, f_high = ranges[0]
        for s in range(1, 4):
            f_low = jnp.where(stage == s, ranges[s][0], f_low)
            f_high = jnp.where(stage == s, ranges[s][1], f_high)
        n = f_high - f_low
        crosses = inside & (f_low < border) & (border < f_high)
        shifted_spins(f_low - 2, (n + 11) // 8)
        cosines(f_low - 1, (n + 9) // 8)
        gradients(f_low - 1, (n + 3) // 2 * 2)
        update(f_low, (n + 7) // 8, stage, False)
        take(jnp.logical_not(crosses))

        @pl.when(crosses)
        def _():
            shifted_spins(border - 4, 1)
            cosines(border - 4, 1)
            if pp.halves:
                border_gradients(stage % 2)
            else:
                gradients(border - 1, 2)
            update(border - 4, 1, stage, True)
            take(True)

        return carry

    lax.fori_loop(0, 4, stage_pair, 0)
    shifted_spins(own - 2, (sz + 11) // 8)
    cosines(own - 1, (sz + 9) // 8)
    gradients(own - 1, (sz + 3) // 2 * 2)

    final = field(own, range(nt))
    results = []
    for j in range(12):
        ca = j % 6
        v = [spin[ca, t, pl.ds(own, 8), :] for t in range(nt)] if j < 6 else final[ca % 2][ca // 2]
        results.append(pp.swapped(v) if pp.halves else v)
    lane16s = lax.broadcasted_iota(jnp.int32, (8, LANES), 1) // cells
    for t in range(nt):
        moved = []
        for j in range(12):
            v = results[j][t]
            moved.append(pltpu.roll(v, j * cells, axis=1) if j else v)
        for k in range(blk):
            u = moved[0]
            for j in range(1, 12):
                u = jnp.where(lane16s == (j + k) % blk, moved[j], u)
            if k:
                u = pltpu.roll(u, LANES - k * cells, axis=1)
            out_ref[t * blk + k] = u[:sz]


def per_device(gx, yz, spin_vectors, pair_weight, mix_weight, mix_bias, out_weight):
    three, two, bx, by, cz = spin_vectors.shape
    n = gx * yz
    sz = max(1, cz // n)
    rep = n * sz // cz
    window = sz + 2 * REACH - 2
    depth = -(-3 * window // 16) * 2
    rows = -(-window // 8) * 8 + 2 * PAD
    nt = n * bx * by // LANES
    brick = three * two * bx * by
    vmem = pl.BlockSpec(memory_space=pltpu.VMEM)

    f32, bf16 = jnp.float32, jnp.bfloat16
    packed, w1, w2 = pl.pallas_call(
        functools.partial(pack_kernel, n, sz, rep, window, depth),
        out_shape=[
            jax.ShapeDtypeStruct((n, depth // 2, 2, LANES), f32),
            jax.ShapeDtypeStruct((2 * LANES, 2 * LANES), bf16),
            jax.ShapeDtypeStruct((2 * LANES, 2 * LANES), bf16),
        ],
        in_specs=[vmem] * 5,
        out_specs=[vmem] * 3,
        scratch_shapes=[
            pltpu.VMEM((2 * cz, LANES), f32),
            pltpu.VMEM((cz + 32, LANES), f32),
            pltpu.VMEM((cz + 32, LANES), f32),
        ],
        name="pack",
    )(spin_vectors.reshape(brick, cz), pair_weight, mix_weight, mix_bias[None], out_weight[None])
    received = lax.all_to_all(packed, ("gx", "yz"), 0, 0, tiled=True)

    result = pl.pallas_call(
        functools.partial(sweep_kernel, gx, yz, bx, by, cz, sz, rep, window, depth),
        out_shape=jax.ShapeDtypeStruct((n, sz, LANES), f32),
        in_specs=[vmem] * 3,
        out_specs=vmem,
        scratch_shapes=[
            pltpu.VMEM((6, nt, rows, LANES), f32),
            pltpu.VMEM((6, nt, rows, LANES), f32),
            pltpu.VMEM((5, 6, nt, rows, LANES), f32),
            pltpu.VMEM((nt, OP * (2 * rows + 1) + 7, LANES), f32),
            pltpu.VMEM((nt, OP * (2 * rows + 1) + 7, LANES), f32),
            pltpu.VMEM((2, LANES, 2 * (2 - nt % 2) * LANES), f32),
            pltpu.VMEM((n, 16, LANES), f32),
        ],
        compiler_params=pltpu.CompilerParams(vmem_limit_bytes=min(56, 8 + 4 * nt) * 2**20),
        name="sweep",
    )(received, w1, w2)
    returned = lax.all_to_all(result, ("gx", "yz"), 0, 0, tiled=True)
    if rep > 1:
        returned = returned[::rep]

    flat = returned.reshape(cz, LANES).T
    outs = [flat[:brick], flat[brick : 2 * brick]]
    return tuple(x.reshape(three, two, bx, by, cz) for x in outs)


def solution(mesh):
    gx, yz = mesh.shape["gx"], mesh.shape["yz"]
    spec = P(None, None, "gx", "yz", None)
    return jax.shard_map(
        functools.partial(per_device, gx, yz),
        mesh=mesh,
        in_specs=(spec, P(), P(), P(), P()),
        out_specs=(spec, spec),
        check_vma=False,
    )
```

```python
import functools
import math

import jax
import jax.numpy as jnp
from jax import lax
from jax.experimental import pallas as pl
from jax.experimental.pallas import tpu as pltpu
from jax.sharding import PartitionSpec as P

NB = 8
TIME_STEP = 0.1
PAD = 8
OP = 16
LANES = 128
REACH = 12

FIRST = [(x, y, z) for x in (-1, 0) for y in (-1, 0) for z in (-1, 0)]
SECOND = [(1, 0, 0), (-1, 0, 0), (0, 1, 0), (0, -1, 0), (0, 0, 1), (0, 0, -1)]


def bonds(a):
    sign = 1 if a == 0 else -1
    first = [(1 - a, sign * x, sign * y, sign * z) for x, y, z in FIRST]
    return first + [(a, *e) for e in SECOND]


def mate_of(o):
    return o if o < 8 else 8 + ((o - 8) ^ 1)


def versions(a):
    s = 1 if a == 0 else -1
    return [(0, 0), (s, 0), (0, s), (s, s), (-s, 0), (0, -s)]


class Plane:
    def __init__(self, gx, yz, bx, by, rows=8):
        self.bx, self.by, self.yz, self.cells = bx, by, yz, bx * by
        self.nl = gx * yz * bx * by
        self.nt = self.nl // LANES
        self.lane = lax.broadcasted_iota(jnp.int32, (rows, LANES), 1)
        self.halves = self.nt == 2 and by == 2
        if self.halves:
            bricks = gx * yz // 2
            x_in = self.lane // 2 % bx
            brick = self.lane // self.cells + self.lane % 2 * bricks
            self.source = {}
            for dx in (-1, 0, 1):
                for dy in (-1, 0, 1):
                    x = (brick // yz * bx + x_in + dx + gx * bx) % (gx * bx)
                    there = x // bx * yz + (brick % yz + dy + yz) % yz
                    self.source[(dx, dy)] = there % bricks * self.cells + x % bx * 2 + there // bricks

    def at(self, t):
        if self.halves:
            return self.lane // 2 % self.bx, jnp.full_like(self.lane, t), None
        lane = self.lane + t * LANES
        return (lane // self.by) % self.bx, lane % self.by, (lane // self.cells) % self.yz

    def roll(self, v, s):
        s = s % self.nl
        q, r = divmod(s, LANES)
        nt = self.nt
        if r == 0:
            return [v[(t + q) % nt] for t in range(nt)]
        rot = [pltpu.roll(x, LANES - r, axis=1) for x in v]
        if nt == 1:
            return rot
        keep = self.lane < LANES - r
        return [jnp.where(keep, rot[(t + q) % nt], rot[(t + q + 1) % nt]) for t in range(nt)]

    def step_x(self, v, d):
        if d == 0:
            return v
        ring = self.cells * self.yz
        inner = self.roll(v, d * self.by)
        outer = self.roll(v, d * (ring - (self.bx - 1) * self.by))
        edge = self.bx - 1 if d > 0 else 0
        return [jnp.where(self.at(t)[0] == edge, outer[t], inner[t]) for t in range(self.nt)]

    def step_y(self, v, d):
        if d == 0:
            return v
        ring = self.cells * self.yz
        hop = d * (self.cells - (self.by - 1))
        inner = self.roll(v, d)
        outer = self.roll(v, hop)
        wrap = self.roll(v, hop - d * ring)
        edge = self.by - 1 if d > 0 else 0
        last = self.yz - 1 if d > 0 else 0
        out = []
        for t in range(self.nt):
            _, yl, brick = self.at(t)
            far = jnp.where(brick == last, wrap[t], outer[t])
            out.append(jnp.where(yl == edge, far, inner[t]))
        return out

    def step_half(self, v, dx, dy, t):
        y = t + dy
        if dx == 0 and y // 2 == 0:
            return v[y % 2]
        return jnp.take_along_axis(v[y % 2], self.source[(dx, y // 2)], axis=1, mode="promise_in_bounds")

    def source_in(self, half, dx, dy):
        if dy == 0:
            return self.source[(dx, 0)]
        first, second = self.source[(dx, dy // 2)], self.source[(dx, (1 + dy) // 2)]
        return jnp.where(half == 0, first, second)

    def swapped(self, v):
        even = self.lane[: v[0].shape[0]] % 2 == 0
        return [
            jnp.where(even, v[0], pltpu.roll(v[1], 1, axis=1)),
            jnp.where(even, pltpu.roll(v[0], LANES - 1, axis=1), v[1]),
        ]

    def step(self, v, dx, dy):
        if not (dx or dy):
            return v
        if self.halves:
            return [self.step_half(v, dx, dy, t) for t in range(2)]
        return self.step_x(self.step_y(v, dy), dx)


def split(x):
    hi = x.astype(jnp.bfloat16)
    return hi, (x - hi.astype(jnp.float32)).astype(jnp.bfloat16)


def half_turn(square):
    v = jnp.sqrt(square)
    n = jnp.round(v * (1.0 / math.pi))
    p = ((v - n * 3.140625) - n * 9.67502593994140625e-4) - n * 1.5099579909783764e-7
    s = p * p
    sine, cosine = -1.0 / 39916800, 1.0 / 479001600
    for k in (9, 7, 5, 3, 1):
        sine = sine * s + (-1.0) ** (k // 2) / math.factorial(k)
    for k in (10, 8, 6, 4, 2, 0):
        cosine = cosine * s + (-1.0) ** (k // 2) / math.factorial(k)
    sn = sine * p
    small = n == 0.0
    return sn, cosine, jnp.where(small, sine, sn / jnp.where(small, 1.0, v))


def runs_of(window, depth):
    runs = []
    for slot in range(8):
        f, end = slot * depth, min((slot + 1) * depth, 3 * window)
        while f < end:
            c, z = divmod(f, window)
            length = min(end - f, window - z)
            runs.append((slot, f - slot * depth, length, c, z))
            f += length
    return runs


def reach_below(z0, cz):
    close = (z0 - 1 - cz // 2 + cz) % cz < REACH
    if isinstance(z0, int):
        return REACH if close else REACH - 2
    return jnp.where(close, REACH, REACH - 2)


def pack_kernel(
    n, sz, rep, window, depth,
    x_ref, pair_ref, mix_ref, bias_ref, outw_ref,
    out_ref, w1, w2,
    ext, first, second,
):
    parts = []
    for k in range(NB):
        part = pair_ref[pl.ds(k, 14, stride=NB), :]
        parts.append(jnp.concatenate([part, jnp.zeros((OP - 14, part.shape[1]), jnp.float32)], 0))
    pair = jnp.concatenate(parts, 0)
    w = jnp.dot(pair, mix_ref[...], precision=lax.Precision.HIGHEST, preferred_element_type=jnp.float32)
    row = lax.broadcasted_iota(jnp.int32, w.shape, 0)
    shift = bias_ref[...]
    rest = shift - split(shift)[0].astype(jnp.float32)
    rest = rest - split(rest)[0].astype(jnp.float32)
    hi, lo = split(jnp.where(row == 14, shift, jnp.where(row == 15, rest, w)).T)
    w1[...] = jnp.concatenate([jnp.concatenate([hi, hi], 1), jnp.concatenate([lo, lo], 1)], 0)
    degree = row // OP + 1
    hi, lo = split(w * degree.astype(jnp.float32) * outw_ref[...])
    w2[...] = jnp.concatenate([jnp.concatenate([hi, hi], 1), jnp.concatenate([lo, lo], 1)], 0)

    rows, cz = x_ref.shape
    field = rows // 3
    x = jnp.concatenate([x_ref[...], jnp.zeros((LANES - rows, cz), jnp.float32)], 0)
    cells = x.T
    ext[pl.ds(0, cz), :] = cells
    ext[pl.ds(cz, cz), :] = cells
    runs = runs_of(window, depth)
    lane = lax.broadcasted_iota(jnp.int32, (cz, LANES), 1) // field
    margin = 16
    for buf, chosen in ((first, [r for r in runs if r[1] == 0]), (second, [r for r in runs if r[1] > 0])):
        total = cells
        for slot, r, _, c, z in chosen:
            part = ext[pl.ds((z - r) % cz, cz), :]
            turn = (slot - c) * field % LANES
            total = jnp.where(lane == slot, pltpu.roll(part, turn, axis=1) if turn else part, total)
        buf[pl.ds(margin, cz), :] = total
        buf[pl.ds(0, margin), :] = total[cz - margin :]
        buf[pl.ds(margin + cz, margin), :] = total[:margin]

    late = [(slot, r) for slot, r, _, _, _ in runs if r > 0]
    row2 = lax.broadcasted_iota(jnp.int32, (2, LANES), 0)
    slot2 = lax.broadcasted_iota(jnp.int32, (2, LANES), 1) // field

    def send(d, carry):
        z0 = (d // rep) * sz
        start = z0 - reach_below(z0, cz) + margin
        for q in range(depth // 2):
            piece = first[pl.ds(start + 2 * q, 2), :]
            mask = None
            for slot, r in late:
                if r < 2 * q + 2:
                    m = (slot2 == slot) & (row2 + 2 * q >= r)
                    mask = m if mask is None else mask | m
            if mask is not None:
                piece = jnp.where(mask, second[pl.ds(start + 2 * q, 2), :], piece)
            out_ref[d, q] = piece
        return carry

    if n <= 32:
        for d in range(n):
            send(d, 0)
    else:
        lax.fori_loop(0, n, send, 0, unroll=8)


def sweep_kernel(
    gx, yz, bx, by, cz, sz, rep, window, depth,
    recv_ref, w1, w2,
    out_ref,
    spin, spin2, ver, cosv, grad, hidden, bricks,
):
    pp = Plane(gx, yz, bx, by)
    nt, cells = pp.nt, pp.cells
    rows = spin.shape[2]
    stride = 2 * rows + 1
    blk = LANES // cells

    lane16 = lax.broadcasted_iota(jnp.int32, (16, LANES), 1) // cells
    runs = runs_of(window, depth)

    def arrive(d, carry):
        for q in range(depth // 2):
            bricks[d, pl.ds(2 * q, 2), :] = recv_ref[d, q]
        return carry

    if gx * yz <= 32:
        for d in range(gx * yz):
            arrive(d, 0)
    else:
        lax.fori_loop(0, gx * yz, arrive, 0, unroll=8)

    def gather(t, carry):
        moved = []
        for k in range(blk):
            v = bricks[t * blk + k]
            moved.append(pltpu.roll(v, k * cells, axis=1) if k else v)
        for j in range(16):
            u = moved[0]
            for k in range(1, blk):
                u = jnp.where(lane16 == (j + k) % blk, moved[k], u)
            if j:
                u = pltpu.roll(u, LANES - j * cells, axis=1)
            for slot, r, length, c, z in runs:
                if slot == j // 2:
                    spin[2 * c + j % 2, t, pl.ds(PAD + z, length), :] = u[r : r + length]
                    if not pp.halves:
                        spin2[2 * c + j % 2, t, pl.ds(PAD + z, length), :] = u[r : r + length]
        return carry

    if nt <= 2:
        for t in range(nt):
            gather(t, 0)
    else:
        lax.fori_loop(0, nt, gather, 0)
    if pp.halves:
        for ca in range(6):
            for i in range((window + 7) // 8):
                at = [(ca, t, pl.ds(PAD + 8 * i, 8), slice(None)) for t in range(2)]
                for t, v in enumerate(pp.swapped([spin[p] for p in at])):
                    spin[at[t]] = v
                    spin2[at[t]] = v
    for t in range(nt):
        cosv[t, pl.ds(14 * stride, 2 * stride), :] = jnp.ones((2 * stride, LANES), jnp.float32)

    me = lax.axis_index("gx") * yz + lax.axis_index("yz")
    z0 = (me // rep) * sz
    hz = cz // 2
    below = reach_below(z0, cz)
    zs = (z0 - below + cz) % cz
    first = ((zs + hz - 1) // hz) * hz
    inside = first - zs < window
    border = PAD + first - zs
    hi_above = first % cz == hz
    own = PAD + below

    def is_hi(row):
        z = row - PAD + zs
        z = jnp.where(z >= cz, z - cz, z)
        return z >= hz

    low, high = own - 2, own + sz + 2
    ranges = []
    for _ in range(4):
        near_low = inside & hi_above & (border > low - 2) & (border < low + 2)
        near_high = inside & jnp.logical_not(hi_above) & (border > high - 2) & (border < high + 2)
        f_low = jnp.where(near_low, low - 2, low)
        f_high = jnp.where(near_high, high + 2, high)
        ranges.append((f_low, f_high))
        low, high = f_low - 2, f_high + 2
    ranges = ranges[::-1]

    def by_threes(count, body):
        if isinstance(count, int) and nt <= 2:
            for i in range(count):
                body(i, 0)
            return

        if nt > 2:
            lax.fori_loop(0, count, body, 0)
            return

        def some(many):
            def run(i, carry):
                for k in range(many):
                    body(3 * i + k, carry)
                return carry

            return run

        lax.fori_loop(0, count // 3, some(3), 0)
        for many in (1, 2):

            @pl.when(count % 3 == many)
            def _(many=many):
                some(many)(count // 3, 0)

    def shifted_spins(start, count):
        def body(i, carry):
            r = start + 8 * i
            for dx, dy in ((1, 0), (-1, 0), (0, 1), (0, -1), (1, 1), (-1, -1)):
                for ca in range(6):
                    if (dx, dy) not in versions(ca % 2):
                        continue
                    n = versions(ca % 2).index((dx, dy))
                    got = pp.step([spin[ca, t, pl.ds(r, 8), :] for t in range(nt)], dx, dy)
                    for t in range(nt):
                        ver[n - 1, ca, t, pl.ds(r, 8), :] = got[t]
            return carry

        by_threes(count, body)

    def neighbour(c, a, dx, dy, t, r):
        n = versions(a).index((dx, dy))
        if n == 0:
            return spin[2 * c + a, t, pl.ds(r, 8), :]
        return ver[n - 1, 2 * c + a, t, pl.ds(r, 8), :]

    def cosines(start, count):
        def body(i, carry):
            r = start + 8 * i
            for t in range(nt):
                for a in range(2):
                    mine = [spin[2 * c + a, t, pl.ds(r, 8), :] for c in range(3)]
                    for o, (b, dx, dy, dz) in enumerate(bonds(a)):
                        total = mine[0] * neighbour(0, b, dx, dy, t, r + dz)
                        for c in (1, 2):
                            total += mine[c] * neighbour(c, b, dx, dy, t, r + dz)
                        cosv[t, pl.ds(o * stride + a * rows + r, 8), :] = total
            return carry

        by_threes(count, body)

    tc = 2 if nt % 2 == 0 else 1
    chunks = nt // tc

    def features(c):
        c2 = c + c
        kinds = [c, c2 * c - 1.0]
        for _ in range(2, NB):
            kinds.append(c2 * kinds[-1] - kinds[-2])
        f_hi, f_lo = split(jnp.concatenate(kinds, 0))
        return jnp.concatenate([f_hi, f_lo], 0)

    def embedded(rhs):
        z = jnp.dot(w1[...], rhs, preferred_element_type=jnp.float32)
        return z[:LANES] + z[LANES:]

    def activated(hid):
        u = jnp.tanh(hid)
        d_hi, d_lo = split(1.0 - u * u)
        return jnp.concatenate([d_hi, d_lo], 0)

    def backward(rhs):
        y = jnp.dot(w2[...], rhs, preferred_element_type=jnp.float32)
        return y[:LANES] + y[LANES:]

    def slopes(c, y):
        c2 = c + c
        b1 = y[(NB - 1) * OP :]
        b2 = None
        for k in range(NB - 2, -1, -1):
            new = y[k * OP : (k + 1) * OP] + c2 * b1
            if b2 is not None:
                new = new - b2
            b1, b2 = new, b1
        return b1

    def bonds_at(t, a, r):
        return t, pl.ds(a * rows + r, OP, stride=stride), slice(None)

    def border_gradients(half):
        near = [bonds_at(t, a, border - a) for a in range(2) for t in range(2)]
        far = [bonds_at(half, a, border - 1 + a) for a in range(2)]
        chunks_of = [near + far]
        rhs = []
        for part in chunks_of:
            rhs.append(embedded(features(jnp.concatenate([cosv[p] for p in part], 1))))
        for part, hid in zip(chunks_of, rhs):
            c = jnp.concatenate([cosv[p] for p in part], 1)
            g = slopes(c, backward(activated(hid)))
            for n, p in enumerate(part):
                grad[p] = g[:, n * LANES : (n + 1) * LANES]

    def gradients(start, count):
        places = [(a, t) for a in range(2) for t in range(tc)]

        def place(i):
            if chunks == 1:
                return start + i, 0
            return start + i // chunks, (i % chunks) * tc

        def cosine(i):
            r, t0 = place(i)
            return jnp.concatenate([cosv[bonds_at(t0 + t, a, r)] for a, t in places], 1)

        def basis(i):
            return features(cosine(i))

        def forward(rhs, slot):
            hidden[slot] = embedded(rhs)

        def activate(slot):
            return activated(hidden[slot])

        def combine(i, y):
            r, t0 = place(i)
            g = slopes(cosine(i), y)
            for n, (a, t) in enumerate(places):
                grad[bonds_at(t0 + t, a, r)] = g[:, n * LANES : (n + 1) * LANES]

        for k in range(2):
            forward(basis(k), k)

        def one(i, slot):
            y = backward(activate(slot))
            forward(basis(i), slot)
            combine(i - 2, y)

        total = count * chunks
        done = 2
        if isinstance(total, int) and total <= 8:
            for i in range(done, total):
                one(i, i % 2)
        else:
            for many in (20, 16, 8, 4, 2) if chunks == 1 else (2,):
                def body(i, first, many=many):
                    for k in range(many):
                        one(first + i * many + k, k % 2)
                    return first

                times = (total - done) // many
                lax.fori_loop(0, times, body, done)
                done = done + times * many
        for k in range(2):
            combine(total - 2 + k, backward(activate(k)))

    def half_field(r, half, lanes):
        out = []
        for a in range(2):
            total = [None] * 3
            for o, (b, dx, dy, dz) in enumerate(bonds(a)):
                m = mate_of(o)
                theirs = grad[half if dy == 0 else 1 - half, pl.ds(m * stride + b * rows + r + dz, 8), :]
                if dx or dy:
                    theirs = jnp.take_along_axis(theirs, lanes[(dx, dy)], axis=1, mode="promise_in_bounds")
                coeff = grad[half, pl.ds(o * stride + a * rows + r, 8), :] + theirs
                for c in range(3):
                    term = coeff * neighbour(c, b, dx, dy, half, r + dz)
                    total[c] = term if total[c] is None else total[c] + term
            out.append([-x for x in total])
        return out

    def field(r, tiles):
        out = []
        for a in range(2):
            total = [[None] * nt for _ in range(3)]
            for o, (b, dx, dy, dz) in enumerate(bonds(a)):
                m = mate_of(o)
                theirs = [grad[t, pl.ds(m * stride + b * rows + r + dz, 8), :] for t in range(nt)]
                if pp.halves:
                    theirs = [pp.step_half(theirs, dx, dy, t) if t in tiles else None for t in range(nt)]
                else:
                    theirs = pp.step(theirs, dx, dy)
                for t in tiles:
                    coeff = grad[t, pl.ds(o * stride + a * rows + r, 8), :] + theirs[t]
                    for c in range(3):
                        term = coeff * neighbour(c, b, dx, dy, t, r + dz)
                        total[c][t] = term if total[c][t] is None else total[c][t] + term
            out.append([[None if x is None else -x for x in per] for per in total])
        return out

    def update(start, count, stage, only_border):
        tiles = [stage % 2] if pp.halves else range(nt)
        if pp.halves:
            lanes = {(dx, dy): pp.source_in(tiles[0], dx, dy) for dx in (-1, 0, 1) for dy in (-1, 0, 1)}

        def body(i, carry):
            r = start + 8 * i
            row = lax.broadcasted_iota(jnp.int32, (8, LANES), 0) + r
            if only_border:
                from_border = jnp.where(hi_above, row - border, border - 1 - row)
                wanted = (from_border >= 0) & (from_border < 2)
            else:
                wanted = True
            h = half_field(r, tiles[0], lanes) if pp.halves else field(r, tiles)
            for a in range(2):
                for t in tiles:
                    xl, yl, _ = pp.at(t)
                    mask = (
                        ((xl >= bx // 2).astype(jnp.int32) == stage // 2)
                        & ((yl >= by // 2).astype(jnp.int32) == stage % 2)
                        & wanted
                    )
                    s = [spin[2 * c + a, t, pl.ds(r, 8), :] for c in range(3)]
                    w = [TIME_STEP * (h[a][c] if pp.halves else h[a][c][t]) for c in range(3)]
                    square = 0.25 * (w[0] * w[0] + w[1] * w[1] + w[2] * w[2])
                    sn, cs, hs = half_turn(square)
                    cosr = 1.0 - 2.0 * sn * sn
                    sinc = hs * cs
                    proj = 0.5 * hs * hs * (w[0] * s[0] + w[1] * s[1] + w[2] * s[2])
                    for c in range(3):
                        p, q = (c + 1) % 3, (c + 2) % 3
                        cross = w[p] * s[q] - w[q] * s[p]
                        new = cosr * s[c] + sinc * cross + proj * w[c]
                        old = spin2[2 * c + a, t, pl.ds(r, 8), :]
                        spin2[2 * c + a, t, pl.ds(r, 8), :] = jnp.where(mask, new, old)
            return carry

        by_threes(count, body)

    def take(everything):
        for i in range((window + 7) // 8):
            r = PAD + 8 * i
            row = lax.broadcasted_iota(jnp.int32, (8, LANES), 0) + r
            sel = True if everything is True else everything | jnp.logical_not(is_hi(row))
            for ca in range(6):
                for t in range(nt):
                    place = (ca, t, pl.ds(r, 8), slice(None))
                    spin[place] = spin2[place] if sel is True else jnp.where(sel, spin2[place], spin[place])

    def stage_pair(stage, carry):
        f_low, f_high = ranges[0]
        for s in range(1, 4):
            f_low = jnp.where(stage == s, ranges[s][0], f_low)
            f_high = jnp.where(stage == s, ranges[s][1], f_high)
        n = f_high - f_low
        crosses = inside & (f_low < border) & (border < f_high)
        shifted_spins(f_low - 2, (n + 11) // 8)
        cosines(f_low - 1, (n + 9) // 8)
        gradients(f_low - 1, (n + 3) // 2 * 2)
        update(f_low, (n + 7) // 8, stage, False)
        take(jnp.logical_not(crosses))

        @pl.when(crosses)
        def _():
            shifted_spins(border - 4, 1)
            cosines(border - 4, 1)
            if pp.halves:
                border_gradients(stage % 2)
            else:
                gradients(border - 1, 2)
            update(border - 4, 1, stage, True)
            take(True)

        return carry

    lax.fori_loop(0, 4, stage_pair, 0)
    shifted_spins(own - 2, (sz + 11) // 8)
    cosines(own - 1, (sz + 9) // 8)
    gradients(own - 1, (sz + 3) // 2 * 2)

    final = field(own, range(nt))
    results = []
    for j in range(12):
        ca = j % 6
        v = [spin[ca, t, pl.ds(own, 8), :] for t in range(nt)] if j < 6 else final[ca % 2][ca // 2]
        results.append(pp.swapped(v) if pp.halves else v)
    lane16s = lax.broadcasted_iota(jnp.int32, (8, LANES), 1) // cells
    for t in range(nt):
        moved = []
        for j in range(12):
            v = results[j][t]
            moved.append(pltpu.roll(v, j * cells, axis=1) if j else v)
        for k in range(blk):
            u = moved[0]
            for j in range(1, 12):
                u = jnp.where(lane16s == (j + k) % blk, moved[j], u)
            if k:
                u = pltpu.roll(u, LANES - k * cells, axis=1)
            out_ref[t * blk + k] = u[:sz]


def per_device(gx, yz, spin_vectors, pair_weight, mix_weight, mix_bias, out_weight):
    three, two, bx, by, cz = spin_vectors.shape
    n = gx * yz
    sz = max(1, cz // n)
    rep = n * sz // cz
    window = sz + 2 * REACH - 2
    depth = -(-3 * window // 16) * 2
    rows = -(-window // 8) * 8 + 2 * PAD
    nt = n * bx * by // LANES
    brick = three * two * bx * by
    vmem = pl.BlockSpec(memory_space=pltpu.VMEM)

    f32, bf16 = jnp.float32, jnp.bfloat16
    packed, w1, w2 = pl.pallas_call(
        functools.partial(pack_kernel, n, sz, rep, window, depth),
        out_shape=[
            jax.ShapeDtypeStruct((n, depth // 2, 2, LANES), f32),
            jax.ShapeDtypeStruct((2 * LANES, 2 * LANES), bf16),
            jax.ShapeDtypeStruct((2 * LANES, 2 * LANES), bf16),
        ],
        in_specs=[vmem] * 5,
        out_specs=[vmem] * 3,
        scratch_shapes=[
            pltpu.VMEM((2 * cz, LANES), f32),
            pltpu.VMEM((cz + 32, LANES), f32),
            pltpu.VMEM((cz + 32, LANES), f32),
        ],
        name="pack",
    )(spin_vectors.reshape(brick, cz), pair_weight, mix_weight, mix_bias[None], out_weight[None])
    received = lax.all_to_all(packed, ("gx", "yz"), 0, 0, tiled=True)

    result = pl.pallas_call(
        functools.partial(sweep_kernel, gx, yz, bx, by, cz, sz, rep, window, depth),
        out_shape=jax.ShapeDtypeStruct((n, sz, LANES), f32),
        in_specs=[vmem] * 3,
        out_specs=vmem,
        scratch_shapes=[
            pltpu.VMEM((6, nt, rows, LANES), f32),
            pltpu.VMEM((6, nt, rows, LANES), f32),
            pltpu.VMEM((5, 6, nt, rows, LANES), f32),
            pltpu.VMEM((nt, OP * (2 * rows + 1) + 7, LANES), f32),
            pltpu.VMEM((nt, OP * (2 * rows + 1) + 7, LANES), f32),
            pltpu.VMEM((2, LANES, 2 * (2 - nt % 2) * LANES), f32),
            pltpu.VMEM((n, 16, LANES), f32),
        ],
        compiler_params=pltpu.CompilerParams(vmem_limit_bytes=min(56, 8 + 4 * nt) * 2**20),
        name="sweep",
    )(received, w1, w2)
    returned = lax.all_to_all(result, ("gx", "yz"), 0, 0, tiled=True)
    if rep > 1:
        returned = returned[::rep]

    flat = returned.reshape(cz, LANES).T
    outs = [flat[:brick], flat[brick : 2 * brick]]
    return tuple(x.reshape(three, two, bx, by, cz) for x in outs)


def solution(mesh):
    gx, yz = mesh.shape["gx"], mesh.shape["yz"]
    spec = P(None, None, "gx", "yz", None)
    return jax.shard_map(
        functools.partial(per_device, gx, yz),
        mesh=mesh,
        in_specs=(spec, P(), P(), P(), P()),
        out_specs=(spec, spec),
        check_vma=False,
    )
```
